32 devices in a mesh: section: 4 (over y, x), dp: 8 (over z, core).
Axes of the slice: x: 2, y: 2, z: 4, core: 2. Of those that a mesh axis runs over, the one named last changes fastest.
Arguments:
- enc_in: bfloat16 [32, 512, 768], P('dp', 'section'), may hold values from -6 to 6
- lengths: int32 [32], P('dp'), may hold values from 40 to 512, as said below
- dec_in: bfloat16 [32, 768], P('dp', 'section'), may hold values from -6 to 6
- gains: bfloat16 [4, 2, 768], P('section'), may hold values from 0.5 to 1.5
- weights: bfloat16 [4, 8, 768, 768], P('section')
- d_out: bfloat16 [32, 768], P('dp', 'section'), may hold values from -6 to 6
Outputs:
- dec_out: bfloat16 [32, 768], P('dp', 'section')
- d_enc_in: bfloat16 [32, 512, 768], P('dp', 'section')
- d_dec_in: bfloat16 [32, 768], P('dp', 'section')
- d_gains: float32 [4, 2, 768], P('section')
- d_weights: float32 [4, 8, 768, 768], P('section')
The draws below stay inside these ranges and needn't reach their ends.
Inputs may be any that keep to these rules, and one draw needn't show every extreme that they name: Positions below lengths[p] are passage p's tokens, the rest padding; some passage has exactly 512 tokens and some exactly 40.
All inputs are finite; a program needn't handle non-finite values.
Results may differ from the reference program's by a relative error of at most 0.017.
Values may be sent and summed in bfloat16 or wider, within the bound.
A program may use at most 192 MiB of HBM per device.

```python
import math
import jax
import jax.numpy as jnp
from jax import lax

D = 768
HEADS = 12
HEAD = 64
LEN = 512
MINLEN = 40
SECTIONS = 4
P_DEV = 4
PASSAGES = 32
N_DP = 8


def draw_lengths(key, part):
    key_rows, key_high, key_low = jax.random.split(jax.random.fold_in(key, 3), 3)
    drawn = jax.random.randint(key_rows, (PASSAGES,), MINLEN, LEN + 1)
    pick_high = jax.random.randint(key_high, (), 0, PASSAGES)
    pick_low = (pick_high + 1 + jax.random.randint(key_low, (), 0, PASSAGES - 1)) % PASSAGES
    drawn = drawn.at[pick_high].set(LEN)
    drawn = drawn.at[pick_low].set(MINLEN)
    return drawn.astype(jnp.int32)


def draw_weights(key, part):
    scale_table = jnp.array([[0.25, 1.0, 1.0, 4.0, 1.0, 1.0, 1.0, 1.0], [1.0, 1.0, 1.0, 1.0, 0.7, 0.7, 0.7, 0.7], [1.0, 1.0, 0.02, 1.0, 1.0, 16.0, 1.0, 1.0], [1.0, 1.0, 1.0, 1.0, 0.7, 0.7, 0.7, 0.7]], jnp.float32)
    inner_key = jax.random.fold_in(key, 11)
    base_draw = jax.random.normal(inner_key, (SECTIONS, 8, D, D), jnp.float32)
    return (base_draw * scale_table[:, :, None, None] / math.sqrt(D)).astype(jnp.bfloat16)


def levels(own_key, dims, pieces, low, high):
    def one(position, parts):
        heights = jax.random.uniform(jax.random.fold_in(jax.random.fold_in(own_key, 6), position), (parts,), jnp.float32, low / len(pieces), high / len(pieces))
        return jnp.repeat(jnp.exp(heights), dims[position] // parts).reshape((-1,) + (1,) * (len(dims) - position - 1))

    gain = one(*pieces[0])
    for cut in pieces[1:]:
        gain = gain * one(*cut)
    return gain


def gaussian(rng, extent, width, reach, cuts=(), held_as=jnp.bfloat16):
    values = jax.random.normal(rng, extent, jnp.float32) * width
    if len(cuts) > 0:
        values = levels(rng, extent, cuts, -0.22, 0.18) * values
    return jnp.clip(values, min=-reach, max=reach).astype(held_as)


def setup_inputs(seed: int = 0) -> dict:
    splits = jax.random.split(jax.random.key(seed), 7)
    return {
        "enc_in": gaussian(splits[0], (PASSAGES, LEN, D), 1.0, 6.0, ((0, 8), (1, 4))),
        "lengths": draw_lengths(jax.random.fold_in(splits[6], 71), 0),
        "dec_in": gaussian(splits[2], (PASSAGES, D), 1.0, 6.0, ((0, 8), (1, 4))),
        "gains": jnp.clip(1.0 + 0.1 * jax.random.normal(splits[3], (SECTIONS, 2, D), jnp.float32), 0.5, 1.5).astype(jnp.bfloat16),
        "weights": draw_weights(jax.random.fold_in(splits[6], 71), 0),
        "d_out": gaussian(splits[5], (PASSAGES, D), 1.0, 6.0, ((0, 8), (1, 4))),
    }


epsilon = 1e-06
masked_score = -1e+30
highest = lax.Precision.HIGHEST

@jax.custom_vjp
def low(v):
    return lax.optimization_barrier(v.astype(jnp.bfloat16)).astype(jnp.float32)

@jax.custom_vjp
def low_back(v):
    return v

def low_keep(v):
    return (low(v), None)

def low_pass(kept, grad):
    return (grad,)

def back_keep(v):
    return (v, None)

def back_low(kept, grad):
    return (low(grad),)
low.defvjp(low_keep, low_pass)
low_back.defvjp(back_keep, back_low)

def norm_rows(values_in, gain_row):
    return values_in * lax.rsqrt(lax.optimization_barrier(jnp.mean(values_in * values_in, axis=-1, keepdims=True)) + epsilon) * gain_row

def feed_forward(values_in, gain_row, blocks):
    acts_low = low(norm_rows(values_in, gain_row))
    hidden_pre = low_back(jnp.einsum('...d,bdf->...bf', acts_low, blocks[0:4], precision=highest))
    hidden_low = low(jax.nn.gelu(hidden_pre, approximate=True))
    result = jnp.einsum('...bf,bfd->...d', hidden_low, blocks[4:8], precision=highest)
    return low_back(low(values_in + result))

def encoder_attention(values_in, gain_row, blocks, lengths):
    group_size, length = (values_in.shape[0], values_in.shape[1])
    acts_low = low(norm_rows(values_in, gain_row))

    def project(block_index):
        result = jnp.einsum('gld,de->gle', acts_low, blocks[block_index], precision=highest)
        return low_back(low(result)).reshape(group_size, length, HEADS, HEAD)
    queries, key_rows, values = (project(0), project(1), project(2))
    scores = low_back(jnp.einsum('glhd,gmhd->ghlm', queries, key_rows, precision=highest))
    is_valid = lax.iota(jnp.int32, length)[None, :] < lengths[:, None]
    probs_low = low(jax.nn.softmax(jnp.where(is_valid[:, None, None, :], scores, masked_score), axis=-1))
    mixed = low_back(low(jnp.einsum('ghlm,gmhd->glhd', probs_low, values, precision=highest)))
    result = jnp.einsum('gld,de->gle', mixed.reshape(group_size, length, D), blocks[3], precision=highest)
    return low_back(low(values_in + result))

def decoder_attention(enc_out, start_in, gain_pair, blocks, lengths):
    group_size, length = (enc_out.shape[0], enc_out.shape[1])
    self_acts = low(norm_rows(start_in, gain_pair[0]))
    self_values = low_back(low(jnp.dot(self_acts, blocks[0], precision=highest)))
    middle = start_in + low_back(jnp.dot(self_values, blocks[1], precision=highest))
    cross_acts = low(norm_rows(middle, gain_pair[1]))
    queries = low_back(low(jnp.dot(cross_acts, blocks[2], precision=highest))).reshape(group_size, HEADS, HEAD)
    key_rows = low_back(low(jnp.einsum('gld,de->gle', enc_out, blocks[3], precision=highest)))
    key_rows = key_rows.reshape(group_size, length, HEADS, HEAD)
    values = low_back(low(jnp.einsum('gld,de->gle', enc_out, blocks[4], precision=highest)))
    values = values.reshape(group_size, length, HEADS, HEAD)
    scores = low_back(jnp.einsum('ghd,glhd->ghl', queries, key_rows, precision=highest))
    is_valid = lax.iota(jnp.int32, length)[None, :] < lengths[:, None]
    probs_low = low(jax.nn.softmax(jnp.where(is_valid[:, None, :], scores, masked_score), axis=-1))
    mixed = low_back(low(jnp.einsum('ghl,glhd->ghd', probs_low, values, precision=highest)))
    mixed = mixed.reshape(group_size, D)
    return low_back(low(middle + jnp.dot(mixed, blocks[5], precision=highest)))

def forward_all(enc_value, start_value, gain_value, weight_value, lengths):
    hidden_state = encoder_attention(enc_value, gain_value[0, 0], weight_value[0], lengths)
    encoded = feed_forward(hidden_state, gain_value[1, 0], weight_value[1])
    decoder_state = decoder_attention(encoded, start_value, gain_value[2], weight_value[2], lengths)
    return feed_forward(decoder_state, gain_value[3, 0], weight_value[3])

def reference(enc_in, lengths, dec_in, gains, weights, d_out):
    gain_full = gains.astype(jnp.float32)
    weight_full = weights.astype(jnp.float32)
    enc_groups = enc_in.astype(jnp.float32).reshape(N_DP, P_DEV, LEN, D)
    start_groups = dec_in.astype(jnp.float32).reshape(N_DP, P_DEV, D)
    length_groups = lengths.reshape(N_DP, P_DEV)
    cot_groups = d_out.astype(jnp.float32).reshape(N_DP, P_DEV, D)

    def scan_step(totals, group_item):
        enc_group, start_group, length_group, cot_group = group_item

        def run_group(enc_value, start_value, gain_value, weight_value):
            return forward_all(enc_value, start_value, gain_value, weight_value, length_group)
        output, pull_back = jax.vjp(run_group, enc_group, start_group, gain_full, weight_full)
        grad_enc, grad_start, grad_gain, grad_weight = pull_back(cot_group)
        totals = (totals[0] + grad_gain, totals[1] + grad_weight)
        return (totals, (output.astype(jnp.bfloat16), grad_enc.astype(jnp.bfloat16), grad_start.astype(jnp.bfloat16)))
    initial = (jnp.zeros_like(gain_full), jnp.zeros_like(weight_full))
    totals, outputs = lax.scan(scan_step, initial, (enc_groups, start_groups, length_groups, cot_groups))
    decoded, grad_enc, grad_start = outputs
    return (decoded.reshape(PASSAGES, D), grad_enc.reshape(PASSAGES, LEN, D), grad_start.reshape(PASSAGES, D), totals[0], totals[1])
```

```python
import functools
import math

import jax
import jax.numpy as jnp
from jax import lax
from jax.experimental import pallas as pl
from jax.experimental.pallas import tpu as pltpu
from jax.sharding import PartitionSpec as P

D = 768
HEADS = 12
HEAD = 64
PAIRS = HEADS // 2
LEN = 512
GROUP = 4
ROWS = GROUP * LEN
epsilon = 1e-06
masked_score = -1e30
gelu_coeff = 0.044715
gelu_scale = math.sqrt(2.0 / math.pi)
log2_e = 1.4426950408889634
bf16 = jnp.bfloat16
f32 = jnp.float32
MESH = pl.DeviceIdType.MESH

W_ROWS = 0
X_ROWS = 3072
Q_ROWS = X_ROWS + ROWS
K_ROWS = Q_ROWS + ROWS
V_ROWS = K_ROWS + ROWS
O_ROWS = V_ROWS + ROWS
H_ROWS = O_ROWS + ROWS
DH_ROWS = H_ROWS + ROWS
IL_ROWS = DH_ROWS + ROWS
POOL_ROWS = IL_ROWS + ROWS
FF_H = 6144
FF_A = FF_H + ROWS
FF_E = FF_A + ROWS
RELAY_F = 6144
GELU_ROWS = 12 * ROWS
WIDE_ROWS = 24 * ROWS

CHUNK = 64
CHUNKS = 4
RELAY = CHUNK * CHUNKS
DIRECT = LEN - RELAY
RELAY_B = RELAY_F + GROUP * RELAY
FAC_ROWS = 176


def nn(a, b):
    return jnp.dot(a, b, preferred_element_type=f32)


def nt(a, b):
    return lax.dot_general(a, b, (((1,), (1,)), ((), ())), preferred_element_type=f32)


def tn(a, b):
    return lax.dot_general(a, b, (((0,), (0,)), ((), ())), preferred_element_type=f32)


def iota(shape, axis):
    return lax.broadcasted_iota(jnp.int32, shape, axis)


def inverse_rms(v):
    return lax.rsqrt(jnp.mean(v * v, axis=-1, keepdims=True) + epsilon)


def norm_back(normed, inverse, gain_row, grad):
    scaled = grad * gain_row
    return inverse * (scaled - normed * jnp.mean(scaled * normed, axis=-1, keepdims=True))


def gelu_both(u):
    square = u * u
    tangent = jnp.tanh(gelu_scale * (u + gelu_coeff * square * u))
    half = 0.5 * (1.0 + tangent)
    slope = half + 0.5 * u * (1.0 - tangent * tangent) * (
        gelu_scale + 3.0 * gelu_coeff * gelu_scale * square
    )
    return (u * half, slope)


class Places:
    def __init__(self, sections):
        self.count = 0
        self.enc = [self.take(GROUP) for _ in range(sections)]
        self.small = [self.take(2) for _ in range(sections)]
        self.direct = self.take(GROUP)
        self.relay = [self.take(GROUP * CHUNKS) for _ in range(3)]
        self.back_direct = self.take(GROUP)
        self.back_relay = [self.take(GROUP * CHUNKS) for _ in range(3)]
        self.qk = self.take(1)
        self.mix = self.take(GROUP)
        self.state = self.take(1)
        self.state_back = self.take(1)
        self.g = self.take(1)
        self.x = self.take(1)
        self.out_enc = [self.take(GROUP) for _ in range(sections)]
        self.out_small = [self.take(2) for _ in range(sections)]

    def take(self, amount):
        first = self.count
        self.count += amount
        return first


def relay_kernel(
    sections,
    places,
    len_ref,
    enc_ref,
    small_ref,
    w_ref,
    gain_ref,
    o_enc,
    o_small,
    o_dw,
    o_fac,
    o_gain,
    pool,
    wide,
    acc,
    cp,
    small,
    qk,
    mix,
    gk,
    xs,
    state,
    state_back,
    fac,
    rows_out,
    gain_sum,
    send_sem,
    recv_sem,
    local_sem,
):
    me = lax.axis_index("section")
    group = lax.axis_index("dp")
    chunk_len = LEN // sections

    def remote(number, src, dst, target):
        return pltpu.make_async_remote_copy(
            src_ref=src,
            dst_ref=dst,
            send_sem=send_sem.at[number],
            recv_sem=recv_sem.at[number],
            device_id=(target, group),
            device_id_type=MESH,
        )

    def local_copy(number, src, dst):
        return pltpu.make_async_copy(src, dst, local_sem.at[number])

    def rows(base, start, count):
        return pool.at[pl.ds(pl.multiple_of(base + start, CHUNK), count)]

    barrier = pltpu.get_barrier_semaphore()
    for step in range(1, sections):
        pl.semaphore_signal(
            barrier,
            inc=1,
            device_id=(lax.rem(me + step, sections), group),
            device_id_type=MESH,
        )
    pl.semaphore_wait(barrier, sections - 1)

    lane = iota((1, 128), 1)
    low_half = lane < HEAD

    def enc_copy(sender, p):
        return remote(
            places.enc[sender] + p,
            enc_ref.at[p],
            rows(X_ROWS, p * LEN + sender * chunk_len, chunk_len),
            0,
        )

    def small_copy(sender, target):
        return remote(places.small[sender] + target - 2, small_ref, small.at[sender], target)

    def direct_copy(p):
        return remote(
            places.direct + p, rows(H_ROWS, p * LEN, DIRECT), rows(FF_H, p * LEN, DIRECT), 1
        )

    def relay_copy(hop, index):
        p = index // CHUNKS
        piece = index % CHUNKS
        whole = p * LEN + DIRECT + piece * CHUNK
        src = rows(H_ROWS, whole, CHUNK) if hop == 0 else rows(RELAY_F, index * CHUNK, CHUNK)
        dst = rows(FF_H, whole, CHUNK) if hop == 2 else rows(RELAY_F, index * CHUNK, CHUNK)
        return remote(places.relay[hop] + index, src, dst, (2, 3, 1)[hop])

    def back_direct_copy(p):
        return remote(
            places.back_direct + p, rows(FF_H, p * LEN, DIRECT), rows(DH_ROWS, p * LEN, DIRECT), 0
        )

    def back_relay_copy(hop, index):
        p = index // CHUNKS
        piece = index % CHUNKS
        whole = p * LEN + DIRECT + piece * CHUNK
        src = rows(FF_H, whole, CHUNK) if hop == 0 else rows(RELAY_B, index * CHUNK, CHUNK)
        dst = rows(DH_ROWS, whole, CHUNK) if hop == 2 else rows(RELAY_B, index * CHUNK, CHUNK)
        return remote(places.back_relay[hop] + index, src, dst, (3, 2, 0)[hop])

    def qk_copy():
        return remote(places.qk, qk, qk, 1)

    def mix_copy(p):
        part = pl.ds(pl.multiple_of(p * 16, 16), 16)
        return remote(places.mix + p, mix.at[part], mix.at[part], 2)

    def state_copy():
        return remote(places.state, state, state, 3)

    def state_back_copy():
        return remote(places.state_back, state_back, state_back, 2)

    def g_copy():
        return remote(places.g, gk, gk, 1)

    def x_copy():
        return remote(places.x, xs, xs, 2)

    def out_enc_copy(target, p):
        return remote(
            places.out_enc[target] + p,
            rows(H_ROWS, p * LEN + target * chunk_len, chunk_len),
            o_enc.at[p],
            target,
        )

    def out_small_copy(target, kind):
        return remote(
            places.out_small[target] + kind, rows_out.at[kind], o_small.at[kind], target
        )

    def each_passage(body):
        def step(p, carry):
            body(p)
            return carry

        lax.fori_loop(0, GROUP, step, 0)

    def weights_in(blocks):
        copies = [
            local_copy(
                i,
                w_ref.at[pl.ds(i * D, D)],
                pool.at[pl.ds(W_ROWS + i * D, D)],
            )
            for i in range(blocks)
        ]
        for c in copies:
            c.start()
        return copies

    def block(i):
        return pool[W_ROWS + i * D : W_ROWS + (i + 1) * D, :]

    def send_inputs():
        def step(p, carry):
            enc_copy(me, p).start()
            return carry

        lax.fori_loop(0, GROUP, step, 0)

    def dynamic_enc_copy(p):
        number = places.enc[0] + me * GROUP + p
        return remote(
            number, enc_ref.at[p], rows(X_ROWS, p * LEN + me * chunk_len, chunk_len), 0
        )

    def dynamic_small_copy(target):
        number = places.small[0] + me * 2 + target - 2
        return remote(number, small_ref, small.at[me], target)

    @pl.when(me != 2)
    def _():
        dynamic_small_copy(2).start()

    @pl.when(me != 3)
    def _():
        dynamic_small_copy(3).start()

    @pl.when(me != 0)
    def _():
        each_passage(lambda p: dynamic_enc_copy(p).start())

    @pl.when(me == 0)
    def _():
        own = [
            local_copy(8 + p, enc_ref.at[p], pool.at[pl.ds(X_ROWS + p * LEN, chunk_len)])
            for p in range(GROUP)
        ]
        for c in own:
            c.start()
        weights = weights_in(4)
        for c in weights:
            c.wait()
        for c in own:
            c.wait()
        gain_row = gain_ref[0:1, :]
        key_row = iota((LEN, 1), 0)

        def pair_columns(hp):
            return pl.ds(pl.multiple_of(hp * 128, 128), 128)

        def forward(p):
            for sender in range(1, sections):
                enc_copy(sender, p).wait_recv()
            start = pl.multiple_of(p * LEN, LEN)
            x = pool[pl.ds(X_ROWS + start, LEN), :].astype(f32)
            a0 = (x * inverse_rms(x) * gain_row).astype(bf16)
            pool[pl.ds(Q_ROWS + start, LEN), :] = (nn(a0, block(0)) * log2_e).astype(bf16)
            pool[pl.ds(K_ROWS + start, LEN), :] = nn(a0, block(1)).astype(bf16)
            pool[pl.ds(V_ROWS + start, LEN), :] = nn(a0, block(2)).astype(bf16)
            bias = jnp.where(key_row < len_ref[p], 0.0, masked_score).astype(bf16)

            def pair(hp, carry):
                c = pair_columns(hp)
                q2 = pool[pl.ds(Q_ROWS + start, LEN), c]
                k2 = pool[pl.ds(K_ROWS + start, LEN), c]
                v2 = pool[pl.ds(V_ROWS + start, LEN), c]
                one = jnp.ones_like(q2)
                zero = jnp.zeros_like(q2)
                queries = [
                    jnp.where(low_half, q2, jnp.where(lane == HEAD, one, zero)),
                    jnp.where(low_half, jnp.where(lane == 0, one, zero), q2),
                ]
                keys = [
                    jnp.where(low_half, k2, jnp.where(lane == HEAD, bias, zero)),
                    jnp.where(low_half, jnp.where(lane == 0, bias, zero), k2),
                ]
                values = [jnp.where(low_half, v2, one), jnp.where(low_half, one, v2)]
                mixes = []
                for half in range(2):
                    s = nt(queries[half], keys[half])
                    e = jnp.exp2(s - jnp.max(s, axis=-1, keepdims=True)).astype(bf16)
                    at = pl.multiple_of((p * HEADS + hp * 2 + half) * 2 * LEN, 2 * LEN)
                    wide[pl.ds(at, LEN), :] = e[:, :256]
                    wide[pl.ds(at + LEN, LEN), :] = e[:, 256:]
                    mixes.append(nn(e, values[half]))
                total = pltpu.roll(jnp.where(low_half, mixes[1], mixes[0]), HEAD, 1)
                inverse = 1.0 / total
                pool[pl.ds(O_ROWS + start, LEN), c] = (
                    jnp.where(low_half, mixes[0], mixes[1]) * inverse
                ).astype(bf16)
                pool[pl.ds(IL_ROWS + start, LEN), c] = inverse.astype(bf16)
                return carry

            lax.fori_loop(0, PAIRS, pair, 0)
            h = x + nn(pool[pl.ds(O_ROWS + start, LEN), :], block(3))
            pool[pl.ds(H_ROWS + start, LEN), :] = h.astype(bf16)
            direct_copy(p).start()
            for piece in range(CHUNKS):
                relay_copy(0, p * CHUNKS + piece).start()

        each_passage(forward)

        def sent(p):
            direct_copy(p).wait_send()
            for piece in range(CHUNKS):
                relay_copy(0, p * CHUNKS + piece).wait_send()

        each_passage(sent)
        gain_sum[...] = jnp.zeros_like(gain_sum)

        def backward(p):
            start = pl.multiple_of(p * LEN, LEN)
            back_direct_copy(p).wait_recv()
            for piece in range(CHUNKS):
                back_relay_copy(2, p * CHUNKS + piece).wait_recv()
            dh = pool[pl.ds(DH_ROWS + start, LEN), :]
            pool[pl.ds(H_ROWS + start, LEN), :] = nt(dh, block(3)).astype(bf16)

            def pair(hp, carry):
                c = pair_columns(hp)
                q2 = pool[pl.ds(Q_ROWS + start, LEN), c]
                k2 = pool[pl.ds(K_ROWS + start, LEN), c]
                v2 = pool[pl.ds(V_ROWS + start, LEN), c]
                da = pool[pl.ds(H_ROWS + start, LEN), c].astype(f32)
                mixed = pool[pl.ds(O_ROWS + start, LEN), c].astype(f32)
                da = da * pool[pl.ds(IL_ROWS + start, LEN), c].astype(f32)
                product = da * mixed
                da = da.astype(bf16)
                one = jnp.ones_like(q2)
                zero = jnp.zeros_like(q2)
                dq = []
                dk = []
                dv = []
                for half in range(2):
                    mine = low_half if half == 0 else lane >= HEAD
                    spare = HEAD if half == 0 else 0
                    centre = -jnp.sum(jnp.where(mine, product, 0.0), axis=-1, keepdims=True)
                    centre_high = centre.astype(bf16)
                    centre_low = (centre - centre_high.astype(f32)).astype(bf16)
                    da_own = jnp.where(mine, da, zero)
                    da_ext = jnp.where(
                        lane == spare,
                        centre_high,
                        jnp.where(lane == spare + 1, centre_low, da_own),
                    )
                    at = pl.multiple_of((p * HEADS + hp * 2 + half) * 2 * LEN, 2 * LEN)
                    e = jnp.concatenate(
                        [wide[pl.ds(at, LEN), :], wide[pl.ds(at + LEN, LEN), :]], axis=1
                    )
                    ds = e * nt(da_ext, jnp.where(mine, v2, one)).astype(bf16)
                    dq.append(nn(ds, k2))
                    dk.append(nn(jnp.where(mine, q2, zero).T, ds))
                    dv.append(nn(da_own.T, e))
                pool[pl.ds(Q_ROWS + start, LEN), c] = jnp.where(low_half, dq[0], dq[1]).astype(bf16)
                pool[pl.ds(K_ROWS + start, LEN), c] = (
                    (dk[0] + dk[1]).T * (1.0 / log2_e)
                ).astype(bf16)
                pool[pl.ds(V_ROWS + start, LEN), c] = (dv[0] + dv[1]).T.astype(bf16)
                return carry

            lax.fori_loop(0, PAIRS, pair, 0)
            grad = (
                nt(pool[pl.ds(Q_ROWS + start, LEN), :], block(0))
                + nt(pool[pl.ds(K_ROWS + start, LEN), :], block(1))
                + nt(pool[pl.ds(V_ROWS + start, LEN), :], block(2))
            )
            x = pool[pl.ds(X_ROWS + start, LEN), :].astype(f32)
            inverse = inverse_rms(x)
            normed = x * inverse
            d_in = dh.astype(f32) + norm_back(normed, inverse, gain_row, grad)
            pool[pl.ds(H_ROWS + start, LEN), :] = d_in.astype(bf16)
            gain_sum[0:1, :] += jnp.sum(grad * normed, axis=0, keepdims=True)
            pool[pl.ds(X_ROWS + start, LEN), :] = (normed * gain_row).astype(bf16)
            for target in range(1, sections):
                out_enc_copy(target, p).start()
            local_copy(8 + p, rows(H_ROWS, start, chunk_len), o_enc.at[p]).start()

        each_passage(backward)
        outs = []
        for i, (left, right) in enumerate(
            ((X_ROWS, Q_ROWS), (X_ROWS, K_ROWS), (X_ROWS, V_ROWS), (O_ROWS, DH_ROWS))
        ):

            def columns(k, carry):
                c = pl.ds(pl.multiple_of(k * 256, 256), 256)
                pool[pl.ds(W_ROWS + i * D, D), c] = tn(
                    pool[left : left + ROWS, :], pool[right : right + ROWS, c]
                ).astype(bf16)
                return carry

            lax.fori_loop(0, 3, columns, 0)
            copy = local_copy(
                i, pool.at[pl.ds(W_ROWS + i * D, D)], o_dw.at[pl.ds(i * D, D)]
            )
            copy.start()
            outs.append(copy)
        for copy in outs:
            copy.wait()

        def finish(p):
            for target in range(1, sections):
                out_enc_copy(target, p).wait_send()
            local_copy(8 + p, rows(H_ROWS, p * LEN, chunk_len), o_enc.at[p]).wait()

        each_passage(finish)

    @pl.when(me == 1)
    def _():
        for c in weights_in(8):
            c.wait()
        gain_row = gain_ref[0:1, :]
        key_place = iota((1, LEN), 1)
        qk_copy().wait_recv()

        def tiles(b, p, base):
            return [
                pl.ds(pl.multiple_of(base + (3 * b + i) * ROWS + p * LEN, LEN), LEN)
                for i in range(3)
            ]

        def forward(p):
            start = pl.multiple_of(p * LEN, LEN)
            direct_copy(p).wait_recv()
            for piece in range(CHUNKS):
                relay_copy(2, p * CHUNKS + piece).wait_recv()
            h = pool[pl.ds(FF_H + start, LEN), :].astype(f32)
            a1 = (h * inverse_rms(h) * gain_row).astype(bf16)
            pool[pl.ds(FF_A + start, LEN), :] = a1
            acc[...] = h
            for b in range(4):
                r, slope = gelu_both(nn(a1, block(b)))
                r = r.astype(bf16)
                slope = slope.astype(bf16)
                for i, (at_r, at_s) in enumerate(zip(tiles(b, p, 0), tiles(b, p, GELU_ROWS))):
                    wide[at_r, :] = r[:, 256 * i : 256 * (i + 1)]
                    wide[at_s, :] = slope[:, 256 * i : 256 * (i + 1)]
                acc[...] += nn(r, block(4 + b))
            e = acc[...].astype(bf16)
            pool[pl.ds(FF_E + start, LEN), :] = e
            part = pl.ds(pl.multiple_of(p * 16, 16), 16)
            score = jnp.where(key_place < len_ref[p], nt(qk[part, :], e), masked_score)
            score = jnp.exp(score - jnp.max(score, axis=-1, keepdims=True))
            probs = score / jnp.sum(score, axis=-1, keepdims=True)
            cp[part, :] = probs
            mix[part, :] = nn(probs.astype(bf16), e).astype(bf16)
            mix_copy(p).start()

        each_passage(forward)
        each_passage(lambda p: mix_copy(p).wait_send())
        gain_sum[...] = jnp.zeros_like(gain_sum)
        g_copy().wait_recv()

        def backward(p):
            start = pl.multiple_of(p * LEN, LEN)
            part = pl.ds(pl.multiple_of(p * 16, 16), 16)
            e = pool[pl.ds(FF_E + start, LEN), :]
            probs = cp[part, :]
            d_probs = nt(gk[part, :], e)
            d_score = probs * (d_probs - jnp.sum(probs * d_probs, axis=-1, keepdims=True))
            d_score = d_score.astype(bf16)
            xs[part, :] = nn(d_score, e).astype(bf16)
            de = tn(d_score, qk[part, :]) + tn(probs.astype(bf16), gk[part, :])
            de = de.astype(bf16)
            pool[pl.ds(FF_E + start, LEN), :] = de
            for b in range(4):
                at = tiles(b, p, GELU_ROWS)
                slope = jnp.concatenate([wide[t, :] for t in at], axis=1)
                du = (nt(de, block(4 + b)) * slope.astype(f32)).astype(bf16)
                for i, t in enumerate(at):
                    wide[t, :] = du[:, 256 * i : 256 * (i + 1)]
                grad = nt(du, block(b))
                if b == 0:
                    acc[...] = grad
                else:
                    acc[...] += grad
            grad = acc[...]
            h = pool[pl.ds(FF_H + start, LEN), :].astype(f32)
            inverse = inverse_rms(h)
            normed = h * inverse
            dh = de.astype(f32) + norm_back(normed, inverse, gain_row, grad)
            gain_sum[0:1, :] += jnp.sum(grad * normed, axis=0, keepdims=True)
            pool[pl.ds(FF_H + start, LEN), :] = dh.astype(bf16)
            back_direct_copy(p).start()
            for piece in range(CHUNKS):
                back_relay_copy(0, p * CHUNKS + piece).start()

        each_passage(backward)
        x_copy().start()

        def term(b, carry):
            for i in range(3):
                t = 3 * b + i
                du = wide[pl.ds(pl.multiple_of(GELU_ROWS + t * ROWS, ROWS), ROWS), :]
                pool[
                    pl.ds(pl.multiple_of(W_ROWS + b * D, D), D), 256 * i : 256 * (i + 1)
                ] = tn(pool[FF_A : FF_A + ROWS, :], du).astype(bf16)
                r = wide[pl.ds(pl.multiple_of(t * ROWS, ROWS), ROWS), :]
                pool[pl.ds(pl.multiple_of(W_ROWS + (4 + b) * D + 256 * i, 256), 256), :] = tn(
                    r, pool[FF_E : FF_E + ROWS, :]
                ).astype(bf16)
            for k in (b, 4 + b):
                local_copy(
                    k,
                    pool.at[pl.ds(pl.multiple_of(W_ROWS + k * D, D), D)],
                    o_dw.at[pl.ds(pl.multiple_of(k * D, D), D)],
                ).start()
            return carry

        lax.fori_loop(0, 4, term, 0)

        def term_out(k, carry):
            local_copy(
                k,
                pool.at[pl.ds(pl.multiple_of(W_ROWS + k * D, D), D)],
                o_dw.at[pl.ds(pl.multiple_of(k * D, D), D)],
            ).wait()
            return carry

        lax.fori_loop(0, 8, term_out, 0)
        x_copy().wait_send()

        def sent(p):
            back_direct_copy(p).wait_send()
            for piece in range(CHUNKS):
                back_relay_copy(0, p * CHUNKS + piece).wait_send()

        each_passage(sent)

    def gathered_rows(own):
        copy = local_copy(20, small_ref, small.at[own])
        copy.start()
        for sender in range(sections):
            if sender != own:
                small_copy(sender, own).wait_recv()
        copy.wait()
        width = D // sections
        total = jnp.zeros((16, D), f32)
        for sender in range(sections):
            row, column = iota((256, D), 0), iota((256, D), 1)
            pick = jnp.where((column == row + width * sender) & (row < width), 1.0, 0.0)
            total = total + nn(small[sender], pick.astype(bf16))
        return total

    def moved(values, first, to):
        row, column = iota((16, 16), 0), iota((16, 16), 1)
        pick = (column - first == row - to) & (row >= to) & (row < to + GROUP)
        return nn(jnp.where(pick, 1.0, 0.0).astype(bf16), values)

    def packed(values):
        total = moved(values[0], 0, 0)
        for i, value in enumerate(values[1:]):
            total = total + moved(value, 0, GROUP * (i + 1))
        return total.astype(bf16)

    head_mask = (iota((64, D), 1) >> 6) == (iota((64, D), 0) & 15)

    def spread_heads(values):
        pick = jnp.where((iota((64, 16), 0) >> 4) == iota((64, 16), 1), 1.0, 0.0)
        return jnp.where(head_mask, nn(pick.astype(bf16), values), 0.0).astype(bf16)

    def join_heads(values):
        pick = jnp.where(iota((16, 64), 0) == (iota((16, 64), 1) >> 4), 1.0, 0.0)
        return nn(pick.astype(bf16), jnp.where(head_mask, values, 0.0).astype(bf16)).astype(bf16)

    def pass_on(copies, number):
        def step(index, carry):
            copies(number - 1, index).wait_recv()
            copies(number, index).start()
            return carry

        lax.fori_loop(0, GROUP * CHUNKS, step, 0)

    def passed(copies, number):
        def step(index, carry):
            copies(number, index).wait_send()
            return carry

        lax.fori_loop(0, GROUP * CHUNKS, step, 0)

    def fac_out():
        copy = local_copy(21, fac, o_fac)
        copy.start()
        copy.wait()

    @pl.when(me == 2)
    def _():
        weights = weights_in(6)
        x = moved(gathered_rows(2).astype(bf16), 0, 0)
        for c in weights:
            c.wait()
        gain_self = gain_ref[0:1, :]
        gain_cross = gain_ref[1:2, :]
        inverse_self = inverse_rms(x)
        normed_self = x * inverse_self
        a2 = (normed_self * gain_self).astype(bf16)
        sv = nn(a2, block(0)).astype(bf16)
        middle = x + nn(sv, block(1))
        inverse_cross = inverse_rms(middle)
        normed_cross = middle * inverse_cross
        a3 = (normed_cross * gain_cross).astype(bf16)
        cq = nn(a3, block(2)).astype(bf16)
        qk[...] = nt(spread_heads(cq), block(3)).astype(bf16)
        qk_copy().start()
        pass_on(relay_copy, 1)
        for p in range(GROUP):
            mix_copy(p).wait_recv()
        co = join_heads(nn(mix[...], block(4)))
        state[...] = (middle + nn(co, block(5))).astype(bf16)
        state_copy().start()
        state_back_copy().wait_recv()
        dy = state_back[...]
        dco = nt(dy, block(5)).astype(bf16)
        gk[...] = nt(spread_heads(dco), block(4)).astype(bf16)
        g_copy().start()
        pass_on(back_relay_copy, 2)
        x_copy().wait_recv()
        dcq = join_heads(nn(xs[...], block(3)))
        grad_cross = nt(dcq, block(2))
        dm = dy.astype(f32) + norm_back(normed_cross, inverse_cross, gain_cross, grad_cross)
        dm_low = dm.astype(bf16)
        dsv = nt(dm_low, block(1)).astype(bf16)
        grad_self = nt(dsv, block(0))
        d_in = dm + norm_back(normed_self, inverse_self, gain_self, grad_self)
        rows_out[1] = d_in.astype(bf16)
        gain_sum[...] = jnp.zeros_like(gain_sum)
        gain_sum[0:1, :] = jnp.sum(grad_self * normed_self, axis=0, keepdims=True)
        gain_sum[1:2, :] = jnp.sum(grad_cross * normed_cross, axis=0, keepdims=True)
        fac[0:16, :] = packed([a2, dsv, sv, dm_low])
        fac[16:32, :] = packed([a3, dcq, co, dy])
        fac[32:48, :] = packed([cq, dco])
        fac[48:112, :] = xs[...]
        fac[112:176, :] = mix[...]
        for target in range(sections):
            if target != 2:
                out_small_copy(target, 1).start()
        own = local_copy(22, rows_out.at[1], o_small.at[1])
        own.start()
        fac_out()
        own.wait()
        for target in range(sections):
            if target != 2:
                out_small_copy(target, 1).wait_send()
        passed(relay_copy, 1)
        passed(back_relay_copy, 2)
        qk_copy().wait_send()
        state_copy().wait_send()
        g_copy().wait_send()

    @pl.when(me == 3)
    def _():
        weights = weights_in(8)
        d_out = moved(gathered_rows(3).astype(bf16), GROUP, 0)
        d_low = d_out.astype(bf16)
        for c in weights:
            c.wait()
        gain_row = gain_ref[0:1, :]
        pass_on(relay_copy, 2)
        state_copy().wait_recv()
        y = state[...].astype(f32)
        inverse = inverse_rms(y)
        normed = y * inverse
        a4 = (normed * gain_row).astype(bf16)
        r4 = []
        du4 = []
        result = y
        grad = jnp.zeros((16, D), f32)
        for b in range(4):
            r, slope = gelu_both(nn(a4, block(b)))
            r4.append(r.astype(bf16))
            result = result + nn(r4[b], block(4 + b))
            du4.append((nt(d_low, block(4 + b)) * slope).astype(bf16))
            grad = grad + nt(du4[b], block(b))
        state_back[...] = (d_out + norm_back(normed, inverse, gain_row, grad)).astype(bf16)
        state_back_copy().start()
        pass_on(back_relay_copy, 1)
        rows_out[0] = result.astype(bf16)
        gain_sum[...] = jnp.zeros_like(gain_sum)
        gain_sum[0:1, :] = jnp.sum(grad * normed, axis=0, keepdims=True)
        fac[...] = jnp.zeros_like(fac)
        fac[0:16, :] = packed([a4, d_low, r4[0], r4[1]])
        fac[16:32, :] = packed([r4[2], r4[3], du4[0], du4[1]])
        fac[32:48, :] = packed([du4[2], du4[3]])
        for target in range(sections):
            if target != 3:
                out_small_copy(target, 0).start()
        own = local_copy(22, rows_out.at[0], o_small.at[0])
        own.start()
        fac_out()
        own.wait()
        for target in range(sections):
            if target != 3:
                out_small_copy(target, 0).wait_send()
        passed(relay_copy, 2)
        passed(back_relay_copy, 1)
        state_back_copy().wait_send()

    gains_out = local_copy(23, gain_sum, o_gain)
    gains_out.start()

    @pl.when(me != 2)
    def _():
        dynamic_small_copy(2).wait_send()
        remote(
            places.out_small[0] + me * 2 + 1, rows_out.at[1], o_small.at[1], 2
        ).wait_recv()

    @pl.when(me != 3)
    def _():
        dynamic_small_copy(3).wait_send()
        remote(places.out_small[0] + me * 2, rows_out.at[0], o_small.at[0], 3).wait_recv()

    @pl.when(me != 0)
    def _():
        def step(p, carry):
            dynamic_enc_copy(p).wait_send()
            remote(
                places.out_enc[0] + me * GROUP + p, rows(H_ROWS, p * LEN, chunk_len), o_enc.at[p], 0
            ).wait_recv()
            return carry

        lax.fori_loop(0, GROUP, step, 0)

    gains_out.wait()


def relay_call(sections, enc_in, lengths, small_in, gain_rows, weights):
    places = Places(sections)
    any_space = pl.BlockSpec(memory_space=pl.ANY)
    return pl.pallas_call(
        functools.partial(relay_kernel, sections, places),
        out_shape=(
            jax.ShapeDtypeStruct(enc_in.shape, bf16),
            jax.ShapeDtypeStruct((2, 16, D), bf16),
            jax.ShapeDtypeStruct((8 * D, D), bf16),
            jax.ShapeDtypeStruct((FAC_ROWS, D), bf16),
            jax.ShapeDtypeStruct((8, D), f32),
        ),
        in_specs=[
            pl.BlockSpec(memory_space=pltpu.SMEM),
            any_space,
            any_space,
            any_space,
            pl.BlockSpec(memory_space=pltpu.VMEM),
        ],
        out_specs=(any_space,) * 5,
        scratch_shapes=[
            pltpu.VMEM((POOL_ROWS, D), bf16),
            pltpu.VMEM((WIDE_ROWS, 256), bf16),
            pltpu.VMEM((LEN, D), f32),
            pltpu.VMEM((64, LEN), f32),
            pltpu.VMEM((sections, 16, 256), bf16),
            pltpu.VMEM((64, D), bf16),
            pltpu.VMEM((64, D), bf16),
            pltpu.VMEM((64, D), bf16),
            pltpu.VMEM((64, D), bf16),
            pltpu.VMEM((16, D), bf16),
            pltpu.VMEM((16, D), bf16),
            pltpu.VMEM((FAC_ROWS, D), bf16),
            pltpu.VMEM((2, 16, D), bf16),
            pltpu.VMEM((8, D), f32),
            pltpu.SemaphoreType.DMA((places.count,)),
            pltpu.SemaphoreType.DMA((places.count,)),
            pltpu.SemaphoreType.DMA((24,)),
        ],
        compiler_params=pltpu.CompilerParams(
            collective_id=0, has_side_effects=True, vmem_limit_bytes=63 * 1024 * 1024
        ),
    )(lengths, enc_in, small_in, weights, gain_rows)


def terms_two(total, fac):
    def part(tile, i):
        return fac[:, 16 * tile + GROUP * i : 16 * tile + GROUP * (i + 1)].reshape(-1, D)

    def outer(a, b):
        return lax.dot_general(a, b, (((0,), (0,)), ((), ())), preferred_element_type=f32)

    def by_head(tall, short):
        tall = tall.reshape(-1, GROUP, 16, D)[:, :, :HEADS].reshape(-1, HEADS, D)
        short = short.reshape(-1, HEADS, HEAD)
        return jnp.einsum("phd,phf->dhf", tall, short, preferred_element_type=f32).reshape(D, D)

    blocks = [
        outer(part(0, 0), part(0, 1)),
        outer(part(0, 2), part(0, 3)),
        outer(part(1, 0), part(1, 1)),
        by_head(fac[:, 48:112], part(2, 0)),
        by_head(fac[:, 112:176], part(2, 1)),
        outer(part(1, 2), part(1, 3)),
    ]
    zero = jnp.zeros((D, D), f32)
    return jnp.stack(blocks + [zero, zero])


def terms_three(total, fac):
    def part(i):
        return fac[:, GROUP * i : GROUP * (i + 1)].reshape(-1, D)

    def outer(a, b):
        return lax.dot_general(a, b, (((0,), (0,)), ((), ())), preferred_element_type=f32)

    blocks = [outer(part(0), part(6 + b)) for b in range(4)]
    blocks += [outer(part(2 + b), part(1)) for b in range(4)]
    return jnp.stack(blocks)


def terms_zero(total, fac):
    zero = jnp.zeros((4, D, D), f32)
    return jnp.concatenate([total[:4].astype(f32), zero], axis=0)


def terms_one(total, fac):
    return total.astype(f32)


def local(enc_in, lengths, dec_in, gains, weights, d_out):
    section = lax.axis_index("section")
    sections = lax.axis_size("section")
    width = dec_in.shape[1]
    small = jnp.concatenate([dec_in, d_out], axis=0)
    small = jnp.pad(small, ((0, 16 - 2 * GROUP), (0, 256 - width)))
    gain_rows = jnp.pad(gains[0].astype(f32), ((0, 6), (0, 0)))
    d_enc, rows_out, partial, fac, gain_part = relay_call(
        sections, enc_in, lengths, small, gain_rows, weights[0].reshape(8 * D, D)
    )
    fac = lax.all_gather(fac, "dp", axis=0)
    total_gains = lax.psum(gain_part, "dp")[:2]
    total = lax.psum(partial.reshape(8, D, D), "dp")
    total_weights = lax.switch(
        section, [terms_zero, terms_one, terms_two, terms_three], total, fac
    )
    own = lax.dynamic_slice(rows_out, (0, 0, section * width), (2, GROUP, width))
    return (own[0], d_enc, own[1], total_gains[None], total_weights[None])


def solution(mesh):
    in_specs = (
        P("dp", "section", None),
        P("dp"),
        P("dp", "section"),
        P("section", None, None),
        P("section", None, None, None),
        P("dp", "section"),
    )
    out_specs = (
        P("dp", "section"),
        P("dp", "section", None),
        P("dp", "section"),
        P("section", None, None),
        P("section", None, None, None),
    )
    return jax.shard_map(local, mesh=mesh, in_specs=in_specs, out_specs=out_specs, check_vma=False)
```

```python
import functools
import math

import jax
import jax.numpy as jnp
from jax import lax
from jax.experimental import pallas as pl
from jax.experimental.pallas import tpu as pltpu
from jax.sharding import PartitionSpec as P

D = 768
HEADS = 12
HEAD = 64
PAIRS = HEADS // 2
LEN = 512
GROUP = 4
ROWS = GROUP * LEN
epsilon = 1e-06
masked_score = -1e30
gelu_coeff = 0.044715
gelu_scale = math.sqrt(2.0 / math.pi)
log2_e = 1.4426950408889634
bf16 = jnp.bfloat16
f32 = jnp.float32
MESH = pl.DeviceIdType.MESH

W_ROWS = 0
X_ROWS = 3072
Q_ROWS = X_ROWS + ROWS
K_ROWS = Q_ROWS + ROWS
V_ROWS = K_ROWS + ROWS
O_ROWS = V_ROWS + ROWS
H_ROWS = O_ROWS + ROWS
DH_ROWS = H_ROWS + ROWS
IL_ROWS = DH_ROWS + ROWS
POOL_ROWS = IL_ROWS + ROWS
FF_H = 6144
FF_A = FF_H + ROWS
FF_E = FF_A + ROWS
RELAY_F = 6144
GELU_ROWS = 12 * ROWS
WIDE_ROWS = 24 * ROWS

CHUNK = 64
CHUNKS = 4
RELAY = CHUNK * CHUNKS
DIRECT = LEN - RELAY
RELAY_B = RELAY_F + GROUP * RELAY
FAC_ROWS = 176
FAC_AT = 8192
HALF = D // 2
JOB = HALF // 2
OWN_BLOCKS = {0: (0, 1, 2), 1: (0, 2, 6, 3, 7)}
LENT_BLOCKS = {0: (3,), 1: (4, 1, 5)}


def nn(a, b):
    return jnp.dot(a, b, preferred_element_type=f32)


def nt(a, b):
    return lax.dot_general(a, b, (((1,), (1,)), ((), ())), preferred_element_type=f32)


def tn(a, b):
    return lax.dot_general(a, b, (((0,), (0,)), ((), ())), preferred_element_type=f32)


def iota(shape, axis):
    return lax.broadcasted_iota(jnp.int32, shape, axis)


def inverse_rms(v):
    return lax.rsqrt(jnp.mean(v * v, axis=-1, keepdims=True) + epsilon)


def norm_back(normed, inverse, gain_row, grad):
    scaled = grad * gain_row
    return inverse * (scaled - normed * jnp.mean(scaled * normed, axis=-1, keepdims=True))


def gelu_both(u):
    square = u * u
    tangent = jnp.tanh(gelu_scale * (u + gelu_coeff * square * u))
    half = 0.5 * (1.0 + tangent)
    slope = half + 0.5 * u * (1.0 - tangent * tangent) * (
        gelu_scale + 3.0 * gelu_coeff * gelu_scale * square
    )
    return (u * half, slope)


class Places:
    def __init__(self, sections, bits):
        self.count = 0
        self.enc = [self.take(GROUP) for _ in range(sections)]
        self.small = [self.take(2) for _ in range(sections)]
        self.direct = self.take(GROUP)
        self.relay = [self.take(GROUP * CHUNKS) for _ in range(3)]
        self.back_direct = self.take(GROUP)
        self.back_relay = [self.take(GROUP * CHUNKS) for _ in range(3)]
        self.qk = self.take(1)
        self.mix = self.take(GROUP)
        self.state = self.take(1)
        self.state_back = self.take(1)
        self.g = self.take(1)
        self.x = self.take(1)
        self.out_enc = [self.take(GROUP) for _ in range(sections)]
        self.out_small = [self.take(2) for _ in range(sections)]
        self.halves = self.take(8)
        self.lend = self.take(8)
        self.lent = self.take(8)
        self.whole = self.take(8)
        self.down = [self.take(16) for _ in range(bits)]
        self.up = [self.take(16) for _ in range(3)]
        self.facs = self.take(bits)
        self.gains = self.take(bits)

    def take(self, amount):
        first = self.count
        self.count += amount
        return first


def relay_kernel(
    sections,
    bits,
    places,
    len_ref,
    enc_ref,
    small_ref,
    w_ref,
    gain_ref,
    o_enc,
    o_small,
    o_dw,
    o_gain,
    pool,
    wide,
    acc,
    cp,
    small,
    qk,
    mix,
    gk,
    xs,
    state,
    state_back,
    fac,
    rows_out,
    gain_sum,
    gain_in,
    send_sem,
    recv_sem,
    local_sem,
    ready_sem,
):
    me = lax.axis_index("section")
    group = lax.axis_index("dp")
    chunk_len = LEN // sections

    def remote(number, src, dst, target):
        return pltpu.make_async_remote_copy(
            src_ref=src,
            dst_ref=dst,
            send_sem=send_sem.at[number],
            recv_sem=recv_sem.at[number],
            device_id=(target, group),
            device_id_type=MESH,
        )

    def local_copy(number, src, dst):
        return pltpu.make_async_copy(src, dst, local_sem.at[number])

    def rows(base, start, count):
        return pool.at[pl.ds(pl.multiple_of(base + start, 16), count)]

    def out_rows(start, count):
        return o_dw.at[pl.ds(pl.multiple_of(start, 16), count)]

    bit = [lax.rem(group // 2**k, 2) for k in range(bits)]
    partner = [group + 2**k * (1 - 2 * bit[k]) for k in range(bits)]

    def across(number, src, dst, k):
        return pltpu.make_async_remote_copy(
            src_ref=src,
            dst_ref=dst,
            send_sem=send_sem.at[number],
            recv_sem=recv_sem.at[number],
            device_id=(me, partner[k]),
            device_id_type=MESH,
        )

    barrier = pltpu.get_barrier_semaphore()
    for step in range(1, sections):
        pl.semaphore_signal(
            barrier,
            inc=1,
            device_id=(lax.rem(me + step, sections), group),
            device_id_type=MESH,
        )
    for k in range(bits):
        pl.semaphore_signal(barrier, inc=1, device_id=(me, partner[k]), device_id_type=MESH)
    pl.semaphore_wait(barrier, sections - 1 + bits)

    lane = iota((1, 128), 1)
    low_half = lane < HEAD

    def enc_copy(sender, p):
        return remote(
            places.enc[sender] + p,
            enc_ref.at[p],
            rows(X_ROWS, p * LEN + sender * chunk_len, chunk_len),
            0,
        )

    def small_copy(sender, target):
        return remote(places.small[sender] + target - 2, small_ref, small.at[sender], target)

    def direct_copy(p):
        return remote(
            places.direct + p, rows(H_ROWS, p * LEN, DIRECT), rows(FF_H, p * LEN, DIRECT), 1
        )

    def relay_copy(hop, index):
        p = index // CHUNKS
        piece = index % CHUNKS
        whole = p * LEN + DIRECT + piece * CHUNK
        src = rows(H_ROWS, whole, CHUNK) if hop == 0 else rows(RELAY_F, index * CHUNK, CHUNK)
        dst = rows(FF_H, whole, CHUNK) if hop == 2 else rows(RELAY_F, index * CHUNK, CHUNK)
        return remote(places.relay[hop] + index, src, dst, (2, 3, 1)[hop])

    def back_direct_copy(p):
        return remote(
            places.back_direct + p, rows(FF_H, p * LEN, DIRECT), rows(DH_ROWS, p * LEN, DIRECT), 0
        )

    def back_relay_copy(hop, index):
        p = index // CHUNKS
        piece = index % CHUNKS
        whole = p * LEN + DIRECT + piece * CHUNK
        src = rows(FF_H, whole, CHUNK) if hop == 0 else rows(RELAY_B, index * CHUNK, CHUNK)
        dst = rows(DH_ROWS, whole, CHUNK) if hop == 2 else rows(RELAY_B, index * CHUNK, CHUNK)
        return remote(places.back_relay[hop] + index, src, dst, (3, 2, 0)[hop])

    def qk_copy():
        return remote(places.qk, qk, qk, 1)

    def mix_copy(p):
        part = pl.ds(pl.multiple_of(p * 16, 16), 16)
        return remote(places.mix + p, mix.at[part], mix.at[part], 2)

    def state_copy():
        return remote(places.state, state, state, 3)

    def state_back_copy():
        return remote(places.state_back, state_back, state_back, 2)

    def g_copy():
        return remote(places.g, gk, gk, 1)

    def x_copy():
        return remote(places.x, xs, xs, 2)

    def out_enc_copy(target, p):
        return remote(
            places.out_enc[target] + p,
            rows(H_ROWS, p * LEN + target * chunk_len, chunk_len),
            o_enc.at[p],
            target,
        )

    def out_small_copy(target, kind):
        return remote(
            places.out_small[target] + kind, rows_out.at[kind], o_small.at[kind], target
        )

    def each_passage(body):
        def step(p, carry):
            body(p)
            return carry

        lax.fori_loop(0, GROUP, step, 0)

    def weights_in(blocks):
        copies = [
            local_copy(
                i,
                w_ref.at[pl.ds(i * D, D)],
                pool.at[pl.ds(W_ROWS + i * D, D)],
            )
            for i in range(blocks)
        ]
        for c in copies:
            c.start()
        return copies

    def block(i):
        return pool[W_ROWS + i * D : W_ROWS + (i + 1) * D, :]

    def send_inputs():
        def step(p, carry):
            enc_copy(me, p).start()
            return carry

        lax.fori_loop(0, GROUP, step, 0)

    def dynamic_enc_copy(p):
        number = places.enc[0] + me * GROUP + p
        return remote(
            number, enc_ref.at[p], rows(X_ROWS, p * LEN + me * chunk_len, chunk_len), 0
        )

    def dynamic_small_copy(target):
        number = places.small[0] + me * 2 + target - 2
        return remote(number, small_ref, small.at[me], target)

    @pl.when(me != 2)
    def _():
        dynamic_small_copy(2).start()

    @pl.when(me != 3)
    def _():
        dynamic_small_copy(3).start()

    @pl.when(me != 0)
    def _():
        each_passage(lambda p: dynamic_enc_copy(p).start())

    def halves_copy(n, landing):
        return across(
            places.halves + n,
            rows(W_ROWS + n * D, (1 - bit[0]) * HALF, HALF),
            rows(landing, n * HALF, HALF),
            0,
        )

    def add_rows(at, landing, count):
        at = pl.ds(pl.multiple_of(at, 16), count)
        landed = pl.ds(pl.multiple_of(landing, 16), count)
        pool[at, :] = (pool[at, :].astype(f32) + pool[landed, :].astype(f32)).astype(bf16)

    def add_halves(n, landing):
        halves_copy(n, landing).wait_recv()
        add_rows(W_ROWS + n * D + bit[0] * HALF, landing + n * HALF, HALF)

    def lend_copy(n, index, landing):
        return remote(
            places.lend + n,
            rows(W_ROWS + n * D, bit[0] * HALF, HALF),
            rows(landing, index * HALF, HALF),
            lax.rem(me + 2, sections),
        )

    def lent_copy(n, index, result):
        return remote(
            places.lent + n,
            rows(result, index * HALF, HALF),
            out_rows(n * D + bit[0] * HALF, HALF),
            lax.rem(me + 2, sections),
        )

    def whole_copy(n):
        half = out_rows(n * D + bit[0] * HALF, HALF)
        return across(places.whole + n, half, half, 0)

    class Job:
        def __init__(self, n, i, at, landing, index, count, result):
            self.number = 2 * n + i
            self.at = at
            self.result = result
            self.keep = [at]
            self.size = [JOB]
            self.landing = [None]
            place = landing
            for k in range(1, bits):
                halved = k < 3
                size = self.size[-1] // 2 if halved else self.size[-1]
                self.keep.append(self.keep[-1] + bit[k] * size if halved else self.keep[-1])
                self.size.append(size)
                self.landing.append(place + index * size)
                place = place + count * size

        def down(self, k):
            size = self.size[k]
            src = self.keep[k - 1] + (1 - bit[k]) * size if k < 3 else self.keep[k]
            return across(
                places.down[k] + self.number, rows(src, 0, size), rows(self.landing[k], 0, size), k
            )

        def take(self, k):
            self.down(k).wait_recv()
            if k >= 3:
                self.down(k).wait_send()
            add_rows(self.keep[k], self.landing[k], self.size[k])

        def own(self):
            return local_copy(
                24 + self.number, rows(self.keep[2], 0, self.size[2]), self.result(self.keep[2], self.size[2])
            )

        def up(self, k):
            place = self.result(self.keep[k], self.size[k])
            src = rows(self.keep[2], 0, self.size[2]) if k == 2 else place
            return across(places.up[k] + self.number, src, place, k)

        def one(self):
            self.down(1).start()

        def two(self):
            self.take(1)
            self.down(2).start()

        def three(self):
            self.take(2)
            for k in range(3, bits):
                self.down(k).start()
                self.take(k)
            self.own().start()
            self.up(2).start()

        def four(self):
            self.up(2).wait_recv()
            self.own().wait()
            self.up(1).start()

        def five(self):
            self.up(1).wait_recv()

        def end(self):
            for k in range(1, min(bits, 3)):
                self.down(k).wait_send()
                self.up(k).wait_send()

    def own_jobs(section, blocks, landing):
        return [
            Job(
                n,
                i,
                W_ROWS + n * D + bit[0] * HALF + i * JOB,
                landing,
                2 * index + i,
                2 * len(blocks),
                lambda at, size: out_rows(at - W_ROWS, size),
            )
            for index, n in enumerate(blocks)
            for i in range(2)
        ]

    def lent_jobs(section, blocks, arrived, landing, result):
        return [
            Job(
                n,
                i,
                arrived + index * HALF + i * JOB,
                landing,
                2 * index + i,
                2 * len(blocks),
                lambda at, size: rows(at - arrived + result, 0, size),
            )
            for index, n in enumerate(blocks)
            for i in range(2)
        ]

    def run_jobs(jobs, before, after, begun=0):
        count = len(jobs)
        for t in range(count + 4):
            if begun <= t < count:
                if t % 2 == 0:
                    before(t // 2)
                jobs[t].one()
            if 0 <= t - 1 < count:
                jobs[t - 1].two()
            if 0 <= t - 2 < count:
                jobs[t - 2].three()
            if 0 <= t - 3 < count:
                jobs[t - 3].four()
            if 0 <= t - 4 < count:
                jobs[t - 4].five()
                if (t - 4) % 2 == 1:
                    after((t - 4) // 2)

    def lent_sums(section, arrived, landing, result):
        blocks = LENT_BLOCKS[section]
        jobs = lent_jobs(section, blocks, arrived, landing, result)
        run_jobs(
            jobs,
            lambda index: lend_copy(blocks[index], index, arrived).wait_recv(),
            lambda index: lent_copy(blocks[index], index, result).start(),
        )
        for job in jobs:
            job.end()
        for index, n in enumerate(blocks):
            lent_copy(n, index, result).wait_send()

    def gain_copy(k):
        return across(places.gains + k, gain_sum, gain_in.at[k], k)

    def sum_gains(first, last):
        for k in range(first, last):
            gain_copy(k).start()
            gain_copy(k).wait()
            gain_sum[...] += gain_in[k]

    def gather_rows(width):
        own = local_copy(21, fac.at[pl.ds(0, width)], rows(FAC_AT, group * width, width))
        own.start()
        own.wait()
        for k in range(bits):
            held = rows(FAC_AT, (group // 2**k) * 2**k * width, 2**k * width)
            copy = across(places.facs + k, held, held, k)
            copy.start()
            copy.wait()

    batch = min(2**bits, 8)

    def gathered_tile(width, first, count, part):
        return jnp.concatenate(
            [
                pool[
                    pl.ds(
                        pl.multiple_of(FAC_AT + (part * batch + i) * width + first, 16), count
                    ),
                    :,
                ]
                for i in range(batch)
            ],
            axis=0,
        )

    def store_block(n, sides):
        for c in range(3):
            columns = slice(256 * c, 256 * (c + 1))

            def term(part):
                left, right = sides(part)
                return tn(left, right[:, columns])

            if 2**bits == batch:
                total = term(0)
            else:
                total = lax.fori_loop(
                    0,
                    2**bits // batch,
                    lambda i, total: total + term(i),
                    jnp.zeros((D, 256), f32),
                )
            pool[W_ROWS + n * D : W_ROWS + (n + 1) * D, columns] = total.astype(bf16)
        local_copy(n, rows(W_ROWS + n * D, 0, D), out_rows(n * D, D)).start()

    def aligned(tile, i, j):
        count = tile.shape[0]
        row, column = iota((count, count), 0), iota((count, count), 1)
        member = row & 15
        pick = (column - row == GROUP * (j - i)) & (member >= GROUP * i) & (member < GROUP * (i + 1))
        return nn(jnp.where(pick, 1.0, 0.0).astype(bf16), tile).astype(bf16)

    def blocks_stored(count):
        for n in range(count):
            local_copy(n, rows(W_ROWS + n * D, 0, D), out_rows(n * D, D)).wait()

    @pl.when(me == 0)
    def _():
        own = [
            local_copy(8 + p, enc_ref.at[p], pool.at[pl.ds(X_ROWS + p * LEN, chunk_len)])
            for p in range(GROUP)
        ]
        for c in own:
            c.start()
        weights = weights_in(4)
        for c in weights:
            c.wait()
        for c in own:
            c.wait()
        gain_row = gain_ref[0:1, :]
        key_row = iota((LEN, 1), 0)

        def pair_columns(hp):
            return pl.ds(pl.multiple_of(hp * 128, 128), 128)

        def forward(p):
            for sender in range(1, sections):
                enc_copy(sender, p).wait_recv()
            start = pl.multiple_of(p * LEN, LEN)
            x = pool[pl.ds(X_ROWS + start, LEN), :].astype(f32)
            a0 = (x * inverse_rms(x) * gain_row).astype(bf16)
            pool[pl.ds(Q_ROWS + start, LEN), :] = (nn(a0, block(0)) * log2_e).astype(bf16)
            pool[pl.ds(K_ROWS + start, LEN), :] = nn(a0, block(1)).astype(bf16)
            pool[pl.ds(V_ROWS + start, LEN), :] = nn(a0, block(2)).astype(bf16)
            bias = jnp.where(key_row < len_ref[p], 0.0, masked_score).astype(bf16)

            def pair(hp, carry):
                c = pair_columns(hp)
                q2 = pool[pl.ds(Q_ROWS + start, LEN), c]
                k2 = pool[pl.ds(K_ROWS + start, LEN), c]
                v2 = pool[pl.ds(V_ROWS + start, LEN), c]
                one = jnp.ones_like(q2)
                zero = jnp.zeros_like(q2)
                queries = [
                    jnp.where(low_half, q2, jnp.where(lane == HEAD, one, zero)),
                    jnp.where(low_half, jnp.where(lane == 0, one, zero), q2),
                ]
                keys = [
                    jnp.where(low_half, k2, jnp.where(lane == HEAD, bias, zero)),
                    jnp.where(low_half, jnp.where(lane == 0, bias, zero), k2),
                ]
                values = [jnp.where(low_half, v2, one), jnp.where(low_half, one, v2)]
                mixes = []
                for half in range(2):
                    s = nt(queries[half], keys[half])
                    e = jnp.exp2(s - jnp.max(s, axis=-1, keepdims=True)).astype(bf16)
                    at = pl.multiple_of((p * HEADS + hp * 2 + half) * 2 * LEN, 2 * LEN)
                    wide[pl.ds(at, LEN), :] = e[:, :256]
                    wide[pl.ds(at + LEN, LEN), :] = e[:, 256:]
                    mixes.append(nn(e, values[half]))
                total = pltpu.roll(jnp.where(low_half, mixes[1], mixes[0]), HEAD, 1)
                inverse = 1.0 / total
                pool[pl.ds(O_ROWS + start, LEN), c] = (
                    jnp.where(low_half, mixes[0], mixes[1]) * inverse
                ).astype(bf16)
                pool[pl.ds(IL_ROWS + start, LEN), c] = inverse.astype(bf16)
                return carry

            lax.fori_loop(0, PAIRS, pair, 0)
            h = x + nn(pool[pl.ds(O_ROWS + start, LEN), :], block(3))
            pool[pl.ds(H_ROWS + start, LEN), :] = h.astype(bf16)
            direct_copy(p).start()
            for piece in range(CHUNKS):
                relay_copy(0, p * CHUNKS + piece).start()

        each_passage(forward)

        def sent(p):
            direct_copy(p).wait_send()
            for piece in range(CHUNKS):
                relay_copy(0, p * CHUNKS + piece).wait_send()

        each_passage(sent)
        gain_sum[...] = jnp.zeros_like(gain_sum)

        def backward(p):
            start = pl.multiple_of(p * LEN, LEN)
            back_direct_copy(p).wait_recv()
            for piece in range(CHUNKS):
                back_relay_copy(2, p * CHUNKS + piece).wait_recv()
            dh = pool[pl.ds(DH_ROWS + start, LEN), :]
            pool[pl.ds(H_ROWS + start, LEN), :] = nt(dh, block(3)).astype(bf16)

            def pair(hp, carry):
                c = pair_columns(hp)
                q2 = pool[pl.ds(Q_ROWS + start, LEN), c]
                k2 = pool[pl.ds(K_ROWS + start, LEN), c]
                v2 = pool[pl.ds(V_ROWS + start, LEN), c]
                da = pool[pl.ds(H_ROWS + start, LEN), c].astype(f32)
                mixed = pool[pl.ds(O_ROWS + start, LEN), c].astype(f32)
                da = da * pool[pl.ds(IL_ROWS + start, LEN), c].astype(f32)
                product = da * mixed
                da = da.astype(bf16)
                one = jnp.ones_like(q2)
                zero = jnp.zeros_like(q2)
                dq = []
                dk = []
                dv = []
                for half in range(2):
                    mine = low_half if half == 0 else lane >= HEAD
                    spare = HEAD if half == 0 else 0
                    centre = -jnp.sum(jnp.where(mine, product, 0.0), axis=-1, keepdims=True)
                    centre_high = centre.astype(bf16)
                    centre_low = (centre - centre_high.astype(f32)).astype(bf16)
                    da_own = jnp.where(mine, da, zero)
                    da_ext = jnp.where(
                        lane == spare,
                        centre_high,
                        jnp.where(lane == spare + 1, centre_low, da_own),
                    )
                    at = pl.multiple_of((p * HEADS + hp * 2 + half) * 2 * LEN, 2 * LEN)
                    e = jnp.concatenate(
                        [wide[pl.ds(at, LEN), :], wide[pl.ds(at + LEN, LEN), :]], axis=1
                    )
                    ds = e * nt(da_ext, jnp.where(mine, v2, one)).astype(bf16)
                    dq.append(nn(ds, k2))
                    dk.append(nn(jnp.where(mine, q2, zero).T, ds))
                    dv.append(nn(da_own.T, e))
                pool[pl.ds(Q_ROWS + start, LEN), c] = jnp.where(low_half, dq[0], dq[1]).astype(bf16)
                pool[pl.ds(K_ROWS + start, LEN), c] = (
                    (dk[0] + dk[1]).T * (1.0 / log2_e)
                ).astype(bf16)
                pool[pl.ds(V_ROWS + start, LEN), c] = (dv[0] + dv[1]).T.astype(bf16)
                return carry

            lax.fori_loop(0, PAIRS, pair, 0)
            grad = (
                nt(pool[pl.ds(Q_ROWS + start, LEN), :], block(0))
                + nt(pool[pl.ds(K_ROWS + start, LEN), :], block(1))
                + nt(pool[pl.ds(V_ROWS + start, LEN), :], block(2))
            )
            x = pool[pl.ds(X_ROWS + start, LEN), :].astype(f32)
            inverse = inverse_rms(x)
            normed = x * inverse
            d_in = dh.astype(f32) + norm_back(normed, inverse, gain_row, grad)
            pool[pl.ds(H_ROWS + start, LEN), :] = d_in.astype(bf16)
            gain_sum[0:1, :] += jnp.sum(grad * normed, axis=0, keepdims=True)
            pool[pl.ds(X_ROWS + start, LEN), :] = (normed * gain_row).astype(bf16)
            for target in range(1, sections):
                out_enc_copy(target, p).start()
            local_copy(8 + p, rows(H_ROWS, start, chunk_len), o_enc.at[p]).start()

        each_passage(backward)
        pl.semaphore_signal(
            ready_sem.at[0], inc=1, device_id=(me, partner[0]), device_id_type=MESH
        )
        sides = (
            (X_ROWS, Q_ROWS),
            (X_ROWS, K_ROWS),
            (X_ROWS, V_ROWS),
            (O_ROWS, DH_ROWS),
        )
        order = LENT_BLOCKS[0] + OWN_BLOCKS[0]
        jobs = own_jobs(0, OWN_BLOCKS[0], H_ROWS)

        def compute(n):
            left, right = sides[n]

            def columns(k, carry):
                c = pl.ds(pl.multiple_of(k * 256, 256), 256)
                pool[pl.ds(W_ROWS + n * D, D), c] = tn(
                    pool[left : left + ROWS, :], pool[right : right + ROWS, c]
                ).astype(bf16)
                return carry

            lax.fori_loop(0, 3, columns, 0)

        compute(order[0])
        pl.semaphore_wait(ready_sem.at[0], 1)
        halves_copy(order[0], IL_ROWS).start()
        compute(order[1])
        halves_copy(order[1], IL_ROWS).start()
        add_halves(order[0], IL_ROWS)
        lend_copy(order[0], 0, 4608).start()

        def finish(p):
            for target in range(1, sections):
                out_enc_copy(target, p).wait_send()
            local_copy(8 + p, rows(H_ROWS, p * LEN, chunk_len), o_enc.at[p]).wait()

        each_passage(finish)
        for k in range(1, bits):
            pl.semaphore_signal(
                ready_sem.at[k], inc=1, device_id=(me, partner[k]), device_id_type=MESH
            )
        compute(order[2])
        halves_copy(order[2], IL_ROWS).start()
        for k in range(1, bits):
            pl.semaphore_wait(ready_sem.at[k], 1)
        add_halves(order[1], IL_ROWS)
        jobs[0].one()
        jobs[1].one()
        compute(order[3])
        halves_copy(order[3], IL_ROWS).start()
        add_halves(order[2], IL_ROWS)
        jobs[2].one()
        jobs[3].one()
        add_halves(order[3], IL_ROWS)
        jobs[4].one()
        jobs[5].one()
        run_jobs(
            jobs, lambda index: None, lambda index: whole_copy(OWN_BLOCKS[0][index]).start(), 6
        )
        sum_gains(0, bits)
        lent_copy(order[0], 0, 4608).wait_recv()
        whole_copy(order[0]).start()
        for n in order:
            whole_copy(n).wait()
            halves_copy(n, IL_ROWS).wait_send()
        lend_copy(order[0], 0, 4608).wait_send()
        for job in jobs:
            job.end()

    @pl.when(me == 1)
    def _():
        for c in weights_in(8):
            c.wait()
        gain_row = gain_ref[0:1, :]
        key_place = iota((1, LEN), 1)
        qk_copy().wait_recv()

        def tiles(b, p, base):
            return [
                pl.ds(pl.multiple_of(base + (3 * b + i) * ROWS + p * LEN, LEN), LEN)
                for i in range(3)
            ]

        def forward(p):
            start = pl.multiple_of(p * LEN, LEN)
            direct_copy(p).wait_recv()
            for piece in range(CHUNKS):
                relay_copy(2, p * CHUNKS + piece).wait_recv()
            h = pool[pl.ds(FF_H + start, LEN), :].astype(f32)
            a1 = (h * inverse_rms(h) * gain_row).astype(bf16)
            pool[pl.ds(FF_A + start, LEN), :] = a1
            acc[...] = h
            for b in range(4):
                r, slope = gelu_both(nn(a1, block(b)))
                r = r.astype(bf16)
                slope = slope.astype(bf16)
                for i, (at_r, at_s) in enumerate(zip(tiles(b, p, 0), tiles(b, p, GELU_ROWS))):
                    wide[at_r, :] = r[:, 256 * i : 256 * (i + 1)]
                    wide[at_s, :] = slope[:, 256 * i : 256 * (i + 1)]
                acc[...] += nn(r, block(4 + b))
            e = acc[...].astype(bf16)
            pool[pl.ds(FF_E + start, LEN), :] = e
            part = pl.ds(pl.multiple_of(p * 16, 16), 16)
            score = jnp.where(key_place < len_ref[p], nt(qk[part, :], e), masked_score)
            score = jnp.exp(score - jnp.max(score, axis=-1, keepdims=True))
            probs = score / jnp.sum(score, axis=-1, keepdims=True)
            cp[part, :] = probs
            mix[part, :] = nn(probs.astype(bf16), e).astype(bf16)
            mix_copy(p).start()

        each_passage(forward)
        each_passage(lambda p: mix_copy(p).wait_send())
        gain_sum[...] = jnp.zeros_like(gain_sum)
        g_copy().wait_recv()

        def backward(p):
            start = pl.multiple_of(p * LEN, LEN)
            part = pl.ds(pl.multiple_of(p * 16, 16), 16)
            e = pool[pl.ds(FF_E + start, LEN), :]
            probs = cp[part, :]
            d_probs = nt(gk[part, :], e)
            d_score = probs * (d_probs - jnp.sum(probs * d_probs, axis=-1, keepdims=True))
            d_score = d_score.astype(bf16)
            xs[part, :] = nn(d_score, e).astype(bf16)
            de = tn(d_score, qk[part, :]) + tn(probs.astype(bf16), gk[part, :])
            de = de.astype(bf16)
            pool[pl.ds(FF_E + start, LEN), :] = de
            for b in range(4):
                at = tiles(b, p, GELU_ROWS)
                slope = jnp.concatenate([wide[t, :] for t in at], axis=1)
                du = (nt(de, block(4 + b)) * slope.astype(f32)).astype(bf16)
                for i, t in enumerate(at):
                    wide[t, :] = du[:, 256 * i : 256 * (i + 1)]
                grad = nt(du, block(b))
                if b == 0:
                    acc[...] = grad
                else:
                    acc[...] += grad
            grad = acc[...]
            h = pool[pl.ds(FF_H + start, LEN), :].astype(f32)
            inverse = inverse_rms(h)
            normed = h * inverse
            dh = de.astype(f32) + norm_back(normed, inverse, gain_row, grad)
            gain_sum[0:1, :] += jnp.sum(grad * normed, axis=0, keepdims=True)
            pool[pl.ds(FF_H + start, LEN), :] = dh.astype(bf16)
            back_direct_copy(p).start()
            for piece in range(CHUNKS):
                back_relay_copy(0, p * CHUNKS + piece).start()

        each_passage(backward)
        x_copy().start()
        halves_at = FF_E + ROWS
        landing = halves_at + 8 * HALF

        def compute(k, carry):
            b = k // 2
            odd = lax.rem(k, 2)
            n = b + 4 * odd

            @pl.when(odd == 0)
            def _():
                for i in range(3):
                    at = pl.ds(pl.multiple_of(GELU_ROWS + (3 * b + i) * ROWS, ROWS), ROWS)
                    pool[
                        pl.ds(pl.multiple_of(W_ROWS + b * D, D), D), 256 * i : 256 * (i + 1)
                    ] = tn(pool[FF_A : FF_A + ROWS, :], wide[at, :]).astype(bf16)

            @pl.when(odd == 1)
            def _():
                for i in range(3):
                    at = pl.ds(pl.multiple_of((3 * b + i) * ROWS, ROWS), ROWS)
                    pool[
                        pl.ds(pl.multiple_of(W_ROWS + (4 + b) * D + 256 * i, 256), 256), :
                    ] = tn(wide[at, :], pool[FF_E : FF_E + ROWS, :]).astype(bf16)

            halves_copy(n, halves_at).start()
            return carry

        own = OWN_BLOCKS[1]
        lent = LENT_BLOCKS[1]
        jobs = own_jobs(1, own, landing)
        lax.fori_loop(0, 4, compute, 0)
        add_halves(own[0], halves_at)
        jobs[0].one()
        jobs[1].one()
        for index, n in enumerate(lent):
            add_halves(n, halves_at)
            lend_copy(n, index, 11264).start()
        lax.fori_loop(4, 6, compute, 0)
        jobs[0].two()
        jobs[1].two()
        add_halves(own[1], halves_at)
        jobs[2].one()
        jobs[3].one()
        lax.fori_loop(6, 8, compute, 0)
        for n, pair in zip(own[2:], ((4, 5), (6, 7), (8, 9))):
            add_halves(n, halves_at)
            for t in pair:
                jobs[t].one()
        jobs[0].three()
        jobs[1].three()
        jobs[2].two()
        jobs[3].two()
        jobs[0].four()
        jobs[2].three()
        jobs[1].four()
        jobs[3].three()
        jobs[0].five()
        jobs[1].five()
        whole_copy(own[0]).start()
        rest = jobs[4:]
        jobs[2].four()
        rest[0].two()
        jobs[3].four()
        rest[1].two()
        jobs[2].five()
        jobs[3].five()
        whole_copy(own[1]).start()
        sum_gains(0, bits)
        for t in range(2, len(rest) + 3):
            if t < len(rest):
                rest[t].two()
            if 0 <= t - 1 < len(rest):
                if t == 2:
                    rest[0].three()
                rest[t - 1].three()
            if 0 <= t - 2 < len(rest):
                rest[t - 2].four()
            if 0 <= t - 3 < len(rest):
                rest[t - 3].five()
                if (t - 3) % 2 == 1:
                    whole_copy(own[2 + (t - 3) // 2]).start()
        for index, n in enumerate(lent):
            lent_copy(n, index, 11264).wait_recv()
            whole_copy(n).start()
        for n in range(8):
            whole_copy(n).wait()
            halves_copy(n, halves_at).wait_send()
        for index, n in enumerate(lent):
            lend_copy(n, index, 11264).wait_send()
        for job in jobs:
            job.end()
        x_copy().wait_send()

        def sent(p):
            back_direct_copy(p).wait_send()
            for piece in range(CHUNKS):
                back_relay_copy(0, p * CHUNKS + piece).wait_send()

        each_passage(sent)

    def gathered_rows(own):
        copy = local_copy(20, small_ref, small.at[own])
        copy.start()
        for sender in range(sections):
            if sender != own:
                small_copy(sender, own).wait_recv()
        copy.wait()
        width = D // sections
        total = jnp.zeros((16, D), f32)
        for sender in range(sections):
            row, column = iota((256, D), 0), iota((256, D), 1)
            pick = jnp.where((column == row + width * sender) & (row < width), 1.0, 0.0)
            total = total + nn(small[sender], pick.astype(bf16))
        return total

    def moved(values, first, to):
        row, column = iota((16, 16), 0), iota((16, 16), 1)
        pick = (column - first == row - to) & (row >= to) & (row < to + GROUP)
        return nn(jnp.where(pick, 1.0, 0.0).astype(bf16), values)

    def packed(values):
        total = moved(values[0], 0, 0)
        for i, value in enumerate(values[1:]):
            total = total + moved(value, 0, GROUP * (i + 1))
        return total.astype(bf16)

    head_mask = (iota((64, D), 1) >> 6) == (iota((64, D), 0) & 15)

    def spread_heads(values):
        pick = jnp.where((iota((64, 16), 0) >> 4) == iota((64, 16), 1), 1.0, 0.0)
        return jnp.where(head_mask, nn(pick.astype(bf16), values), 0.0).astype(bf16)

    def join_heads(values):
        pick = jnp.where(iota((16, 64), 0) == (iota((16, 64), 1) >> 4), 1.0, 0.0)
        return nn(pick.astype(bf16), jnp.where(head_mask, values, 0.0).astype(bf16)).astype(bf16)

    def pass_on(copies, number):
        def step(index, carry):
            copies(number - 1, index).wait_recv()
            copies(number, index).start()
            return carry

        lax.fori_loop(0, GROUP * CHUNKS, step, 0)

    def passed(copies, number):
        def step(index, carry):
            copies(number, index).wait_send()
            return carry

        lax.fori_loop(0, GROUP * CHUNKS, step, 0)

    @pl.when(me == 2)
    def _():
        weights = weights_in(6)
        x = moved(gathered_rows(2).astype(bf16), 0, 0)
        for c in weights:
            c.wait()
        gain_self = gain_ref[0:1, :]
        gain_cross = gain_ref[1:2, :]
        inverse_self = inverse_rms(x)
        normed_self = x * inverse_self
        a2 = (normed_self * gain_self).astype(bf16)
        sv = nn(a2, block(0)).astype(bf16)
        middle = x + nn(sv, block(1))
        inverse_cross = inverse_rms(middle)
        normed_cross = middle * inverse_cross
        a3 = (normed_cross * gain_cross).astype(bf16)
        cq = nn(a3, block(2)).astype(bf16)
        qk[...] = nt(spread_heads(cq), block(3)).astype(bf16)
        qk_copy().start()
        pass_on(relay_copy, 1)
        for p in range(GROUP):
            mix_copy(p).wait_recv()
        co = join_heads(nn(mix[...], block(4)))
        state[...] = (middle + nn(co, block(5))).astype(bf16)
        state_copy().start()
        state_back_copy().wait_recv()
        dy = state_back[...]
        dco = nt(dy, block(5)).astype(bf16)
        gk[...] = nt(spread_heads(dco), block(4)).astype(bf16)
        g_copy().start()
        pass_on(back_relay_copy, 2)
        x_copy().wait_recv()
        dcq = join_heads(nn(xs[...], block(3)))
        grad_cross = nt(dcq, block(2))
        dm = dy.astype(f32) + norm_back(normed_cross, inverse_cross, gain_cross, grad_cross)
        dm_low = dm.astype(bf16)
        dsv = nt(dm_low, block(1)).astype(bf16)
        grad_self = nt(dsv, block(0))
        d_in = dm + norm_back(normed_self, inverse_self, gain_self, grad_self)
        rows_out[1] = d_in.astype(bf16)
        gain_sum[...] = jnp.zeros_like(gain_sum)
        gain_sum[0:1, :] = jnp.sum(grad_self * normed_self, axis=0, keepdims=True)
        gain_sum[1:2, :] = jnp.sum(grad_cross * normed_cross, axis=0, keepdims=True)
        fac[0:16, :] = packed([a2, dsv, sv, dm_low])
        fac[16:32, :] = packed([a3, dcq, co, dy])
        fac[32:48, :] = packed([cq, dco])
        fac[48:112, :] = xs[...]
        fac[112:176, :] = mix[...]
        for target in range(sections):
            if target != 2:
                out_small_copy(target, 1).start()
        own = local_copy(22, rows_out.at[1], o_small.at[1])
        own.start()
        gather_rows(FAC_ROWS)
        own.wait()
        sum_gains(0, bits)
        def pair_term(first, left, right):
            def term(part):
                tile = gathered_tile(FAC_ROWS, first, 16, part)
                return (tile, aligned(tile, left, right))

            return term

        store_block(0, pair_term(0, 0, 1))
        store_block(1, pair_term(0, 2, 3))
        store_block(2, pair_term(16, 0, 1))
        store_block(5, pair_term(16, 2, 3))

        def head_term(first, member):
            def term(part):
                tall, short = (64 * batch, 16 * batch)
                row, column = iota((tall, short), 0), iota((tall, short), 1)
                heads = (iota((tall, D), 1) >> 6) == (iota((tall, D), 0) & 15)
                pick = column == (row >> 6) * 16 + GROUP * member + ((row >> 4) & 3)
                short_rows = nn(
                    jnp.where(pick, 1.0, 0.0).astype(bf16), gathered_tile(FAC_ROWS, 32, 16, part)
                )
                short_rows = jnp.where(heads, short_rows, 0.0).astype(bf16)
                return (gathered_tile(FAC_ROWS, first, 64, part), short_rows)

            return term

        store_block(3, head_term(48, 0))
        store_block(4, head_term(112, 1))
        lent_sums(0, 4608, 4608 + 2 * HALF, 4608 + HALF)
        blocks_stored(6)
        for target in range(sections):
            if target != 2:
                out_small_copy(target, 1).wait_send()
        passed(relay_copy, 1)
        passed(back_relay_copy, 2)
        qk_copy().wait_send()
        state_copy().wait_send()
        g_copy().wait_send()

    @pl.when(me == 3)
    def _():
        weights = weights_in(8)
        d_out = moved(gathered_rows(3).astype(bf16), GROUP, 0)
        d_low = d_out.astype(bf16)
        for c in weights:
            c.wait()
        gain_row = gain_ref[0:1, :]
        pass_on(relay_copy, 2)
        state_copy().wait_recv()
        y = state[...].astype(f32)
        inverse = inverse_rms(y)
        normed = y * inverse
        a4 = (normed * gain_row).astype(bf16)
        r4 = []
        du4 = []
        result = y
        grad = jnp.zeros((16, D), f32)
        for b in range(4):
            r, slope = gelu_both(nn(a4, block(b)))
            r4.append(r.astype(bf16))
            result = result + nn(r4[b], block(4 + b))
            du4.append((nt(d_low, block(4 + b)) * slope).astype(bf16))
            grad = grad + nt(du4[b], block(b))
        state_back[...] = (d_out + norm_back(normed, inverse, gain_row, grad)).astype(bf16)
        state_back_copy().start()
        pass_on(back_relay_copy, 1)
        rows_out[0] = result.astype(bf16)
        gain_sum[...] = jnp.zeros_like(gain_sum)
        gain_sum[0:1, :] = jnp.sum(grad * normed, axis=0, keepdims=True)
        fac[...] = jnp.zeros_like(fac)
        fac[0:16, :] = packed([a4, d_low, r4[0], r4[1]])
        fac[16:32, :] = packed([r4[2], r4[3], du4[0], du4[1]])
        fac[32:48, :] = packed([du4[2], du4[3]])
        for target in range(sections):
            if target != 3:
                out_small_copy(target, 0).start()
        own = local_copy(22, rows_out.at[0], o_small.at[0])
        own.start()
        gather_rows(48)
        own.wait()
        sum_gains(0, bits)

        def member(slot, part):
            return aligned(gathered_tile(48, 16 * (slot // 4), 16, part), 0, slot % 4)

        for b in range(4):
            store_block(b, lambda part: (member(0, part), member(6 + b, part)))
            store_block(4 + b, lambda part: (member(2 + b, part), member(1, part)))
        lent_sums(1, 11264, 11264 + 6 * HALF, 11264 + 3 * HALF)
        blocks_stored(8)
        for target in range(sections):
            if target != 3:
                out_small_copy(target, 0).wait_send()
        passed(relay_copy, 2)
        passed(back_relay_copy, 1)
        state_back_copy().wait_send()

    gains_out = local_copy(23, gain_sum, o_gain)
    gains_out.start()

    @pl.when(me != 2)
    def _():
        dynamic_small_copy(2).wait_send()
        remote(
            places.out_small[0] + me * 2 + 1, rows_out.at[1], o_small.at[1], 2
        ).wait_recv()

    @pl.when(me != 3)
    def _():
        dynamic_small_copy(3).wait_send()
        remote(places.out_small[0] + me * 2, rows_out.at[0], o_small.at[0], 3).wait_recv()

    @pl.when(me != 0)
    def _():
        def step(p, carry):
            dynamic_enc_copy(p).wait_send()
            remote(
                places.out_enc[0] + me * GROUP + p, rows(H_ROWS, p * LEN, chunk_len), o_enc.at[p], 0
            ).wait_recv()
            return carry

        lax.fori_loop(0, GROUP, step, 0)

    gains_out.wait()


def relay_call(sections, bits, enc_in, lengths, small_in, gain_rows, weights):
    places = Places(sections, bits)
    any_space = pl.BlockSpec(memory_space=pl.ANY)
    return pl.pallas_call(
        functools.partial(relay_kernel, sections, bits, places),
        out_shape=(
            jax.ShapeDtypeStruct(enc_in.shape, bf16),
            jax.ShapeDtypeStruct((2, 16, D), bf16),
            jax.ShapeDtypeStruct((8 * D, D), bf16),
            jax.ShapeDtypeStruct((8, D), f32),
        ),
        in_specs=[
            pl.BlockSpec(memory_space=pltpu.SMEM),
            any_space,
            any_space,
            any_space,
            pl.BlockSpec(memory_space=pltpu.VMEM),
        ],
        out_specs=(any_space,) * 4,
        scratch_shapes=[
            pltpu.VMEM((POOL_ROWS, D), bf16),
            pltpu.VMEM((WIDE_ROWS, 256), bf16),
            pltpu.VMEM((LEN, D), f32),
            pltpu.VMEM((64, LEN), f32),
            pltpu.VMEM((sections, 16, 256), bf16),
            pltpu.VMEM((64, D), bf16),
            pltpu.VMEM((64, D), bf16),
            pltpu.VMEM((64, D), bf16),
            pltpu.VMEM((64, D), bf16),
            pltpu.VMEM((16, D), bf16),
            pltpu.VMEM((16, D), bf16),
            pltpu.VMEM((FAC_ROWS, D), bf16),
            pltpu.VMEM((2, 16, D), bf16),
            pltpu.VMEM((8, D), f32),
            pltpu.VMEM((bits, 8, D), f32),
            pltpu.SemaphoreType.DMA((places.count,)),
            pltpu.SemaphoreType.DMA((places.count,)),
            pltpu.SemaphoreType.DMA((40,)),
            pltpu.SemaphoreType.REGULAR((bits,)),
        ],
        compiler_params=pltpu.CompilerParams(
            collective_id=0, has_side_effects=True, vmem_limit_bytes=67_000_000
        ),
    )(lengths, enc_in, small_in, weights, gain_rows)


def local(enc_in, lengths, dec_in, gains, weights, d_out):
    section = lax.axis_index("section")
    sections = lax.axis_size("section")
    width = dec_in.shape[1]
    small = jnp.concatenate([dec_in, d_out], axis=0)
    small = jnp.pad(small, ((0, 16 - 2 * GROUP), (0, 256 - width)))
    gain_rows = jnp.pad(gains[0].astype(f32), ((0, 6), (0, 0)))
    bits = lax.axis_size("dp").bit_length() - 1
    d_enc, rows_out, total, total_gains = relay_call(
        sections, bits, enc_in, lengths, small, gain_rows, weights[0].reshape(8 * D, D)
    )
    used = jnp.where(section == 0, 4, jnp.where(section == 2, 6, 8))
    is_used = lax.broadcasted_iota(jnp.int32, (8, D, D), 0) < used
    total_weights = jnp.where(is_used, total.reshape(8, D, D).astype(f32), 0.0)
    own = lax.dynamic_slice(rows_out, (0, 0, section * width), (2, GROUP, width))
    return (own[0], d_enc, own[1], total_gains[None, :2], total_weights[None])


def solution(mesh):
    in_specs = (
        P("dp", "section", None),
        P("dp"),
        P("dp", "section"),
        P("section", None, None),
        P("section", None, None, None),
        P("dp", "section"),
    )
    out_specs = (
        P("dp", "section"),
        P("dp", "section", None),
        P("dp", "section"),
        P("section", None, None),
        P("section", None, None, None),
    )
    return jax.shard_map(local, mesh=mesh, in_specs=in_specs, out_specs=out_specs, check_vma=False)
```

```python
import functools
import math

import jax
import jax.numpy as jnp
from jax import lax
from jax.experimental import pallas as pl
from jax.experimental.pallas import tpu as pltpu
from jax.sharding import PartitionSpec as P

D = 768
HEADS = 12
HEAD = 64
PAIRS = HEADS // 2
LEN = 512
GROUP = 4
ROWS = GROUP * LEN
epsilon = 1e-06
masked_score = -1e30
gelu_coeff = 0.044715
gelu_scale = math.sqrt(2.0 / math.pi)
log2_e = 1.4426950408889634
bf16 = jnp.bfloat16
f32 = jnp.float32
MESH = pl.DeviceIdType.MESH

W_ROWS = 0
X_ROWS = 3072
Q_ROWS = X_ROWS + ROWS
K_ROWS = Q_ROWS + ROWS
V_ROWS = K_ROWS + ROWS
O_ROWS = V_ROWS + ROWS
IL_ROWS = O_ROWS + ROWS
H_ROWS = IL_ROWS + ROWS
DH_ROWS = H_ROWS + ROWS
POOL_ROWS = DH_ROWS + ROWS
FF_H = 6144
FF_A = FF_H + ROWS
FF_E = FF_A + ROWS
RELAY_F = 6144
GELU_ROWS = 12 * ROWS
WIDE_ROWS = 24 * ROWS

CHUNK = 64
CHUNKS = 4
RELAY = CHUNK * CHUNKS
DIRECT = LEN - RELAY
RELAY_B = RELAY_F + GROUP * RELAY
FAC_ROWS = 176
FAC_AT = 8192
HALF = D // 2
JOB = HALF // 2
OWN_BLOCKS = {0: (0, 1, 2), 1: (0, 2, 6, 3, 7)}
LENT_BLOCKS = {0: (3,), 1: (4, 1, 5)}


def nn(a, b):
    return jnp.dot(a, b, preferred_element_type=f32)


def nt(a, b):
    return lax.dot_general(a, b, (((1,), (1,)), ((), ())), preferred_element_type=f32)


def tn(a, b):
    return lax.dot_general(a, b, (((0,), (0,)), ((), ())), preferred_element_type=f32)


def iota(shape, axis):
    return lax.broadcasted_iota(jnp.int32, shape, axis)


def inverse_rms(v):
    return lax.rsqrt(jnp.mean(v * v, axis=-1, keepdims=True) + epsilon)


def norm_back(normed, inverse, gain_row, grad):
    scaled = grad * gain_row
    return inverse * (scaled - normed * jnp.mean(scaled * normed, axis=-1, keepdims=True))


def gelu_both(u):
    square = u * u
    tangent = jnp.tanh(gelu_scale * (u + gelu_coeff * square * u))
    half = 0.5 * (1.0 + tangent)
    slope = half + 0.5 * u * (1.0 - tangent * tangent) * (
        gelu_scale + 3.0 * gelu_coeff * gelu_scale * square
    )
    return (u * half, slope)


class Places:
    def __init__(self, sections, bits):
        self.count = 0
        self.enc = [self.take(GROUP) for _ in range(sections)]
        self.small = [self.take(2) for _ in range(sections)]
        self.direct = self.take(GROUP)
        self.relay = [self.take(GROUP * CHUNKS) for _ in range(3)]
        self.back_direct = self.take(GROUP)
        self.back_relay = [self.take(GROUP * CHUNKS) for _ in range(3)]
        self.qk = self.take(1)
        self.mix = self.take(GROUP)
        self.state = self.take(1)
        self.state_back = self.take(1)
        self.g = self.take(1)
        self.x = self.take(1)
        self.out_enc = [self.take(GROUP) for _ in range(sections)]
        self.out_small = [self.take(2) for _ in range(sections)]
        self.halves = self.take(8)
        self.lend = self.take(8)
        self.lent = self.take(8)
        self.whole = self.take(8)
        self.inward = self.take(16)
        self.middle = self.take(16)
        self.outward = self.take(16)
        self.facs = self.take(2 ** bits - 1)
        self.gains = self.take(bits)

    def take(self, amount):
        first = self.count
        self.count += amount
        return first


def relay_kernel(
    sections,
    bits,
    places,
    len_ref,
    enc_ref,
    small_ref,
    w_ref,
    gain_ref,
    o_enc,
    o_small,
    o_dw,
    o_gain,
    pool,
    wide,
    acc,
    cp,
    small,
    qk,
    mix,
    gk,
    xs,
    state,
    state_back,
    fac,
    rows_out,
    gain_sum,
    gain_in,
    send_sem,
    recv_sem,
    local_sem,
    ready_sem,
):
    me = lax.axis_index("section")
    group = lax.axis_index("dp")
    chunk_len = LEN // sections

    def remote(number, src, dst, target):
        return pltpu.make_async_remote_copy(
            src_ref=src,
            dst_ref=dst,
            send_sem=send_sem.at[number],
            recv_sem=recv_sem.at[number],
            device_id=(target, group),
            device_id_type=MESH,
        )

    def local_copy(number, src, dst):
        return pltpu.make_async_copy(src, dst, local_sem.at[number])

    def rows(base, start, count):
        return pool.at[pl.ds(pl.multiple_of(base + start, 16), count)]

    def out_rows(start, count):
        return o_dw.at[pl.ds(pl.multiple_of(start, 16), count)]

    bit = [lax.rem(group // 2**k, 2) for k in range(bits)]
    partner = [group + 2**k * (1 - 2 * bit[k]) for k in range(bits)]

    chips = 2 ** (bits - 1)
    chip = group // 2
    on_left = chip < chips // 2
    inward = jnp.where(on_left, group + 2, group - 2)
    outward = jnp.where(on_left, group - 2, group + 2)
    in_middle = (chip == chips // 2 - 1) | (chip == chips // 2)
    at_end = (chip == 0) | (chip == chips - 1)

    def along(number, src, dst, target):
        return pltpu.make_async_remote_copy(
            src_ref=src,
            dst_ref=dst,
            send_sem=send_sem.at[number],
            recv_sem=recv_sem.at[number],
            device_id=(me, target),
            device_id_type=MESH,
        )

    def across(number, src, dst, k):
        return pltpu.make_async_remote_copy(
            src_ref=src,
            dst_ref=dst,
            send_sem=send_sem.at[number],
            recv_sem=recv_sem.at[number],
            device_id=(me, partner[k]),
            device_id_type=MESH,
        )

    barrier = pltpu.get_barrier_semaphore()
    for step in range(1, sections):
        pl.semaphore_signal(
            barrier,
            inc=1,
            device_id=(lax.rem(me + step, sections), group),
            device_id_type=MESH,
        )
    for k in range(bits):
        pl.semaphore_signal(barrier, inc=1, device_id=(me, partner[k]), device_id_type=MESH)
    pl.semaphore_signal(barrier, inc=1, device_id=(me, inward), device_id_type=MESH)

    @pl.when(jnp.logical_not(at_end))
    def _():
        pl.semaphore_signal(barrier, inc=1, device_id=(me, outward), device_id_type=MESH)
        pl.semaphore_wait(barrier, sections + bits + 1)

    @pl.when(at_end)
    def _():
        pl.semaphore_wait(barrier, sections + bits)

    lane = iota((1, 128), 1)
    low_half = lane < HEAD

    def enc_copy(sender, p):
        return remote(
            places.enc[sender] + p,
            enc_ref.at[p],
            rows(X_ROWS, p * LEN + sender * chunk_len, chunk_len),
            0,
        )

    def small_copy(sender, target):
        return remote(places.small[sender] + target - 2, small_ref, small.at[sender], target)

    def direct_copy(p):
        return remote(
            places.direct + p, rows(H_ROWS, p * LEN, DIRECT), rows(FF_H, p * LEN, DIRECT), 1
        )

    def relay_copy(hop, index):
        p = index // CHUNKS
        piece = index % CHUNKS
        whole = p * LEN + DIRECT + piece * CHUNK
        src = rows(H_ROWS, whole, CHUNK) if hop == 0 else rows(RELAY_F, index * CHUNK, CHUNK)
        dst = rows(FF_H, whole, CHUNK) if hop == 2 else rows(RELAY_F, index * CHUNK, CHUNK)
        return remote(places.relay[hop] + index, src, dst, (2, 3, 1)[hop])

    def back_direct_copy(p):
        return remote(
            places.back_direct + p, rows(FF_H, p * LEN, DIRECT), rows(DH_ROWS, p * LEN, DIRECT), 0
        )

    def back_relay_copy(hop, index):
        p = index // CHUNKS
        piece = index % CHUNKS
        whole = p * LEN + DIRECT + piece * CHUNK
        src = rows(FF_H, whole, CHUNK) if hop == 0 else rows(RELAY_B, index * CHUNK, CHUNK)
        dst = rows(DH_ROWS, whole, CHUNK) if hop == 2 else rows(RELAY_B, index * CHUNK, CHUNK)
        return remote(places.back_relay[hop] + index, src, dst, (3, 2, 0)[hop])

    def qk_copy():
        return remote(places.qk, qk, qk, 1)

    def mix_copy(p):
        part = pl.ds(pl.multiple_of(p * 16, 16), 16)
        return remote(places.mix + p, mix.at[part], mix.at[part], 2)

    def state_copy():
        return remote(places.state, state, state, 3)

    def state_back_copy():
        return remote(places.state_back, state_back, state_back, 2)

    def g_copy():
        return remote(places.g, gk, gk, 1)

    def x_copy():
        return remote(places.x, xs, xs, 2)

    def out_enc_copy(target, p):
        return remote(
            places.out_enc[target] + p,
            rows(H_ROWS, p * LEN + target * chunk_len, chunk_len),
            o_enc.at[p],
            target,
        )

    def out_small_copy(target, kind):
        return remote(
            places.out_small[target] + kind, rows_out.at[kind], o_small.at[kind], target
        )

    def each_passage(body):
        def step(p, carry):
            body(p)
            return carry

        lax.fori_loop(0, GROUP, step, 0)

    def weights_in(blocks):
        copies = [
            local_copy(
                i,
                w_ref.at[pl.ds(i * D, D)],
                pool.at[pl.ds(W_ROWS + i * D, D)],
            )
            for i in range(blocks)
        ]
        for c in copies:
            c.start()
        return copies

    def block(i):
        return pool[W_ROWS + i * D : W_ROWS + (i + 1) * D, :]

    def send_inputs():
        def step(p, carry):
            enc_copy(me, p).start()
            return carry

        lax.fori_loop(0, GROUP, step, 0)

    def dynamic_enc_copy(p):
        number = places.enc[0] + me * GROUP + p
        return remote(
            number, enc_ref.at[p], rows(X_ROWS, p * LEN + me * chunk_len, chunk_len), 0
        )

    def dynamic_small_copy(target):
        number = places.small[0] + me * 2 + target - 2
        return remote(number, small_ref, small.at[me], target)

    @pl.when(me != 2)
    def _():
        dynamic_small_copy(2).start()

    @pl.when(me != 3)
    def _():
        dynamic_small_copy(3).start()

    @pl.when(me != 0)
    def _():
        each_passage(lambda p: dynamic_enc_copy(p).start())

    def halves_copy(n, landing):
        return across(
            places.halves + n,
            rows(W_ROWS + n * D, (1 - bit[0]) * HALF, HALF),
            rows(landing, n * HALF, HALF),
            0,
        )

    def add_rows(at, landing, count):
        at = pl.ds(pl.multiple_of(at, 16), count)
        landed = pl.ds(pl.multiple_of(landing, 16), count)
        pool[at, :] = (pool[at, :].astype(f32) + pool[landed, :].astype(f32)).astype(bf16)

    def add_halves(n, landing):
        halves_copy(n, landing).wait_recv()
        add_rows(W_ROWS + n * D + bit[0] * HALF, landing + n * HALF, HALF)

    def lend_copy(n, index, landing):
        return remote(
            places.lend + n,
            rows(W_ROWS + n * D, bit[0] * HALF, HALF),
            rows(landing, index * HALF, HALF),
            lax.rem(me + 2, sections),
        )

    def lent_copy(n, index, result):
        return remote(
            places.lent + n,
            rows(result, index * HALF, HALF),
            out_rows(n * D + bit[0] * HALF, HALF),
            lax.rem(me + 2, sections),
        )

    def whole_copy(n):
        half = out_rows(n * D + bit[0] * HALF, HALF)
        return across(places.whole + n, half, half, 0)

    class Job:
        def __init__(self, n, i, at, landing, index, result):
            self.number = 2 * n + i
            self.place = rows(at, 0, JOB)
            self.at = at
            self.from_out = landing + 2 * index * JOB
            self.from_in = landing + (2 * index + 1) * JOB
            self.result = result(at)

        def to_inward(self):
            return along(
                places.inward + self.number, self.place, rows(self.from_out, 0, JOB), inward
            )

        def to_middle(self):
            return along(
                places.middle + self.number, self.place, rows(self.from_in, 0, JOB), inward
            )

        def total_out(self):
            return along(places.outward + self.number, self.place, self.result, outward)

        def total_on(self):
            return along(places.outward + self.number, self.result, self.result, outward)

        def own(self):
            return local_copy(24 + self.number, self.place, self.result)

        def one(self):
            @pl.when(at_end)
            def _():
                self.to_inward().start()

        def two(self):
            @pl.when(jnp.logical_not(at_end))
            def _():
                self.to_inward().wait_recv()
                add_rows(self.at, self.from_out, JOB)

            if chips > 4:

                @pl.when(jnp.logical_not(at_end) & jnp.logical_not(in_middle))
                def _():
                    self.to_inward().start()

            @pl.when(in_middle)
            def _():
                self.to_middle().start()

        def three(self):
            @pl.when(in_middle)
            def _():
                self.to_middle().wait_recv()
                self.to_middle().wait_send()
                add_rows(self.at, self.from_in, JOB)
                self.own().start()
                self.total_out().start()

        def four(self):
            @pl.when(in_middle)
            def _():
                self.own().wait()

            @pl.when(jnp.logical_not(in_middle))
            def _():
                self.total_on().wait_recv()

            if chips > 4:

                @pl.when(jnp.logical_not(at_end) & jnp.logical_not(in_middle))
                def _():
                    self.total_on().start()

        def end(self):
            @pl.when(jnp.logical_not(in_middle))
            def _():
                self.to_inward().wait_send()

            @pl.when(in_middle)
            def _():
                self.total_out().wait_send()

            if chips > 4:

                @pl.when(jnp.logical_not(at_end) & jnp.logical_not(in_middle))
                def _():
                    self.total_on().wait_send()

    def own_jobs(blocks, landing):
        return [
            Job(
                n,
                i,
                W_ROWS + n * D + bit[0] * HALF + i * JOB,
                landing,
                2 * index + i,
                lambda at: out_rows(at - W_ROWS, JOB),
            )
            for index, n in enumerate(blocks)
            for i in range(2)
        ]

    def lent_jobs(blocks, arrived, landing, result):
        return [
            Job(
                n,
                i,
                arrived + index * HALF + i * JOB,
                landing,
                2 * index + i,
                lambda at: rows(at - arrived + result, 0, JOB),
            )
            for index, n in enumerate(blocks)
            for i in range(2)
        ]

    def finish_jobs(jobs, done, steps=()):
        count = len(jobs)
        steps = list(steps) + [1] * (count - len(steps))
        for t in range(count + 3):
            if t < count and steps[t] < 2:
                jobs[t].two()
            if 0 <= t - 1 < count and steps[t - 1] < 3:
                jobs[t - 1].three()
            if 0 <= t - 3 < count:
                jobs[t - 3].four()
                if (t - 3) % 2 == 1:
                    done((t - 3) // 2)

    def lent_sums(section, arrived, landing, result, between=()):
        blocks = LENT_BLOCKS[section]
        jobs = lent_jobs(blocks, arrived, landing, result)
        count = len(jobs)
        pieces = list(between)
        for t in range(count + 3):
            if t < count:
                if t % 2 == 0:
                    lend_copy(blocks[t // 2], t // 2, arrived).wait_recv()
                    jobs[t].one()
                    jobs[t + 1].one()
                if pieces and t % 2 == 0:
                    pieces.pop(0)()
                jobs[t].two()
            if pieces:
                pieces.pop(0)()
            if 0 <= t - 1 < count:
                jobs[t - 1].three()
            if 0 <= t - 3 < count:
                jobs[t - 3].four()
                if (t - 3) % 2 == 1:
                    lent_copy(blocks[(t - 3) // 2], (t - 3) // 2, result).start()
        for piece in pieces:
            piece()
        for job in jobs:
            job.end()
        for index, n in enumerate(blocks):
            lent_copy(n, index, result).wait_send()

    def gain_copy(k):
        return across(places.gains + k, gain_sum, gain_in.at[k], k)

    def gains_step(k, last=False):
        for step in range(k, bits + 1 if last else k + 1):
            if 0 < step <= bits:
                gain_copy(step - 1).wait()
                gain_sum[...] += gain_in[step - 1]
            if step < bits:
                gain_copy(step).start()

    def slot(width, core, place):
        return rows(FAC_AT, (core * chips + place) * width, width)

    def to_right(width, h):
        number = places.facs + 2 * (h - 1)
        place = slot(width, bit[0], chip - (h - 1))
        return along(number, place, place, group + 2)

    def to_left(width, h):
        number = places.facs + 2 * (h - 1) + 1
        place = slot(width, bit[0], chip + (h - 1))
        return along(number, place, place, group - 2)

    def from_left(width, h):
        number = places.facs + 2 * (h - 1)
        place = slot(width, bit[0], chip - h)
        return along(number, place, place, group - 2)

    def from_right(width, h):
        number = places.facs + 2 * (h - 1) + 1
        place = slot(width, bit[0], chip + h)
        return along(number, place, place, group + 2)

    def gather_first(width):
        own = local_copy(21, fac.at[pl.ds(0, width)], slot(width, bit[0], chip))
        own.start()
        own.wait()

    def gather_send(width, h, act):
        @pl.when((chip >= h - 1) & (chip < chips - 1))
        def _():
            act(to_right(width, h))

        @pl.when((chip + h - 1 <= chips - 1) & (chip > 0))
        def _():
            act(to_left(width, h))

    def gather_take(width, h):
        @pl.when(chip >= h)
        def _():
            from_left(width, h).wait_recv()

        @pl.when(chip + h <= chips - 1)
        def _():
            from_right(width, h).wait_recv()

    def gather_step(width, h, last=False):
        for step in range(h, chips + 1 if last else h + 1):
            if step > 1:
                gather_take(width, step - 1)
            if step < chips:
                gather_send(width, step, lambda copy: copy.start())

    def gather_cores(width):
        half = rows(FAC_AT, bit[0] * chips * width, chips * width)
        return across(places.facs + 2 * (chips - 1), half, half, 0)

    def gather_end(width):
        for h in range(1, chips):
            gather_send(width, h, lambda copy: copy.wait_send())

    batch = min(2**bits, 8)

    def gathered_tile(width, first, count, part):
        return jnp.concatenate(
            [
                pool[
                    pl.ds(
                        pl.multiple_of(FAC_AT + (part * batch + i) * width + first, 16), count
                    ),
                    :,
                ]
                for i in range(batch)
            ],
            axis=0,
        )

    def store_block(n, sides):
        for c in range(3):
            columns = slice(256 * c, 256 * (c + 1))

            def term(part):
                left, right = sides(part)
                return tn(left, right[:, columns])

            if 2**bits == batch:
                total = term(0)
            else:
                total = lax.fori_loop(
                    0,
                    2**bits // batch,
                    lambda i, total: total + term(i),
                    jnp.zeros((D, 256), f32),
                )
            pool[W_ROWS + n * D : W_ROWS + (n + 1) * D, columns] = total.astype(bf16)
        local_copy(n, rows(W_ROWS + n * D, 0, D), out_rows(n * D, D)).start()

    def aligned(tile, i, j):
        count = tile.shape[0]
        row, column = iota((count, count), 0), iota((count, count), 1)
        member = row & 15
        pick = (column - row == GROUP * (j - i)) & (member >= GROUP * i) & (member < GROUP * (i + 1))
        return nn(jnp.where(pick, 1.0, 0.0).astype(bf16), tile).astype(bf16)

    def blocks_stored(count):
        for n in range(count):
            local_copy(n, rows(W_ROWS + n * D, 0, D), out_rows(n * D, D)).wait()

    @pl.when(me == 0)
    def _():
        own = [
            local_copy(8 + p, enc_ref.at[p], pool.at[pl.ds(X_ROWS + p * LEN, chunk_len)])
            for p in range(GROUP)
        ]
        for c in own:
            c.start()
        weights = weights_in(4)
        for c in weights:
            c.wait()
        for c in own:
            c.wait()
        gain_row = gain_ref[0:1, :]
        key_row = iota((LEN, 1), 0)

        def pair_columns(hp):
            return pl.ds(pl.multiple_of(hp * 128, 128), 128)

        def forward(p):
            for sender in range(1, sections):
                enc_copy(sender, p).wait_recv()
            start = pl.multiple_of(p * LEN, LEN)
            x = pool[pl.ds(X_ROWS + start, LEN), :].astype(f32)
            a0 = (x * inverse_rms(x) * gain_row).astype(bf16)
            pool[pl.ds(Q_ROWS + start, LEN), :] = (nn(a0, block(0)) * log2_e).astype(bf16)
            pool[pl.ds(K_ROWS + start, LEN), :] = nn(a0, block(1)).astype(bf16)
            pool[pl.ds(V_ROWS + start, LEN), :] = nn(a0, block(2)).astype(bf16)
            bias = jnp.where(key_row < len_ref[p], 0.0, masked_score).astype(bf16)

            def pair(hp, carry):
                c = pair_columns(hp)
                q2 = pool[pl.ds(Q_ROWS + start, LEN), c]
                k2 = pool[pl.ds(K_ROWS + start, LEN), c]
                v2 = pool[pl.ds(V_ROWS + start, LEN), c]
                one = jnp.ones_like(q2)
                zero = jnp.zeros_like(q2)
                queries = [
                    jnp.where(low_half, q2, jnp.where(lane == HEAD, one, zero)),
                    jnp.where(low_half, jnp.where(lane == 0, one, zero), q2),
                ]
                keys = [
                    jnp.where(low_half, k2, jnp.where(lane == HEAD, bias, zero)),
                    jnp.where(low_half, jnp.where(lane == 0, bias, zero), k2),
                ]
                values = [jnp.where(low_half, v2, one), jnp.where(low_half, one, v2)]
                scores = [nt(queries[half], keys[half]) for half in range(2)]
                probs = [
                    jnp.exp2(s - jnp.max(s, axis=-1, keepdims=True)).astype(bf16) for s in scores
                ]
                for half, e in enumerate(probs):
                    at = pl.multiple_of((p * HEADS + hp * 2 + half) * 2 * LEN, 2 * LEN)
                    wide[pl.ds(at, LEN), :] = e[:, :256]
                    wide[pl.ds(at + LEN, LEN), :] = e[:, 256:]
                mixes = [nn(e, value) for e, value in zip(probs, values)]
                total = pltpu.roll(jnp.where(low_half, mixes[1], mixes[0]), HEAD, 1)
                inverse = 1.0 / total
                pool[pl.ds(O_ROWS + start, LEN), c] = (
                    jnp.where(low_half, mixes[0], mixes[1]) * inverse
                ).astype(bf16)
                pool[pl.ds(IL_ROWS + start, LEN), c] = inverse.astype(bf16)
                return carry

            lax.fori_loop(0, PAIRS, pair, 0)
            h = x + nn(pool[pl.ds(O_ROWS + start, LEN), :], block(3))
            pool[pl.ds(H_ROWS + start, LEN), :] = h.astype(bf16)
            direct_copy(p).start()
            for piece in range(CHUNKS):
                relay_copy(0, p * CHUNKS + piece).start()

        each_passage(forward)

        def sent(p):
            direct_copy(p).wait_send()
            for piece in range(CHUNKS):
                relay_copy(0, p * CHUNKS + piece).wait_send()

        each_passage(sent)
        gain_sum[...] = jnp.zeros_like(gain_sum)

        def backward(p):
            start = pl.multiple_of(p * LEN, LEN)
            back_direct_copy(p).wait_recv()
            for piece in range(CHUNKS):
                back_relay_copy(2, p * CHUNKS + piece).wait_recv()
            dh = pool[pl.ds(DH_ROWS + start, LEN), :]
            pool[pl.ds(H_ROWS + start, LEN), :] = nt(dh, block(3)).astype(bf16)

            def pair(hp, carry):
                c = pair_columns(hp)
                q2 = pool[pl.ds(Q_ROWS + start, LEN), c]
                k2 = pool[pl.ds(K_ROWS + start, LEN), c]
                v2 = pool[pl.ds(V_ROWS + start, LEN), c]
                da = pool[pl.ds(H_ROWS + start, LEN), c].astype(f32)
                mixed = pool[pl.ds(O_ROWS + start, LEN), c].astype(f32)
                da = da * pool[pl.ds(IL_ROWS + start, LEN), c].astype(f32)
                product = da * mixed
                da = da.astype(bf16)
                one = jnp.ones_like(q2)
                zero = jnp.zeros_like(q2)
                dq = []
                dk = []
                dv = []
                for half in range(2):
                    mine = low_half if half == 0 else lane >= HEAD
                    spare = HEAD if half == 0 else 0
                    centre = -jnp.sum(jnp.where(mine, product, 0.0), axis=-1, keepdims=True)
                    centre_high = centre.astype(bf16)
                    centre_low = (centre - centre_high.astype(f32)).astype(bf16)
                    da_own = jnp.where(mine, da, zero)
                    da_ext = jnp.where(
                        lane == spare,
                        centre_high,
                        jnp.where(lane == spare + 1, centre_low, da_own),
                    )
                    at = pl.multiple_of((p * HEADS + hp * 2 + half) * 2 * LEN, 2 * LEN)
                    e = jnp.concatenate(
                        [wide[pl.ds(at, LEN), :], wide[pl.ds(at + LEN, LEN), :]], axis=1
                    )
                    ds = e * nt(da_ext, jnp.where(mine, v2, one)).astype(bf16)
                    dq.append(nn(ds, k2))
                    dk.append(nn(jnp.where(mine, q2, zero).T, ds))
                    dv.append(nn(da_own.T, e))
                pool[pl.ds(Q_ROWS + start, LEN), c] = jnp.where(low_half, dq[0], dq[1]).astype(bf16)
                pool[pl.ds(K_ROWS + start, LEN), c] = (
                    (dk[0] + dk[1]).T * (1.0 / log2_e)
                ).astype(bf16)
                pool[pl.ds(V_ROWS + start, LEN), c] = (dv[0] + dv[1]).T.astype(bf16)
                return carry

            lax.fori_loop(0, PAIRS, pair, 0)
            grad = (
                nt(pool[pl.ds(Q_ROWS + start, LEN), :], block(0))
                + nt(pool[pl.ds(K_ROWS + start, LEN), :], block(1))
                + nt(pool[pl.ds(V_ROWS + start, LEN), :], block(2))
            )
            x = pool[pl.ds(X_ROWS + start, LEN), :].astype(f32)
            inverse = inverse_rms(x)
            normed = x * inverse
            d_in = dh.astype(f32) + norm_back(normed, inverse, gain_row, grad)
            pool[pl.ds(H_ROWS + start, LEN), :] = d_in.astype(bf16)
            gain_sum[0:1, :] += jnp.sum(grad * normed, axis=0, keepdims=True)
            pool[pl.ds(X_ROWS + start, LEN), :] = (normed * gain_row).astype(bf16)
            for target in range(1, sections):
                out_enc_copy(target, p).start()
            local_copy(8 + p, rows(H_ROWS, start, chunk_len), o_enc.at[p]).start()

        each_passage(backward)
        sides = (
            (X_ROWS, Q_ROWS),
            (X_ROWS, K_ROWS),
            (X_ROWS, V_ROWS),
            (O_ROWS, DH_ROWS),
        )
        order = LENT_BLOCKS[0] + OWN_BLOCKS[0]
        jobs = own_jobs(OWN_BLOCKS[0], O_ROWS)

        def compute(n):
            left, right = sides[n]

            def columns(k, carry):
                c = pl.ds(pl.multiple_of(k * 256, 256), 256)
                pool[pl.ds(W_ROWS + n * D, D), c] = tn(
                    pool[left : left + ROWS, :], pool[right : right + ROWS, c]
                ).astype(bf16)
                return carry

            lax.fori_loop(0, 3, columns, 0)

        gains_step(0)
        compute(order[0])
        gains_step(1)
        pl.semaphore_signal(
            ready_sem.at[0], inc=1, device_id=(me, partner[0]), device_id_type=MESH
        )

        @pl.when(in_middle)
        def _():
            pl.semaphore_signal(
                ready_sem.at[3], inc=1, device_id=(me, inward), device_id_type=MESH
            )

        @pl.when(jnp.logical_not(in_middle))
        def _():
            pl.semaphore_signal(
                ready_sem.at[1], inc=1, device_id=(me, inward), device_id_type=MESH
            )

        @pl.when(jnp.logical_not(at_end))
        def _():
            pl.semaphore_signal(
                ready_sem.at[2], inc=1, device_id=(me, outward), device_id_type=MESH
            )

        pl.semaphore_wait(ready_sem.at[0], 1)
        halves_copy(order[0], DH_ROWS).start()
        compute(order[1])
        gains_step(2)
        halves_copy(order[1], DH_ROWS).start()
        add_halves(order[0], DH_ROWS)
        lend_copy(order[0], 0, 4608).start()
        compute(order[2])
        gains_step(3, last=True)
        halves_copy(order[2], DH_ROWS).start()

        @pl.when(in_middle)
        def _():
            pl.semaphore_wait(ready_sem.at[3], 1)

        @pl.when(jnp.logical_not(in_middle))
        def _():
            pl.semaphore_wait(ready_sem.at[2], 1)

        @pl.when(jnp.logical_not(at_end))
        def _():
            pl.semaphore_wait(ready_sem.at[1], 1)

        add_halves(order[1], DH_ROWS)
        jobs[0].one()
        jobs[1].one()
        compute(order[3])
        halves_copy(order[3], DH_ROWS).start()
        add_halves(order[2], DH_ROWS)
        jobs[2].one()
        jobs[3].one()
        jobs[0].two()
        add_halves(order[3], DH_ROWS)
        jobs[4].one()
        jobs[5].one()
        finish_jobs(jobs, lambda index: whole_copy(OWN_BLOCKS[0][index]).start(), (2,))

        def finish(p):
            for target in range(1, sections):
                out_enc_copy(target, p).wait_send()
            local_copy(8 + p, rows(H_ROWS, p * LEN, chunk_len), o_enc.at[p]).wait()

        each_passage(finish)
        lent_copy(order[0], 0, 4608).wait_recv()
        whole_copy(order[0]).start()
        for n in order:
            whole_copy(n).wait()
            halves_copy(n, DH_ROWS).wait_send()
        lend_copy(order[0], 0, 4608).wait_send()
        for job in jobs:
            job.end()

    @pl.when(me == 1)
    def _():
        for c in weights_in(8):
            c.wait()
        gain_row = gain_ref[0:1, :]
        key_place = iota((1, LEN), 1)
        qk_copy().wait_recv()

        def tiles(b, p, base):
            return [
                pl.ds(pl.multiple_of(base + (3 * b + i) * ROWS + p * LEN, LEN), LEN)
                for i in range(3)
            ]

        def forward(p):
            start = pl.multiple_of(p * LEN, LEN)
            direct_copy(p).wait_recv()
            for piece in range(CHUNKS):
                relay_copy(2, p * CHUNKS + piece).wait_recv()
            h = pool[pl.ds(FF_H + start, LEN), :].astype(f32)
            a1 = (h * inverse_rms(h) * gain_row).astype(bf16)
            pool[pl.ds(FF_A + start, LEN), :] = a1
            acc[...] = h
            for b in range(4):
                r, slope = gelu_both(nn(a1, block(b)))
                r = r.astype(bf16)
                slope = slope.astype(bf16)
                for i, (at_r, at_s) in enumerate(zip(tiles(b, p, 0), tiles(b, p, GELU_ROWS))):
                    wide[at_r, :] = r[:, 256 * i : 256 * (i + 1)]
                    wide[at_s, :] = slope[:, 256 * i : 256 * (i + 1)]
                acc[...] += nn(r, block(4 + b))
            e = acc[...].astype(bf16)
            pool[pl.ds(FF_E + start, LEN), :] = e
            part = pl.ds(pl.multiple_of(p * 16, 16), 16)
            score = jnp.where(key_place < len_ref[p], nt(qk[part, :], e), masked_score)
            score = jnp.exp(score - jnp.max(score, axis=-1, keepdims=True))
            probs = score / jnp.sum(score, axis=-1, keepdims=True)
            cp[part, :] = probs
            mix[part, :] = nn(probs.astype(bf16), e).astype(bf16)
            mix_copy(p).start()

        each_passage(forward)
        each_passage(lambda p: mix_copy(p).wait_send())
        gain_sum[...] = jnp.zeros_like(gain_sum)
        g_copy().wait_recv()

        def backward(p):
            start = pl.multiple_of(p * LEN, LEN)
            part = pl.ds(pl.multiple_of(p * 16, 16), 16)
            e = pool[pl.ds(FF_E + start, LEN), :]
            probs = cp[part, :]
            d_probs = nt(gk[part, :], e)
            d_score = probs * (d_probs - jnp.sum(probs * d_probs, axis=-1, keepdims=True))
            d_score = d_score.astype(bf16)
            xs[part, :] = nn(d_score, e).astype(bf16)
            de = tn(d_score, qk[part, :]) + tn(probs.astype(bf16), gk[part, :])
            de = de.astype(bf16)
            pool[pl.ds(FF_E + start, LEN), :] = de
            for b in range(4):
                at = tiles(b, p, GELU_ROWS)
                slope = jnp.concatenate([wide[t, :] for t in at], axis=1)
                du = (nt(de, block(4 + b)) * slope.astype(f32)).astype(bf16)
                for i, t in enumerate(at):
                    wide[t, :] = du[:, 256 * i : 256 * (i + 1)]
                grad = nt(du, block(b))
                if b == 0:
                    acc[...] = grad
                else:
                    acc[...] += grad
            grad = acc[...]
            h = pool[pl.ds(FF_H + start, LEN), :].astype(f32)
            inverse = inverse_rms(h)
            normed = h * inverse
            dh = de.astype(f32) + norm_back(normed, inverse, gain_row, grad)
            gain_sum[0:1, :] += jnp.sum(grad * normed, axis=0, keepdims=True)
            pool[pl.ds(FF_H + start, LEN), :] = dh.astype(bf16)
            back_direct_copy(p).start()
            for piece in range(CHUNKS):
                back_relay_copy(0, p * CHUNKS + piece).start()

        each_passage(backward)
        x_copy().start()
        halves_at = FF_E + ROWS
        landing = halves_at + 8 * HALF

        def compute(n):
            b = n % 4
            for i in range(3):
                t = 3 * b + i
                if n < 4:
                    du = wide[GELU_ROWS + t * ROWS : GELU_ROWS + (t + 1) * ROWS, :]
                    pool[W_ROWS + n * D : W_ROWS + (n + 1) * D, 256 * i : 256 * (i + 1)] = tn(
                        pool[FF_A : FF_A + ROWS, :], du
                    ).astype(bf16)
                else:
                    first = W_ROWS + n * D + 256 * i
                    pool[first : first + 256, :] = tn(
                        wide[t * ROWS : (t + 1) * ROWS, :], pool[FF_E : FF_E + ROWS, :]
                    ).astype(bf16)
            halves_copy(n, halves_at).start()

        own = OWN_BLOCKS[1]
        lent = LENT_BLOCKS[1]
        jobs = own_jobs(own, landing)

        def begin(index):
            add_halves(own[index], halves_at)
            jobs[2 * index].one()
            jobs[2 * index + 1].one()

        def lend(index):
            add_halves(lent[index], halves_at)
            lend_copy(lent[index], index, 11264).start()

        gains_step(0)
        compute(own[0])
        gains_step(1)
        compute(lent[0])
        begin(0)
        gains_step(2)
        compute(lent[1])
        lend(0)
        gains_step(3, last=True)
        compute(lent[2])
        lend(1)
        jobs[0].two()
        compute(own[1])
        lend(2)
        jobs[1].two()
        compute(own[2])
        begin(1)
        jobs[0].three()
        compute(own[3])
        begin(2)
        jobs[1].three()
        jobs[2].two()
        compute(own[4])
        begin(3)
        jobs[3].two()
        jobs[2].three()
        begin(4)
        finish_jobs(jobs, lambda index: whole_copy(own[index]).start(), (3, 3, 3, 2))
        for index, n in enumerate(lent):
            lent_copy(n, index, 11264).wait_recv()
            whole_copy(n).start()
        for n in range(8):
            whole_copy(n).wait()
            halves_copy(n, halves_at).wait_send()
        for index, n in enumerate(lent):
            lend_copy(n, index, 11264).wait_send()
        for job in jobs:
            job.end()
        x_copy().wait_send()

        def sent(p):
            back_direct_copy(p).wait_send()
            for piece in range(CHUNKS):
                back_relay_copy(0, p * CHUNKS + piece).wait_send()

        each_passage(sent)

    def gathered_rows(own):
        copy = local_copy(20, small_ref, small.at[own])
        copy.start()
        for sender in range(sections):
            if sender != own:
                small_copy(sender, own).wait_recv()
        copy.wait()
        width = D // sections
        total = jnp.zeros((16, D), f32)
        for sender in range(sections):
            row, column = iota((256, D), 0), iota((256, D), 1)
            pick = jnp.where((column == row + width * sender) & (row < width), 1.0, 0.0)
            total = total + nn(small[sender], pick.astype(bf16))
        return total

    def moved(values, first, to):
        row, column = iota((16, 16), 0), iota((16, 16), 1)
        pick = (column - first == row - to) & (row >= to) & (row < to + GROUP)
        return nn(jnp.where(pick, 1.0, 0.0).astype(bf16), values)

    def packed(values):
        total = moved(values[0], 0, 0)
        for i, value in enumerate(values[1:]):
            total = total + moved(value, 0, GROUP * (i + 1))
        return total.astype(bf16)

    head_mask = (iota((64, D), 1) >> 6) == (iota((64, D), 0) & 15)

    def spread_heads(values):
        pick = jnp.where((iota((64, 16), 0) >> 4) == iota((64, 16), 1), 1.0, 0.0)
        return jnp.where(head_mask, nn(pick.astype(bf16), values), 0.0).astype(bf16)

    def join_heads(values):
        pick = jnp.where(iota((16, 64), 0) == (iota((16, 64), 1) >> 4), 1.0, 0.0)
        return nn(pick.astype(bf16), jnp.where(head_mask, values, 0.0).astype(bf16)).astype(bf16)

    def pass_on(copies, number):
        def step(index, carry):
            copies(number - 1, index).wait_recv()
            copies(number, index).start()
            return carry

        lax.fori_loop(0, GROUP * CHUNKS, step, 0)

    def passed(copies, number):
        def step(index, carry):
            copies(number, index).wait_send()
            return carry

        lax.fori_loop(0, GROUP * CHUNKS, step, 0)

    @pl.when(me == 2)
    def _():
        weights = weights_in(6)
        x = moved(gathered_rows(2).astype(bf16), 0, 0)
        for c in weights:
            c.wait()
        gain_self = gain_ref[0:1, :]
        gain_cross = gain_ref[1:2, :]
        inverse_self = inverse_rms(x)
        normed_self = x * inverse_self
        a2 = (normed_self * gain_self).astype(bf16)
        sv = nn(a2, block(0)).astype(bf16)
        middle = x + nn(sv, block(1))
        inverse_cross = inverse_rms(middle)
        normed_cross = middle * inverse_cross
        a3 = (normed_cross * gain_cross).astype(bf16)
        cq = nn(a3, block(2)).astype(bf16)
        qk[...] = nt(spread_heads(cq), block(3)).astype(bf16)
        qk_copy().start()
        pass_on(relay_copy, 1)
        for p in range(GROUP):
            mix_copy(p).wait_recv()
        co = join_heads(nn(mix[...], block(4)))
        state[...] = (middle + nn(co, block(5))).astype(bf16)
        state_copy().start()
        state_back_copy().wait_recv()
        dy = state_back[...]
        dco = nt(dy, block(5)).astype(bf16)
        gk[...] = nt(spread_heads(dco), block(4)).astype(bf16)
        g_copy().start()
        pass_on(back_relay_copy, 2)
        x_copy().wait_recv()
        dcq = join_heads(nn(xs[...], block(3)))
        grad_cross = nt(dcq, block(2))
        dm = dy.astype(f32) + norm_back(normed_cross, inverse_cross, gain_cross, grad_cross)
        dm_low = dm.astype(bf16)
        dsv = nt(dm_low, block(1)).astype(bf16)
        grad_self = nt(dsv, block(0))
        d_in = dm + norm_back(normed_self, inverse_self, gain_self, grad_self)
        rows_out[1] = d_in.astype(bf16)
        gain_sum[...] = jnp.zeros_like(gain_sum)
        gain_sum[0:1, :] = jnp.sum(grad_self * normed_self, axis=0, keepdims=True)
        gain_sum[1:2, :] = jnp.sum(grad_cross * normed_cross, axis=0, keepdims=True)
        fac[0:16, :] = packed([a2, dsv, sv, dm_low])
        fac[16:32, :] = packed([a3, dcq, co, dy])
        fac[32:48, :] = packed([cq, dco])
        fac[48:112, :] = xs[...]
        fac[112:176, :] = mix[...]
        for target in range(sections):
            if target != 2:
                out_small_copy(target, 1).start()
        own = local_copy(22, rows_out.at[1], o_small.at[1])
        own.start()
        gather_first(FAC_ROWS)
        gather_step(FAC_ROWS, 1)
        gains_step(0)
        own.wait()
        gains_step(1)
        gather_step(FAC_ROWS, 2)
        gains_step(2)
        gather_step(FAC_ROWS, 3)
        gains_step(3, last=True)
        gather_step(FAC_ROWS, 4, last=True)
        gather_cores(FAC_ROWS).start()
        gather_cores(FAC_ROWS).wait()
        gather_end(FAC_ROWS)
        def pair_term(first, left, right):
            def term(part):
                tile = gathered_tile(FAC_ROWS, first, 16, part)
                return (tile, aligned(tile, left, right))

            return term

        def head_term(first, member):
            def term(part):
                tall, short = (64 * batch, 16 * batch)
                row, column = iota((tall, short), 0), iota((tall, short), 1)
                heads = (iota((tall, D), 1) >> 6) == (iota((tall, D), 0) & 15)
                pick = column == (row >> 6) * 16 + GROUP * member + ((row >> 4) & 3)
                short_rows = nn(
                    jnp.where(pick, 1.0, 0.0).astype(bf16), gathered_tile(FAC_ROWS, 32, 16, part)
                )
                short_rows = jnp.where(heads, short_rows, 0.0).astype(bf16)
                return (gathered_tile(FAC_ROWS, first, 64, part), short_rows)

            return term

        lent_sums(
            0,
            4608,
            4608 + 2 * HALF,
            4608 + HALF,
            (
                lambda: store_block(3, head_term(48, 0)),
                lambda: store_block(4, head_term(112, 1)),
                lambda: store_block(0, pair_term(0, 0, 1)),
                lambda: store_block(1, pair_term(0, 2, 3)),
                lambda: store_block(2, pair_term(16, 0, 1)),
                lambda: store_block(5, pair_term(16, 2, 3)),
            ),
        )
        blocks_stored(6)
        for target in range(sections):
            if target != 2:
                out_small_copy(target, 1).wait_send()
        passed(relay_copy, 1)
        passed(back_relay_copy, 2)
        qk_copy().wait_send()
        state_copy().wait_send()
        g_copy().wait_send()

    @pl.when(me == 3)
    def _():
        weights = weights_in(8)
        d_out = moved(gathered_rows(3).astype(bf16), GROUP, 0)
        d_low = d_out.astype(bf16)
        for c in weights:
            c.wait()
        gain_row = gain_ref[0:1, :]
        pass_on(relay_copy, 2)
        state_copy().wait_recv()
        y = state[...].astype(f32)
        inverse = inverse_rms(y)
        normed = y * inverse
        a4 = (normed * gain_row).astype(bf16)
        r4 = []
        du4 = []
        result = y
        grad = jnp.zeros((16, D), f32)
        for b in range(4):
            r, slope = gelu_both(nn(a4, block(b)))
            r4.append(r.astype(bf16))
            result = result + nn(r4[b], block(4 + b))
            du4.append((nt(d_low, block(4 + b)) * slope).astype(bf16))
            grad = grad + nt(du4[b], block(b))
        state_back[...] = (d_out + norm_back(normed, inverse, gain_row, grad)).astype(bf16)
        state_back_copy().start()
        pass_on(back_relay_copy, 1)
        rows_out[0] = result.astype(bf16)
        gain_sum[...] = jnp.zeros_like(gain_sum)
        gain_sum[0:1, :] = jnp.sum(grad * normed, axis=0, keepdims=True)
        fac[...] = jnp.zeros_like(fac)
        fac[0:16, :] = packed([a4, d_low, r4[0], r4[1]])
        fac[16:32, :] = packed([r4[2], r4[3], du4[0], du4[1]])
        fac[32:48, :] = packed([du4[2], du4[3]])
        for target in range(sections):
            if target != 3:
                out_small_copy(target, 0).start()
        own = local_copy(22, rows_out.at[0], o_small.at[0])
        own.start()
        gather_first(48)
        gather_step(48, 1)
        gains_step(0)
        own.wait()
        gather_step(48, 2)
        gains_step(1)
        gather_step(48, 3)
        gains_step(2)
        gather_step(48, 4, last=True)
        gather_cores(48).start()
        gains_step(3, last=True)
        gather_cores(48).wait()
        gather_end(48)

        def member(slot, part):
            return aligned(gathered_tile(48, 16 * (slot // 4), 16, part), 0, slot % 4)

        def stored(n):
            b = n % 4
            sides = ((0, 6 + b), (2 + b, 1))[n // 4]
            return lambda: store_block(
                n, lambda part: (member(sides[0], part), member(sides[1], part))
            )

        lent_sums(
            1, 11264, 11264 + 6 * HALF, 11264 + 3 * HALF, tuple(stored(n) for n in range(8))
        )
        blocks_stored(8)
        for target in range(sections):
            if target != 3:
                out_small_copy(target, 0).wait_send()
        passed(relay_copy, 2)
        passed(back_relay_copy, 1)
        state_back_copy().wait_send()

    gains_out = local_copy(23, gain_sum, o_gain)
    gains_out.start()

    @pl.when(me != 2)
    def _():
        dynamic_small_copy(2).wait_send()
        remote(
            places.out_small[0] + me * 2 + 1, rows_out.at[1], o_small.at[1], 2
        ).wait_recv()

    @pl.when(me != 3)
    def _():
        dynamic_small_copy(3).wait_send()
        remote(places.out_small[0] + me * 2, rows_out.at[0], o_small.at[0], 3).wait_recv()

    @pl.when(me != 0)
    def _():
        def step(p, carry):
            dynamic_enc_copy(p).wait_send()
            remote(
                places.out_enc[0] + me * GROUP + p, rows(H_ROWS, p * LEN, chunk_len), o_enc.at[p], 0
            ).wait_recv()
            return carry

        lax.fori_loop(0, GROUP, step, 0)

    gains_out.wait()


def relay_call(sections, bits, enc_in, lengths, small_in, gain_rows, weights):
    places = Places(sections, bits)
    any_space = pl.BlockSpec(memory_space=pl.ANY)
    return pl.pallas_call(
        functools.partial(relay_kernel, sections, bits, places),
        out_shape=(
            jax.ShapeDtypeStruct(enc_in.shape, bf16),
            jax.ShapeDtypeStruct((2, 16, D), bf16),
            jax.ShapeDtypeStruct((8 * D, D), bf16),
            jax.ShapeDtypeStruct((8, D), f32),
        ),
        in_specs=[
            pl.BlockSpec(memory_space=pltpu.SMEM),
            any_space,
            any_space,
            any_space,
            pl.BlockSpec(memory_space=pltpu.VMEM),
        ],
        out_specs=(any_space,) * 4,
        scratch_shapes=[
            pltpu.VMEM((POOL_ROWS, D), bf16),
            pltpu.VMEM((WIDE_ROWS, 256), bf16),
            pltpu.VMEM((LEN, D), f32),
            pltpu.VMEM((64, LEN), f32),
            pltpu.VMEM((sections, 16, 256), bf16),
            pltpu.VMEM((64, D), bf16),
            pltpu.VMEM((64, D), bf16),
            pltpu.VMEM((64, D), bf16),
            pltpu.VMEM((64, D), bf16),
            pltpu.VMEM((16, D), bf16),
            pltpu.VMEM((16, D), bf16),
            pltpu.VMEM((FAC_ROWS, D), bf16),
            pltpu.VMEM((2, 16, D), bf16),
            pltpu.VMEM((8, D), f32),
            pltpu.VMEM((bits, 8, D), f32),
            pltpu.SemaphoreType.DMA((places.count,)),
            pltpu.SemaphoreType.DMA((places.count,)),
            pltpu.SemaphoreType.DMA((40,)),
            pltpu.SemaphoreType.REGULAR((4,)),
        ],
        compiler_params=pltpu.CompilerParams(
            collective_id=0, has_side_effects=True, vmem_limit_bytes=67_000_000
        ),
    )(lengths, enc_in, small_in, weights, gain_rows)


def local(enc_in, lengths, dec_in, gains, weights, d_out):
    section = lax.axis_index("section")
    sections = lax.axis_size("section")
    width = dec_in.shape[1]
    small = jnp.concatenate([dec_in, d_out], axis=0)
    small = jnp.pad(small, ((0, 16 - 2 * GROUP), (0, 256 - width)))
    gain_rows = jnp.pad(gains[0].astype(f32), ((0, 6), (0, 0)))
    bits = lax.axis_size("dp").bit_length() - 1
    d_enc, rows_out, total, total_gains = relay_call(
        sections, bits, enc_in, lengths, small, gain_rows, weights[0].reshape(8 * D, D)
    )
    used = jnp.where(section == 0, 4, jnp.where(section == 2, 6, 8))
    is_used = lax.broadcasted_iota(jnp.int32, (8, D, D), 0) < used
    total_weights = jnp.where(is_used, total.reshape(8, D, D).astype(f32), 0.0)
    own = lax.dynamic_slice(rows_out, (0, 0, section * width), (2, GROUP, width))
    return (own[0], d_enc, own[1], total_gains[None, :2], total_weights[None])


def solution(mesh):
    in_specs = (
        P("dp", "section", None),
        P("dp"),
        P("dp", "section"),
        P("section", None, None),
        P("section", None, None, None),
        P("dp", "section"),
    )
    out_specs = (
        P("dp", "section"),
        P("dp", "section", None),
        P("dp", "section"),
        P("section", None, None),
        P("section", None, None, None),
    )
    return jax.shard_map(local, mesh=mesh, in_specs=in_specs, out_specs=out_specs, check_vma=False)
```

```python
import functools
import math

import jax
import jax.numpy as jnp
from jax import lax
from jax.experimental import pallas as pl
from jax.experimental.pallas import tpu as pltpu
from jax.sharding import PartitionSpec as P

D = 768
HEADS = 12
HEAD = 64
PAIRS = HEADS // 2
LEN = 512
GROUP = 4
ROWS = GROUP * LEN
epsilon = 1e-06
masked_score = -1e30
gelu_coeff = 0.044715
gelu_scale = math.sqrt(2.0 / math.pi)
log2_e = 1.4426950408889634
bf16 = jnp.bfloat16
f32 = jnp.float32
MESH = pl.DeviceIdType.MESH

W_ROWS = 0
X_ROWS = 3072
Q_ROWS = X_ROWS + ROWS
K_ROWS = Q_ROWS + ROWS
V_ROWS = K_ROWS + ROWS
O_ROWS = V_ROWS + ROWS
IL_ROWS = O_ROWS + ROWS
H_ROWS = IL_ROWS + ROWS
DH_ROWS = H_ROWS + ROWS
POOL_ROWS = DH_ROWS + ROWS
FF_H = 6144
FF_A = FF_H + ROWS
FF_E = FF_A + ROWS
RELAY_F = 6144
GELU_ROWS = 12 * ROWS
WIDE_ROWS = 24 * ROWS

CHUNK = 48
CHUNKS = 5
RELAY = CHUNK * CHUNKS
DIRECT = LEN - RELAY
RELAY_B = RELAY_F + GROUP * RELAY
FAC_ROWS = 176
FAC_AT = 8192
HALF = D // 2
PARTS = 2
JOB = HALF // PARTS
OWN_BLOCKS = {0: (3, 0, 1), 1: (0, 1, 2, 3, 7)}
LENT_BLOCKS = {0: (2,), 1: (4, 5, 6)}


def nn(a, b):
    return jnp.dot(a, b, preferred_element_type=f32)


def nt(a, b):
    return lax.dot_general(a, b, (((1,), (1,)), ((), ())), preferred_element_type=f32)


def tn(a, b):
    return lax.dot_general(a, b, (((0,), (0,)), ((), ())), preferred_element_type=f32)


def iota(shape, axis):
    return lax.broadcasted_iota(jnp.int32, shape, axis)


def inverse_rms(v):
    return lax.rsqrt(jnp.mean(v * v, axis=-1, keepdims=True) + epsilon)


def norm_back(normed, inverse, gain_row, grad):
    scaled = grad * gain_row
    return inverse * (scaled - normed * jnp.mean(scaled * normed, axis=-1, keepdims=True))


def gelu_both(u):
    square = u * u
    tangent = jnp.tanh(gelu_scale * (u + gelu_coeff * square * u))
    half = 0.5 * (1.0 + tangent)
    slope = half + 0.5 * u * (1.0 - tangent * tangent) * (
        gelu_scale + 3.0 * gelu_coeff * gelu_scale * square
    )
    return (u * half, slope)


class Places:
    def __init__(self, sections, bits):
        self.count = 0
        self.enc = [self.take(GROUP) for _ in range(sections)]
        self.small = [self.take(2) for _ in range(sections)]
        self.direct = self.take(GROUP)
        self.relay = [self.take(GROUP * CHUNKS) for _ in range(3)]
        self.back_direct = self.take(GROUP)
        self.back_relay = [self.take(GROUP * CHUNKS) for _ in range(3)]
        self.qk = self.take(1)
        self.mix = self.take(GROUP)
        self.state = self.take(1)
        self.state_back = self.take(1)
        self.g = self.take(1)
        self.x = self.take(1)
        self.out_enc = [self.take(GROUP) for _ in range(sections)]
        self.out_small = [self.take(2) for _ in range(sections)]
        self.halves = self.take(8)
        self.lend = self.take(8 * PARTS)
        self.lent = self.take(8 * PARTS)
        self.whole = self.take(8)
        self.inward = self.take(8 * PARTS)
        self.middle = self.take(8 * PARTS)
        self.outward = self.take(8 * PARTS)
        self.facs = self.take(2 ** bits - 1)
        self.gains = self.take(bits)

    def take(self, amount):
        first = self.count
        self.count += amount
        return first


def relay_kernel(
    sections,
    bits,
    places,
    len_ref,
    enc_ref,
    dec_ref,
    d_out_ref,
    w_ref,
    gain_ref,
    o_enc,
    o_dec,
    o_start,
    o_dw,
    o_gain,
    pool,
    wide,
    acc,
    cp,
    small,
    qk,
    mix,
    gk,
    xs,
    state,
    state_back,
    fac,
    rows_out,
    rows_in,
    small_wide,
    small_ref,
    gain_sum,
    gain_in,
    send_sem,
    recv_sem,
    local_sem,
    ready_sem,
):
    me = lax.axis_index("section")
    group = lax.axis_index("dp")
    chunk_len = LEN // sections

    def remote(number, src, dst, target):
        return pltpu.make_async_remote_copy(
            src_ref=src,
            dst_ref=dst,
            send_sem=send_sem.at[number],
            recv_sem=recv_sem.at[number],
            device_id=(target, group),
            device_id_type=MESH,
        )

    def local_copy(number, src, dst):
        return pltpu.make_async_copy(src, dst, local_sem.at[number])

    def rows(base, start, count):
        return pool.at[pl.ds(pl.multiple_of(base + start, 16), count)]

    def out_rows(start, count):
        return o_dw.at[pl.ds(pl.multiple_of(start, 16), count)]

    bit = [lax.rem(group // 2**k, 2) for k in range(bits)]
    partner = [group + 2**k * (1 - 2 * bit[k]) for k in range(bits)]

    chips = 2 ** (bits - 1)
    chip = group // 2
    on_left = chip < chips // 2
    inward = jnp.where(on_left, group + 2, group - 2)
    outward = jnp.where(on_left, group - 2, group + 2)
    in_middle = (chip == chips // 2 - 1) | (chip == chips // 2)
    at_end = (chip == 0) | (chip == chips - 1)

    def along(number, src, dst, target):
        return pltpu.make_async_remote_copy(
            src_ref=src,
            dst_ref=dst,
            send_sem=send_sem.at[number],
            recv_sem=recv_sem.at[number],
            device_id=(me, target),
            device_id_type=MESH,
        )

    def across(number, src, dst, k):
        return pltpu.make_async_remote_copy(
            src_ref=src,
            dst_ref=dst,
            send_sem=send_sem.at[number],
            recv_sem=recv_sem.at[number],
            device_id=(me, partner[k]),
            device_id_type=MESH,
        )

    barrier = pltpu.get_barrier_semaphore()
    for step in range(1, sections):
        pl.semaphore_signal(
            barrier,
            inc=1,
            device_id=(lax.rem(me + step, sections), group),
            device_id_type=MESH,
        )
    for k in range(bits):
        pl.semaphore_signal(barrier, inc=1, device_id=(me, partner[k]), device_id_type=MESH)
    pl.semaphore_signal(barrier, inc=1, device_id=(me, inward), device_id_type=MESH)

    @pl.when(jnp.logical_not(at_end))
    def _():
        pl.semaphore_signal(barrier, inc=1, device_id=(me, outward), device_id_type=MESH)
        pl.semaphore_wait(barrier, sections + bits + 1)

    @pl.when(at_end)
    def _():
        pl.semaphore_wait(barrier, sections + bits)

    lane = iota((1, 128), 1)
    low_half = lane < HEAD

    def enc_copy(sender, p):
        return remote(
            places.enc[sender] + p,
            enc_ref.at[p],
            rows(X_ROWS, p * LEN + sender * chunk_len, chunk_len),
            0,
        )

    def small_copy(sender, target):
        return remote(places.small[sender] + target - 2, small_ref, small.at[sender], target)

    def direct_copy(p):
        return remote(
            places.direct + p, rows(H_ROWS, p * LEN, DIRECT), rows(FF_H, p * LEN, DIRECT), 1
        )

    def relay_copy(hop, index):
        p = index // CHUNKS
        piece = index % CHUNKS
        whole = p * LEN + DIRECT + piece * CHUNK
        src = rows(H_ROWS, whole, CHUNK) if hop == 0 else rows(RELAY_F, index * CHUNK, CHUNK)
        dst = rows(FF_H, whole, CHUNK) if hop == 2 else rows(RELAY_F, index * CHUNK, CHUNK)
        return remote(places.relay[hop] + index, src, dst, (2, 3, 1)[hop])

    def back_direct_copy(p):
        return remote(
            places.back_direct + p, rows(FF_H, p * LEN, DIRECT), rows(DH_ROWS, p * LEN, DIRECT), 0
        )

    def back_relay_copy(hop, index):
        p = index // CHUNKS
        piece = index % CHUNKS
        whole = p * LEN + DIRECT + piece * CHUNK
        src = rows(FF_H, whole, CHUNK) if hop == 0 else rows(RELAY_B, index * CHUNK, CHUNK)
        dst = rows(DH_ROWS, whole, CHUNK) if hop == 2 else rows(RELAY_B, index * CHUNK, CHUNK)
        return remote(places.back_relay[hop] + index, src, dst, (3, 2, 0)[hop])

    def qk_copy():
        return remote(places.qk, qk, qk, 1)

    def mix_copy(p):
        part = pl.ds(pl.multiple_of(p * 16, 16), 16)
        return remote(places.mix + p, mix.at[part], mix.at[part], 2)

    def state_copy():
        return remote(places.state, state, state, 3)

    def state_back_copy():
        return remote(places.state_back, state_back, state_back, 2)

    def g_copy():
        return remote(places.g, gk, gk, 1)

    def x_copy():
        return remote(places.x, xs, xs, 2)

    def out_enc_copy(target, p):
        return remote(
            places.out_enc[target] + p,
            rows(H_ROWS, p * LEN + target * chunk_len, chunk_len),
            o_enc.at[p],
            target,
        )

    def out_small_copy(target, kind):
        return remote(
            places.out_small[target] + kind, rows_out.at[kind], rows_in.at[kind], target
        )

    def each_passage(body):
        def step(p, carry):
            body(p)
            return carry

        lax.fori_loop(0, GROUP, step, 0)

    def weights_in(blocks):
        copies = [
            local_copy(
                i,
                w_ref.at[pl.ds(i * D, D)],
                pool.at[pl.ds(W_ROWS + i * D, D)],
            )
            for i in range(blocks)
        ]
        for c in copies:
            c.start()
        return copies

    def block(i):
        return pool[W_ROWS + i * D : W_ROWS + (i + 1) * D, :]

    def send_inputs():
        def step(p, carry):
            enc_copy(me, p).start()
            return carry

        lax.fori_loop(0, GROUP, step, 0)

    def dynamic_enc_copy(p):
        number = places.enc[0] + me * GROUP + p
        return remote(
            number, enc_ref.at[p], rows(X_ROWS, p * LEN + me * chunk_len, chunk_len), 0
        )

    def dynamic_small_copy(target):
        number = places.small[0] + me * 2 + target - 2
        return remote(number, small_ref, small.at[me], target)

    width = D // sections
    small_wide[...] = jnp.zeros_like(small_wide)
    small_wide[0:GROUP, 0:width] = dec_ref[...].astype(f32)
    small_wide[GROUP : 2 * GROUP, 0:width] = d_out_ref[...].astype(f32)
    small_ref[...] = small_wide[...].astype(bf16)

    @pl.when(me != 2)
    def _():
        dynamic_small_copy(2).start()

    @pl.when(me != 3)
    def _():
        dynamic_small_copy(3).start()

    @pl.when((me == 1) | (me == 2))
    def _():
        each_passage(lambda p: dynamic_enc_copy(p).start())

    @pl.when(me == 3)
    def _():
        dynamic_enc_copy(0).start()

    def halves_copy(n, landing):
        return across(
            places.halves + n,
            rows(W_ROWS + n * D, (1 - bit[0]) * HALF, HALF),
            rows(landing, n * HALF, HALF),
            0,
        )

    def add_rows(at, landing, count):
        at = pl.ds(pl.multiple_of(at, 16), count)
        landed = pl.ds(pl.multiple_of(landing, 16), count)
        pool[at, :] = (pool[at, :].astype(f32) + pool[landed, :].astype(f32)).astype(bf16)

    def add_halves(n, landing):
        halves_copy(n, landing).wait_recv()
        add_rows(W_ROWS + n * D + bit[0] * HALF, landing + n * HALF, HALF)

    def lend_copy(n, i, index, landing):
        return remote(
            places.lend + PARTS * n + i,
            rows(W_ROWS + n * D + i * JOB, bit[0] * HALF, JOB),
            rows(landing, index * HALF + i * JOB, JOB),
            lax.rem(me + 2, sections),
        )

    def lent_copy(n, i, index, result):
        return remote(
            places.lent + PARTS * n + i,
            rows(result, index * HALF + i * JOB, JOB),
            out_rows(n * D + bit[0] * HALF + i * JOB, JOB),
            lax.rem(me + 2, sections),
        )

    def whole_copy(n):
        half = out_rows(n * D + bit[0] * HALF, HALF)
        return across(places.whole + n, half, half, 0)

    class Job:
        def __init__(self, n, i, at, landing, index, result):
            self.number = PARTS * n + i
            self.place = rows(at, 0, JOB)
            self.at = at
            self.from_out = landing + 2 * index * JOB
            self.from_in = landing + (2 * index + 1) * JOB
            self.result = result(at)

        def to_inward(self):
            return along(
                places.inward + self.number, self.place, rows(self.from_out, 0, JOB), inward
            )

        def to_middle(self):
            return along(
                places.middle + self.number, self.place, rows(self.from_in, 0, JOB), inward
            )

        def total_out(self):
            return along(places.outward + self.number, self.place, self.result, outward)

        def total_on(self):
            return along(places.outward + self.number, self.result, self.result, outward)

        def own(self):
            return local_copy(24 + self.number, self.place, self.result)

        def one(self):
            @pl.when(at_end)
            def _():
                self.to_inward().start()

        def two(self):
            @pl.when(jnp.logical_not(at_end))
            def _():
                self.to_inward().wait_recv()
                add_rows(self.at, self.from_out, JOB)

            if chips > 4:

                @pl.when(jnp.logical_not(at_end) & jnp.logical_not(in_middle))
                def _():
                    self.to_inward().start()

            @pl.when(in_middle)
            def _():
                self.to_middle().start()

        def three(self):
            @pl.when(in_middle)
            def _():
                self.to_middle().wait_recv()
                self.to_middle().wait_send()
                add_rows(self.at, self.from_in, JOB)
                self.own().start()
                self.total_out().start()

        def four(self):
            @pl.when(in_middle)
            def _():
                self.own().wait()

            @pl.when(jnp.logical_not(in_middle))
            def _():
                self.total_on().wait_recv()

            if chips > 4:

                @pl.when(jnp.logical_not(at_end) & jnp.logical_not(in_middle))
                def _():
                    self.total_on().start()

        def end(self):
            @pl.when(jnp.logical_not(in_middle))
            def _():
                self.to_inward().wait_send()

            @pl.when(in_middle)
            def _():
                self.total_out().wait_send()

            if chips > 4:

                @pl.when(jnp.logical_not(at_end) & jnp.logical_not(in_middle))
                def _():
                    self.total_on().wait_send()

    def own_jobs(blocks, landing):
        return [
            Job(
                n,
                i,
                W_ROWS + n * D + bit[0] * HALF + i * JOB,
                landing,
                PARTS * index + i,
                lambda at: out_rows(at - W_ROWS, JOB),
            )
            for index, n in enumerate(blocks)
            for i in range(PARTS)
        ]

    def lent_jobs(blocks, arrived, landing, result):
        return [
            Job(
                n,
                i,
                arrived + index * HALF + i * JOB,
                landing,
                PARTS * index + i,
                lambda at: rows(at - arrived + result, 0, JOB),
            )
            for index, n in enumerate(blocks)
            for i in range(PARTS)
        ]

    def finish_jobs(jobs, done, steps=()):
        count = len(jobs)
        steps = list(steps) + [1] * (count - len(steps))
        for t in range(count + 3):
            if t < count and steps[t] < 2:
                jobs[t].two()
            if 0 <= t - 1 < count and steps[t - 1] < 3:
                jobs[t - 1].three()
            if 0 <= t - 3 < count:
                jobs[t - 3].four()
                if (t - 3) % PARTS == PARTS - 1:
                    done((t - 3) // PARTS)

    def lent_sums(blocks, arrived, landing, result, between):
        jobs = lent_jobs(blocks, arrived, landing, result)
        count = len(jobs)
        pieces = list(between)
        for t in range(count + 3):
            if t < count:
                lend_copy(blocks[t // PARTS], t % PARTS, t // PARTS, arrived).wait_recv()
                jobs[t].one()
                jobs[t].two()
            if 0 <= t - 1 < count:
                jobs[t - 1].three()
            if 0 <= t - 3 < count:
                jobs[t - 3].four()
                index, i = ((t - 3) // PARTS, (t - 3) % PARTS)
                lent_copy(blocks[index], i, index, result).start()
            if pieces:
                pieces.pop(0)()
        for piece in pieces:
            piece()
        for job in jobs:
            job.end()
        for index, n in enumerate(blocks):
            for i in range(PARTS):
                lent_copy(n, i, index, result).wait_send()

    def gain_copy(k):
        return across(places.gains + k, gain_sum, gain_in.at[k], k)

    def gains_step(k, last=False):
        for step in range(k, bits + 1 if last else k + 1):
            if 0 < step <= bits:
                gain_copy(step - 1).wait()
                gain_sum[...] += gain_in[step - 1]
            if step < bits:
                gain_copy(step).start()

    def slot(width, core, place):
        return rows(FAC_AT, (core * chips + place) * width, width)

    def to_right(width, h):
        number = places.facs + 2 * (h - 1)
        place = slot(width, bit[0], chip - (h - 1))
        return along(number, place, place, group + 2)

    def to_left(width, h):
        number = places.facs + 2 * (h - 1) + 1
        place = slot(width, bit[0], chip + (h - 1))
        return along(number, place, place, group - 2)

    def from_left(width, h):
        number = places.facs + 2 * (h - 1)
        place = slot(width, bit[0], chip - h)
        return along(number, place, place, group - 2)

    def from_right(width, h):
        number = places.facs + 2 * (h - 1) + 1
        place = slot(width, bit[0], chip + h)
        return along(number, place, place, group + 2)

    def gather_first(width):
        own = local_copy(21, fac.at[pl.ds(0, width)], slot(width, bit[0], chip))
        own.start()
        own.wait()

    def gather_send(width, h, act):
        @pl.when((chip >= h - 1) & (chip < chips - 1))
        def _():
            act(to_right(width, h))

        @pl.when((chip + h - 1 <= chips - 1) & (chip > 0))
        def _():
            act(to_left(width, h))

    def gather_take(width, h):
        @pl.when(chip >= h)
        def _():
            from_left(width, h).wait_recv()

        @pl.when(chip + h <= chips - 1)
        def _():
            from_right(width, h).wait_recv()

    def gather_step(width, h, last=False):
        for step in range(h, chips + 1 if last else h + 1):
            if step > 1:
                gather_take(width, step - 1)
            if step < chips:
                gather_send(width, step, lambda copy: copy.start())

    def gather_cores(width):
        half = rows(FAC_AT, bit[0] * chips * width, chips * width)
        return across(places.facs + 2 * (chips - 1), half, half, 0)

    def gather_end(width):
        for h in range(1, chips):
            gather_send(width, h, lambda copy: copy.wait_send())

    batch = min(2**bits, 8)

    def gathered_tile(width, first, count, part):
        return jnp.concatenate(
            [
                pool[
                    pl.ds(
                        pl.multiple_of(FAC_AT + (part * batch + i) * width + first, 16), count
                    ),
                    :,
                ]
                for i in range(batch)
            ],
            axis=0,
        )

    def store_block(n, sides):
        for c in range(3):
            columns = slice(256 * c, 256 * (c + 1))

            def term(part):
                left, right = sides(part)
                return tn(left, right[:, columns])

            if 2**bits == batch:
                total = term(0)
            else:
                total = lax.fori_loop(
                    0,
                    2**bits // batch,
                    lambda i, total: total + term(i),
                    jnp.zeros((D, 256), f32),
                )
            pool[W_ROWS + n * D : W_ROWS + (n + 1) * D, columns] = total.astype(bf16)
        local_copy(n, rows(W_ROWS + n * D, 0, D), out_rows(n * D, D)).start()

    def aligned(tile, i, j):
        count = tile.shape[0]
        row, column = iota((count, count), 0), iota((count, count), 1)
        member = row & 15
        pick = (column - row == GROUP * (j - i)) & (member >= GROUP * i) & (member < GROUP * (i + 1))
        return nn(jnp.where(pick, 1.0, 0.0).astype(bf16), tile).astype(bf16)

    def blocks_stored(count):
        for n in range(count):
            local_copy(n, rows(W_ROWS + n * D, 0, D), out_rows(n * D, D)).wait()

    @pl.when(me == 0)
    def _():
        own = [
            local_copy(8 + p, enc_ref.at[p], pool.at[pl.ds(X_ROWS + p * LEN, chunk_len)])
            for p in range(GROUP)
        ]
        for c in own:
            c.start()
        weights = weights_in(4)
        for c in weights:
            c.wait()
        for c in own:
            c.wait()
        gain_row = gain_ref[0:1, :].astype(f32)
        key_row = iota((LEN, 1), 0)

        def pair_columns(hp):
            return pl.ds(pl.multiple_of(hp * 128, 128), 128)

        def forward(p):
            for sender in range(1, sections):
                enc_copy(sender, p).wait_recv()

            @pl.when(p < GROUP - 1)
            def _():
                pl.semaphore_signal(
                    ready_sem.at[4], inc=1, device_id=(3, group), device_id_type=MESH
                )

            start = pl.multiple_of(p * LEN, LEN)
            x = pool[pl.ds(X_ROWS + start, LEN), :].astype(f32)
            a0 = (x * inverse_rms(x) * gain_row).astype(bf16)
            pool[pl.ds(Q_ROWS + start, LEN), :] = (nn(a0, block(0)) * log2_e).astype(bf16)
            pool[pl.ds(K_ROWS + start, LEN), :] = nn(a0, block(1)).astype(bf16)
            pool[pl.ds(V_ROWS + start, LEN), :] = nn(a0, block(2)).astype(bf16)
            bias = jnp.where(key_row < len_ref[p], 0.0, masked_score).astype(bf16)

            def pair(hp, carry):
                c = pair_columns(hp)
                q2 = pool[pl.ds(Q_ROWS + start, LEN), c]
                k2 = pool[pl.ds(K_ROWS + start, LEN), c]
                v2 = pool[pl.ds(V_ROWS + start, LEN), c]
                one = jnp.ones_like(q2)
                zero = jnp.zeros_like(q2)
                queries = [
                    jnp.where(low_half, q2, jnp.where(lane == HEAD, one, zero)),
                    jnp.where(low_half, jnp.where(lane == 0, one, zero), q2),
                ]
                keys = [
                    jnp.where(low_half, k2, jnp.where(lane == HEAD, bias, zero)),
                    jnp.where(low_half, jnp.where(lane == 0, bias, zero), k2),
                ]
                values = [jnp.where(low_half, v2, one), jnp.where(low_half, one, v2)]
                scores = [nt(queries[half], keys[half]) for half in range(2)]
                probs = [
                    jnp.exp2(s - jnp.max(s, axis=-1, keepdims=True)).astype(bf16) for s in scores
                ]
                for half, e in enumerate(probs):
                    at = pl.multiple_of((p * HEADS + hp * 2 + half) * 2 * LEN, 2 * LEN)
                    wide[pl.ds(at, LEN), :] = e[:, :256]
                    wide[pl.ds(at + LEN, LEN), :] = e[:, 256:]
                mixes = [nn(e, value) for e, value in zip(probs, values)]
                total = pltpu.roll(jnp.where(low_half, mixes[1], mixes[0]), HEAD, 1)
                inverse = 1.0 / total
                pool[pl.ds(O_ROWS + start, LEN), c] = (
                    jnp.where(low_half, mixes[0], mixes[1]) * inverse
                ).astype(bf16)
                pool[pl.ds(IL_ROWS + start, LEN), c] = inverse.astype(bf16)
                return carry

            lax.fori_loop(0, PAIRS, pair, 0)
            h = x + nn(pool[pl.ds(O_ROWS + start, LEN), :], block(3))
            pool[pl.ds(H_ROWS + start, LEN), :] = h.astype(bf16)
            direct_copy(p).start()
            for piece in range(CHUNKS):
                relay_copy(0, p * CHUNKS + piece).start()

        each_passage(forward)

        def sent(p):
            direct_copy(p).wait_send()
            for piece in range(CHUNKS):
                relay_copy(0, p * CHUNKS + piece).wait_send()

        each_passage(sent)
        gain_sum[...] = jnp.zeros_like(gain_sum)

        def backward(p):
            start = pl.multiple_of(p * LEN, LEN)
            back_direct_copy(p).wait_recv()
            for piece in range(CHUNKS):
                back_relay_copy(2, p * CHUNKS + piece).wait_recv()
            dh = pool[pl.ds(DH_ROWS + start, LEN), :]
            pool[pl.ds(H_ROWS + start, LEN), :] = nt(dh, block(3)).astype(bf16)

            def pair(hp, carry):
                c = pair_columns(hp)
                q2 = pool[pl.ds(Q_ROWS + start, LEN), c]
                k2 = pool[pl.ds(K_ROWS + start, LEN), c]
                v2 = pool[pl.ds(V_ROWS + start, LEN), c]
                da = pool[pl.ds(H_ROWS + start, LEN), c].astype(f32)
                mixed = pool[pl.ds(O_ROWS + start, LEN), c].astype(f32)
                da = da * pool[pl.ds(IL_ROWS + start, LEN), c].astype(f32)
                product = da * mixed
                da = da.astype(bf16)
                one = jnp.ones_like(q2)
                zero = jnp.zeros_like(q2)
                dq = []
                dk = []
                dv = []
                for half in range(2):
                    mine = low_half if half == 0 else lane >= HEAD
                    spare = HEAD if half == 0 else 0
                    centre = -jnp.sum(jnp.where(mine, product, 0.0), axis=-1, keepdims=True)
                    centre_high = centre.astype(bf16)
                    centre_low = (centre - centre_high.astype(f32)).astype(bf16)
                    da_own = jnp.where(mine, da, zero)
                    da_ext = jnp.where(
                        lane == spare,
                        centre_high,
                        jnp.where(lane == spare + 1, centre_low, da_own),
                    )
                    at = pl.multiple_of((p * HEADS + hp * 2 + half) * 2 * LEN, 2 * LEN)
                    e = jnp.concatenate(
                        [wide[pl.ds(at, LEN), :], wide[pl.ds(at + LEN, LEN), :]], axis=1
                    )
                    ds = e * nt(da_ext, jnp.where(mine, v2, one)).astype(bf16)
                    dq.append(nn(ds, k2))
                    dk.append(nn(jnp.where(mine, q2, zero).T, ds))
                    dv.append(nn(da_own.T, e))
                pool[pl.ds(Q_ROWS + start, LEN), c] = jnp.where(low_half, dq[0], dq[1]).astype(bf16)
                pool[pl.ds(K_ROWS + start, LEN), c] = (
                    (dk[0] + dk[1]).T * (1.0 / log2_e)
                ).astype(bf16)
                pool[pl.ds(V_ROWS + start, LEN), c] = (dv[0] + dv[1]).T.astype(bf16)
                return carry

            lax.fori_loop(0, PAIRS, pair, 0)
            grad = (
                nt(pool[pl.ds(Q_ROWS + start, LEN), :], block(0))
                + nt(pool[pl.ds(K_ROWS + start, LEN), :], block(1))
                + nt(pool[pl.ds(V_ROWS + start, LEN), :], block(2))
            )
            x = pool[pl.ds(X_ROWS + start, LEN), :].astype(f32)
            inverse = inverse_rms(x)
            normed = x * inverse
            d_in = dh.astype(f32) + norm_back(normed, inverse, gain_row, grad)
            pool[pl.ds(H_ROWS + start, LEN), :] = d_in.astype(bf16)
            gain_sum[0:1, :] += jnp.sum(grad * normed, axis=0, keepdims=True)
            pool[pl.ds(X_ROWS + start, LEN), :] = (normed * gain_row).astype(bf16)
            for target in range(1, sections - 1):
                out_enc_copy(target, p).start()
            local_copy(8 + p, rows(H_ROWS, start, chunk_len), o_enc.at[p]).start()

        each_passage(backward)
        each_passage(lambda p: out_enc_copy(sections - 1, p).start())
        sides = (
            (X_ROWS, Q_ROWS),
            (X_ROWS, K_ROWS),
            (X_ROWS, V_ROWS),
            (O_ROWS, DH_ROWS),
        )
        own = OWN_BLOCKS[0]
        lent = LENT_BLOCKS[0][0]
        jobs = own_jobs(OWN_BLOCKS[0], O_ROWS)

        def compute(n):
            left, right = sides[n]

            def columns(k, carry):
                c = pl.ds(pl.multiple_of(k * 256, 256), 256)
                pool[pl.ds(W_ROWS + n * D, D), c] = tn(
                    pool[left : left + ROWS, :], pool[right : right + ROWS, c]
                ).astype(bf16)
                return carry

            lax.fori_loop(0, 3, columns, 0)

        def begin(index):
            add_halves(own[index], DH_ROWS)
            for job in jobs[PARTS * index : PARTS * (index + 1)]:
                job.one()

        gains_step(0)
        compute(own[0])
        gains_step(1)
        pl.semaphore_signal(
            ready_sem.at[0], inc=1, device_id=(me, partner[0]), device_id_type=MESH
        )

        @pl.when(in_middle)
        def _():
            pl.semaphore_signal(
                ready_sem.at[3], inc=1, device_id=(me, inward), device_id_type=MESH
            )

        @pl.when(jnp.logical_not(in_middle))
        def _():
            pl.semaphore_signal(
                ready_sem.at[1], inc=1, device_id=(me, inward), device_id_type=MESH
            )

        @pl.when(jnp.logical_not(at_end))
        def _():
            pl.semaphore_signal(
                ready_sem.at[2], inc=1, device_id=(me, outward), device_id_type=MESH
            )

        pl.semaphore_wait(ready_sem.at[0], 1)
        halves_copy(own[0], DH_ROWS).start()

        @pl.when(in_middle)
        def _():
            pl.semaphore_wait(ready_sem.at[3], 1)

        @pl.when(jnp.logical_not(in_middle))
        def _():
            pl.semaphore_wait(ready_sem.at[2], 1)

        @pl.when(jnp.logical_not(at_end))
        def _():
            pl.semaphore_wait(ready_sem.at[1], 1)

        begin(0)
        compute(lent)
        gains_step(2)
        halves_copy(lent, DH_ROWS).start()
        compute(own[1])
        gains_step(3, last=True)
        halves_copy(own[1], DH_ROWS).start()
        add_halves(lent, DH_ROWS)
        for i in range(PARTS):
            lend_copy(lent, i, 0, 4608).start()
        for job in jobs[: PARTS // 2]:
            job.two()
        compute(own[2])
        halves_copy(own[2], DH_ROWS).start()
        begin(1)
        for job in jobs[PARTS // 2 : PARTS]:
            job.two()
        for job in jobs[: PARTS // 2]:
            job.three()
        begin(2)
        finish_jobs(
            jobs,
            lambda index: whole_copy(own[index]).start(),
            (3,) * (PARTS // 2) + (2,) * (PARTS // 2),
        )
        for i in range(PARTS):
            lent_copy(lent, i, 0, 4608).wait_recv()
        whole_copy(lent).start()

        def finish(p):
            for target in range(1, sections):
                out_enc_copy(target, p).wait_send()
            local_copy(8 + p, rows(H_ROWS, p * LEN, chunk_len), o_enc.at[p]).wait()

        each_passage(finish)
        for n in own + (lent,):
            whole_copy(n).wait()
            halves_copy(n, DH_ROWS).wait_send()
        for i in range(PARTS):
            lend_copy(lent, i, 0, 4608).wait_send()
        for job in jobs:
            job.end()

    @pl.when(me == 1)
    def _():
        for c in weights_in(8):
            c.wait()
        gain_row = gain_ref[0:1, :].astype(f32)
        key_place = iota((1, LEN), 1)
        qk_copy().wait_recv()

        def tiles(b, p, base):
            return [
                pl.ds(pl.multiple_of(base + (3 * b + i) * ROWS + p * LEN, LEN), LEN)
                for i in range(3)
            ]

        def forward(p):
            start = pl.multiple_of(p * LEN, LEN)
            direct_copy(p).wait_recv()
            for piece in range(CHUNKS):
                relay_copy(2, p * CHUNKS + piece).wait_recv()
            h = pool[pl.ds(FF_H + start, LEN), :].astype(f32)
            a1 = (h * inverse_rms(h) * gain_row).astype(bf16)
            pool[pl.ds(FF_A + start, LEN), :] = a1
            acc[...] = h
            for b in range(4):
                r, slope = gelu_both(nn(a1, block(b)))
                r = r.astype(bf16)
                slope = slope.astype(bf16)
                for i, (at_r, at_s) in enumerate(zip(tiles(b, p, 0), tiles(b, p, GELU_ROWS))):
                    wide[at_r, :] = r[:, 256 * i : 256 * (i + 1)]
                    wide[at_s, :] = slope[:, 256 * i : 256 * (i + 1)]
                acc[...] += nn(r, block(4 + b))
            e = acc[...].astype(bf16)
            pool[pl.ds(FF_E + start, LEN), :] = e
            part = pl.ds(pl.multiple_of(p * 16, 16), 16)
            score = jnp.where(key_place < len_ref[p], nt(qk[part, :], e), masked_score)
            score = jnp.exp(score - jnp.max(score, axis=-1, keepdims=True))
            probs = score / jnp.sum(score, axis=-1, keepdims=True)
            cp[part, :] = probs
            mix[part, :] = nn(probs.astype(bf16), e).astype(bf16)
            mix_copy(p).start()

        each_passage(forward)
        each_passage(lambda p: mix_copy(p).wait_send())
        gain_sum[...] = jnp.zeros_like(gain_sum)
        g_copy().wait_recv()

        def backward(p):
            start = pl.multiple_of(p * LEN, LEN)
            part = pl.ds(pl.multiple_of(p * 16, 16), 16)
            e = pool[pl.ds(FF_E + start, LEN), :]
            probs = cp[part, :]
            d_probs = nt(gk[part, :], e)
            d_score = probs * (d_probs - jnp.sum(probs * d_probs, axis=-1, keepdims=True))
            d_score = d_score.astype(bf16)
            xs[part, :] = nn(d_score, e).astype(bf16)
            de = tn(d_score, qk[part, :]) + tn(probs.astype(bf16), gk[part, :])
            de = de.astype(bf16)
            pool[pl.ds(FF_E + start, LEN), :] = de
            for b in range(4):
                at = tiles(b, p, GELU_ROWS)
                slope = jnp.concatenate([wide[t, :] for t in at], axis=1)
                du = (nt(de, block(4 + b)) * slope.astype(f32)).astype(bf16)
                for i, t in enumerate(at):
                    wide[t, :] = du[:, 256 * i : 256 * (i + 1)]
                grad = nt(du, block(b))
                if b == 0:
                    acc[...] = grad
                else:
                    acc[...] += grad
            grad = acc[...]
            h = pool[pl.ds(FF_H + start, LEN), :].astype(f32)
            inverse = inverse_rms(h)
            normed = h * inverse
            dh = de.astype(f32) + norm_back(normed, inverse, gain_row, grad)
            gain_sum[0:1, :] += jnp.sum(grad * normed, axis=0, keepdims=True)
            pool[pl.ds(FF_H + start, LEN), :] = dh.astype(bf16)
            back_direct_copy(p).start()
            for piece in range(CHUNKS):
                back_relay_copy(0, p * CHUNKS + piece).start()

        each_passage(backward)
        x_copy().start()
        halves_at = FF_E + ROWS
        landing = halves_at + 8 * HALF

        def compute(n):
            b = n % 4
            for i in range(3):
                t = 3 * b + i
                if n < 4:
                    du = wide[GELU_ROWS + t * ROWS : GELU_ROWS + (t + 1) * ROWS, :]
                    pool[W_ROWS + n * D : W_ROWS + (n + 1) * D, 256 * i : 256 * (i + 1)] = tn(
                        pool[FF_A : FF_A + ROWS, :], du
                    ).astype(bf16)
                else:
                    first = W_ROWS + n * D + 256 * i
                    pool[first : first + 256, :] = tn(
                        wide[t * ROWS : (t + 1) * ROWS, :], pool[FF_E : FF_E + ROWS, :]
                    ).astype(bf16)
            halves_copy(n, halves_at).start()

        own = OWN_BLOCKS[1]
        lent = LENT_BLOCKS[1]
        jobs = own_jobs(own, landing)

        def begin(index):
            add_halves(own[index], halves_at)
            for job in jobs[PARTS * index : PARTS * (index + 1)]:
                job.one()

        half_parts = PARTS // 2

        def half_block(index):
            return jobs[half_parts * index : half_parts * (index + 1)]

        def lend(index):
            add_halves(lent[index], halves_at)
            for i in range(PARTS):
                lend_copy(lent[index], i, index, 11264).start()

        gains_step(0)
        compute(own[0])
        gains_step(1)
        compute(lent[0])
        begin(0)
        gains_step(2)
        compute(own[1])
        lend(0)
        gains_step(3, last=True)
        compute(lent[1])
        begin(1)
        compute(own[2])
        lend(1)
        for job in half_block(0):
            job.two()
        compute(lent[2])
        begin(2)
        for job in half_block(1):
            job.two()
        compute(own[3])
        lend(2)
        for job in half_block(0):
            job.three()
        compute(own[4])
        begin(3)
        for job in half_block(1):
            job.three()
        for job in half_block(2):
            job.two()
        begin(4)
        for job in half_block(3):
            job.two()
        finish_jobs(
            jobs,
            lambda index: whole_copy(own[index]).start(),
            (3,) * (2 * half_parts) + (2,) * (2 * half_parts),
        )
        for index, n in enumerate(lent):
            for i in range(PARTS):
                lent_copy(n, i, index, 11264).wait_recv()
            whole_copy(n).start()
        for n in range(8):
            whole_copy(n).wait()
            halves_copy(n, halves_at).wait_send()
        for index, n in enumerate(lent):
            for i in range(PARTS):
                lend_copy(n, i, index, 11264).wait_send()
        for job in jobs:
            job.end()
        x_copy().wait_send()

        def sent(p):
            back_direct_copy(p).wait_send()
            for piece in range(CHUNKS):
                back_relay_copy(0, p * CHUNKS + piece).wait_send()

        each_passage(sent)

    def gathered_rows(own):
        copy = local_copy(20, small_ref, small.at[own])
        copy.start()
        for sender in range(sections):
            if sender != own:
                small_copy(sender, own).wait_recv()
        copy.wait()
        total = jnp.zeros((16, D), f32)
        for sender in range(sections):
            row, column = iota((256, D), 0), iota((256, D), 1)
            pick = jnp.where((column == row + width * sender) & (row < width), 1.0, 0.0)
            total = total + nn(small[sender], pick.astype(bf16))
        return total

    def moved(values, first, to):
        row, column = iota((16, 16), 0), iota((16, 16), 1)
        pick = (column - first == row - to) & (row >= to) & (row < to + GROUP)
        return nn(jnp.where(pick, 1.0, 0.0).astype(bf16), values)

    def packed(values):
        total = moved(values[0], 0, 0)
        for i, value in enumerate(values[1:]):
            total = total + moved(value, 0, GROUP * (i + 1))
        return total.astype(bf16)

    head_mask = (iota((64, D), 1) >> 6) == (iota((64, D), 0) & 15)

    def spread_heads(values):
        pick = jnp.where((iota((64, 16), 0) >> 4) == iota((64, 16), 1), 1.0, 0.0)
        return jnp.where(head_mask, nn(pick.astype(bf16), values), 0.0).astype(bf16)

    def join_heads(values):
        pick = jnp.where(iota((16, 64), 0) == (iota((16, 64), 1) >> 4), 1.0, 0.0)
        return nn(pick.astype(bf16), jnp.where(head_mask, values, 0.0).astype(bf16)).astype(bf16)

    def pass_on(copies, number, first=0, last=GROUP * CHUNKS):
        def step(index, carry):
            copies(number - 1, index).wait_recv()
            copies(number, index).start()
            return carry

        lax.fori_loop(first, last, step, 0)

    def passed(copies, number):
        def step(index, carry):
            copies(number, index).wait_send()
            return carry

        lax.fori_loop(0, GROUP * CHUNKS, step, 0)

    @pl.when(me == 2)
    def _():
        weights = weights_in(6)
        x = moved(gathered_rows(2).astype(bf16), 0, 0)
        for c in weights:
            c.wait()
        gain_self = gain_ref[0:1, :].astype(f32)
        gain_cross = gain_ref[1:2, :].astype(f32)
        inverse_self = inverse_rms(x)
        normed_self = x * inverse_self
        a2 = (normed_self * gain_self).astype(bf16)
        sv = nn(a2, block(0)).astype(bf16)
        middle = x + nn(sv, block(1))
        inverse_cross = inverse_rms(middle)
        normed_cross = middle * inverse_cross
        a3 = (normed_cross * gain_cross).astype(bf16)
        cq = nn(a3, block(2)).astype(bf16)
        qk[...] = nt(spread_heads(cq), block(3)).astype(bf16)
        qk_copy().start()
        pass_on(relay_copy, 1)
        for p in range(GROUP):
            mix_copy(p).wait_recv()
        co = join_heads(nn(mix[...], block(4)))
        state[...] = (middle + nn(co, block(5))).astype(bf16)
        state_copy().start()
        state_back_copy().wait_recv()
        dy = state_back[...]
        dco = nt(dy, block(5)).astype(bf16)
        gk[...] = nt(spread_heads(dco), block(4)).astype(bf16)
        g_copy().start()
        pass_on(back_relay_copy, 2)
        x_copy().wait_recv()
        dcq = join_heads(nn(xs[...], block(3)))
        grad_cross = nt(dcq, block(2))
        dm = dy.astype(f32) + norm_back(normed_cross, inverse_cross, gain_cross, grad_cross)
        dm_low = dm.astype(bf16)
        dsv = nt(dm_low, block(1)).astype(bf16)
        grad_self = nt(dsv, block(0))
        d_in = dm + norm_back(normed_self, inverse_self, gain_self, grad_self)
        rows_out[1] = d_in.astype(bf16)
        gain_sum[...] = jnp.zeros_like(gain_sum)
        gain_sum[0:1, :] = jnp.sum(grad_self * normed_self, axis=0, keepdims=True)
        gain_sum[1:2, :] = jnp.sum(grad_cross * normed_cross, axis=0, keepdims=True)
        fac[0:16, :] = packed([a2, dsv, sv, dm_low])
        fac[16:32, :] = packed([a3, dcq, co, dy])
        fac[32:48, :] = packed([cq, dco])
        fac[48:112, :] = xs[...]
        fac[112:176, :] = mix[...]
        for target in range(sections):
            if target != 2:
                out_small_copy(target, 1).start()
        rows_in[1] = rows_out[1]
        gather_first(FAC_ROWS)
        gather_step(FAC_ROWS, 1)
        gains_step(0)
        gains_step(1)
        gather_step(FAC_ROWS, 2)
        gains_step(2)
        gather_step(FAC_ROWS, 3)
        gains_step(3, last=True)
        gather_step(FAC_ROWS, 4, last=True)
        gather_cores(FAC_ROWS).start()
        gather_cores(FAC_ROWS).wait()
        gather_end(FAC_ROWS)
        def pair_term(first, left, right):
            def term(part):
                tile = gathered_tile(FAC_ROWS, first, 16, part)
                return (tile, aligned(tile, left, right))

            return term

        def head_term(first, member):
            def term(part):
                tall, short = (64 * batch, 16 * batch)
                row, column = iota((tall, short), 0), iota((tall, short), 1)
                heads = (iota((tall, D), 1) >> 6) == (iota((tall, D), 0) & 15)
                pick = column == (row >> 6) * 16 + GROUP * member + ((row >> 4) & 3)
                short_rows = nn(
                    jnp.where(pick, 1.0, 0.0).astype(bf16), gathered_tile(FAC_ROWS, 32, 16, part)
                )
                short_rows = jnp.where(heads, short_rows, 0.0).astype(bf16)
                return (gathered_tile(FAC_ROWS, first, 64, part), short_rows)

            return term

        store_block(3, head_term(48, 0))
        store_block(4, head_term(112, 1))
        store_block(0, pair_term(0, 0, 1))
        store_block(1, pair_term(0, 2, 3))
        store_block(2, pair_term(16, 0, 1))
        store_block(5, pair_term(16, 2, 3))
        lent_sums(LENT_BLOCKS[0], 4608, 4608 + 2 * HALF, 4608 + HALF, ())
        blocks_stored(6)
        for target in range(sections):
            if target != 2:
                out_small_copy(target, 1).wait_send()
        passed(relay_copy, 1)
        passed(back_relay_copy, 2)
        qk_copy().wait_send()
        state_copy().wait_send()
        g_copy().wait_send()

    @pl.when(me == 3)
    def _():
        weights = weights_in(8)
        d_out = moved(gathered_rows(3).astype(bf16), GROUP, 0)
        d_low = d_out.astype(bf16)
        for c in weights:
            c.wait()
        gain_row = gain_ref[0:1, :].astype(f32)

        def next_passage(p):
            pl.semaphore_wait(ready_sem.at[4], 1)
            dynamic_enc_copy(p).start()

        next_passage(1)
        next_passage(2)
        pass_on(relay_copy, 2, 0, CHUNKS)
        next_passage(3)
        pass_on(relay_copy, 2, CHUNKS)
        state_copy().wait_recv()
        y = state[...].astype(f32)
        inverse = inverse_rms(y)
        normed = y * inverse
        a4 = (normed * gain_row).astype(bf16)
        r4 = []
        du4 = []
        result = y
        grad = jnp.zeros((16, D), f32)
        for b in range(4):
            r, slope = gelu_both(nn(a4, block(b)))
            r4.append(r.astype(bf16))
            result = result + nn(r4[b], block(4 + b))
            du4.append((nt(d_low, block(4 + b)) * slope).astype(bf16))
            grad = grad + nt(du4[b], block(b))
        state_back[...] = (d_out + norm_back(normed, inverse, gain_row, grad)).astype(bf16)
        state_back_copy().start()
        pass_on(back_relay_copy, 1)
        rows_out[0] = result.astype(bf16)
        gain_sum[...] = jnp.zeros_like(gain_sum)
        gain_sum[0:1, :] = jnp.sum(grad * normed, axis=0, keepdims=True)
        fac[...] = jnp.zeros_like(fac)
        fac[0:16, :] = packed([a4, d_low, r4[0], r4[1]])
        fac[16:32, :] = packed([r4[2], r4[3], du4[0], du4[1]])
        fac[32:48, :] = packed([du4[2], du4[3]])
        for target in range(sections):
            if target != 3:
                out_small_copy(target, 0).start()
        rows_in[0] = rows_out[0]
        gather_first(48)
        gather_step(48, 1)
        gains_step(0)
        gather_step(48, 2)
        gains_step(1)
        gather_step(48, 3)
        gains_step(2)
        gather_step(48, 4, last=True)
        gather_cores(48).start()
        gains_step(3, last=True)
        gather_cores(48).wait()
        gather_end(48)

        def member(slot, part):
            return aligned(gathered_tile(48, 16 * (slot // 4), 16, part), 0, slot % 4)

        def stored(n):
            b = n % 4
            sides = ((0, 6 + b), (2 + b, 1))[n // 4]
            return lambda: store_block(
                n, lambda part: (member(sides[0], part), member(sides[1], part))
            )

        count = len(LENT_BLOCKS[1])
        lent_sums(
            LENT_BLOCKS[1],
            11264,
            11264 + 2 * count * HALF,
            11264 + count * HALF,
            tuple(stored(n) for n in range(8)),
        )
        blocks_stored(8)
        for target in range(sections):
            if target != 3:
                out_small_copy(target, 0).wait_send()
        passed(relay_copy, 2)
        passed(back_relay_copy, 1)
        state_back_copy().wait_send()

    o_gain[...] = gain_sum[0:2, :]

    @pl.when(me != 2)
    def _():
        dynamic_small_copy(2).wait_send()
        remote(
            places.out_small[0] + me * 2 + 1, rows_out.at[1], rows_in.at[1], 2
        ).wait_recv()

    @pl.when(me != 3)
    def _():
        dynamic_small_copy(3).wait_send()
        remote(places.out_small[0] + me * 2, rows_out.at[0], rows_in.at[0], 3).wait_recv()

    @pl.when(me != 0)
    def _():
        def step(p, carry):
            dynamic_enc_copy(p).wait_send()
            remote(
                places.out_enc[0] + me * GROUP + p, rows(H_ROWS, p * LEN, chunk_len), o_enc.at[p], 0
            ).wait_recv()
            return carry

        lax.fori_loop(0, GROUP, step, 0)

    row, column = iota((D, width), 0), iota((D, width), 1)
    pick = jnp.where(row == column + me * width, 1.0, 0.0).astype(bf16)
    o_dec[...] = nn(rows_in[0], pick)[0:GROUP, :].astype(bf16)
    o_start[...] = nn(rows_in[1], pick)[0:GROUP, :].astype(bf16)


def relay_call(sections, bits, enc_in, lengths, dec_in, d_out, gains, weights):
    places = Places(sections, bits)
    any_space = pl.BlockSpec(memory_space=pl.ANY)
    vmem = pl.BlockSpec(memory_space=pltpu.VMEM)
    return pl.pallas_call(
        functools.partial(relay_kernel, sections, bits, places),
        out_shape=(
            jax.ShapeDtypeStruct(enc_in.shape, bf16),
            jax.ShapeDtypeStruct(dec_in.shape, bf16),
            jax.ShapeDtypeStruct(dec_in.shape, bf16),
            jax.ShapeDtypeStruct((8 * D, D), bf16),
            jax.ShapeDtypeStruct((2, D), f32),
        ),
        in_specs=[
            pl.BlockSpec(memory_space=pltpu.SMEM),
            any_space,
            vmem,
            vmem,
            any_space,
            vmem,
        ],
        out_specs=(any_space, vmem, vmem, any_space, vmem),
        scratch_shapes=[
            pltpu.VMEM((POOL_ROWS, D), bf16),
            pltpu.VMEM((WIDE_ROWS, 256), bf16),
            pltpu.VMEM((LEN, D), f32),
            pltpu.VMEM((64, LEN), f32),
            pltpu.VMEM((sections, 16, 256), bf16),
            pltpu.VMEM((64, D), bf16),
            pltpu.VMEM((64, D), bf16),
            pltpu.VMEM((64, D), bf16),
            pltpu.VMEM((64, D), bf16),
            pltpu.VMEM((16, D), bf16),
            pltpu.VMEM((16, D), bf16),
            pltpu.VMEM((FAC_ROWS, D), bf16),
            pltpu.VMEM((2, 16, D), bf16),
            pltpu.VMEM((2, 16, D), bf16),
            pltpu.VMEM((16, 256), f32),
            pltpu.VMEM((16, 256), bf16),
            pltpu.VMEM((8, D), f32),
            pltpu.VMEM((bits, 8, D), f32),
            pltpu.SemaphoreType.DMA((places.count,)),
            pltpu.SemaphoreType.DMA((places.count,)),
            pltpu.SemaphoreType.DMA((24 + 8 * PARTS,)),
            pltpu.SemaphoreType.REGULAR((5,)),
        ],
        compiler_params=pltpu.CompilerParams(
            collective_id=0, has_side_effects=True, vmem_limit_bytes=67_000_000
        ),
    )(lengths, enc_in, dec_in, d_out, weights, gains)


def local(enc_in, lengths, dec_in, gains, weights, d_out):
    sections = lax.axis_size("section")
    bits = lax.axis_size("dp").bit_length() - 1
    d_enc, decoded, d_start, total, total_gains = relay_call(
        sections, bits, enc_in, lengths, dec_in, d_out, gains[0], weights[0].reshape(8 * D, D)
    )
    section = lax.axis_index("section")
    used = jnp.where(section == 0, 4, jnp.where(section == 2, 6, 8))
    is_used = lax.broadcasted_iota(jnp.int32, (8, D, D), 0) < used
    total_weights = jnp.where(is_used, total.reshape(8, D, D).astype(f32), 0.0)
    return (decoded, d_enc, d_start, total_gains[None], total_weights[None])


def solution(mesh):
    in_specs = (
        P("dp", "section", None),
        P("dp"),
        P("dp", "section"),
        P("section", None, None),
        P("section", None, None, None),
        P("dp", "section"),
    )
    out_specs = (
        P("dp", "section"),
        P("dp", "section", None),
        P("dp", "section"),
        P("section", None, None),
        P("section", None, None, None),
    )
    return jax.shard_map(local, mesh=mesh, in_specs=in_specs, out_specs=out_specs, check_vma=False)
```

```python
import functools
import math

import jax
import jax.numpy as jnp
from jax import lax
from jax.experimental import pallas as pl
from jax.experimental.pallas import tpu as pltpu
from jax.sharding import PartitionSpec as P

D = 768
HEADS = 12
HEAD = 64
PAIRS = HEADS // 2
LEN = 512
GROUP = 4
ROWS = GROUP * LEN
epsilon = 1e-06
masked_score = -1e30
gelu_coeff = 0.044715
gelu_scale = math.sqrt(2.0 / math.pi)
log2_e = 1.4426950408889634
bf16 = jnp.bfloat16
f32 = jnp.float32
MESH = pl.DeviceIdType.MESH

W_ROWS = 0
X_ROWS = 3072
Q_ROWS = X_ROWS + ROWS
K_ROWS = Q_ROWS + ROWS
V_ROWS = K_ROWS + ROWS
O_ROWS = V_ROWS + ROWS
IL_ROWS = O_ROWS + ROWS
H_ROWS = IL_ROWS + ROWS
DH_ROWS = H_ROWS + ROWS
POOL_ROWS = DH_ROWS + ROWS
FF_H = 6144
FF_A = FF_H + ROWS
FF_E = FF_A + ROWS
RELAY_F = 6144
GELU_ROWS = 12 * ROWS
WIDE_ROWS = 24 * ROWS

CHUNK = 48
CHUNKS = 5
RELAY = CHUNK * CHUNKS
DIRECT = LEN - RELAY
RELAY_B = RELAY_F + GROUP * RELAY
FAC_ROWS = 176
FAC_AT = 8192
HALF = D // 2
PARTS = 2
JOB = HALF // PARTS
OWN_BLOCKS = {0: (3, 0, 1), 1: (0, 1, 2, 3, 7)}
LENT_BLOCKS = {0: (2,), 1: (4, 5, 6)}


def nn(a, b):
    return jnp.dot(a, b, preferred_element_type=f32)


def nt(a, b):
    return lax.dot_general(a, b, (((1,), (1,)), ((), ())), preferred_element_type=f32)


def tn(a, b):
    return lax.dot_general(a, b, (((0,), (0,)), ((), ())), preferred_element_type=f32)


def iota(shape, axis):
    return lax.broadcasted_iota(jnp.int32, shape, axis)


def inverse_rms(v):
    return lax.rsqrt(jnp.mean(v * v, axis=-1, keepdims=True) + epsilon)


def norm_back(normed, inverse, gain_row, grad):
    scaled = grad * gain_row
    return inverse * (scaled - normed * jnp.mean(scaled * normed, axis=-1, keepdims=True))


def gelu_both(u):
    square = u * u
    tangent = jnp.tanh(gelu_scale * (u + gelu_coeff * square * u))
    half = 0.5 * (1.0 + tangent)
    slope = half + 0.5 * u * (1.0 - tangent * tangent) * (
        gelu_scale + 3.0 * gelu_coeff * gelu_scale * square
    )
    return (u * half, slope)


class Places:
    def __init__(self, sections, bits):
        self.count = 0
        self.enc = [self.take(GROUP) for _ in range(sections)]
        self.small = [self.take(2) for _ in range(sections)]
        self.direct = self.take(GROUP)
        self.relay = [self.take(GROUP * CHUNKS) for _ in range(3)]
        self.back_direct = self.take(GROUP)
        self.back_relay = [self.take(GROUP * CHUNKS) for _ in range(3)]
        self.qk = self.take(1)
        self.mix = self.take(GROUP)
        self.state = self.take(1)
        self.state_back = self.take(1)
        self.g = self.take(1)
        self.x = self.take(1)
        self.out_enc = [self.take(GROUP) for _ in range(sections)]
        self.out_small = [self.take(2) for _ in range(sections)]
        self.halves = self.take(8)
        self.lend = self.take(8 * PARTS)
        self.lent = self.take(8 * PARTS)
        self.whole = self.take(8)
        self.inward = self.take(8 * PARTS)
        self.middle = self.take(8 * PARTS)
        self.outward = self.take(8 * PARTS)
        self.facs = self.take(2 ** bits - 1)
        self.gains = self.take(bits)

    def take(self, amount):
        first = self.count
        self.count += amount
        return first


def relay_kernel(
    sections,
    bits,
    places,
    len_ref,
    enc_ref,
    dec_ref,
    d_out_ref,
    w_ref,
    gain_ref,
    o_enc,
    o_dec,
    o_start,
    o_dw,
    o_gain,
    pool,
    wide,
    acc,
    cp,
    small,
    qk,
    mix,
    gk,
    xs,
    state,
    state_back,
    fac,
    rows_out,
    rows_in,
    small_wide,
    small_ref,
    gain_sum,
    gain_in,
    send_sem,
    recv_sem,
    local_sem,
    ready_sem,
):
    me = lax.axis_index("section")
    group = lax.axis_index("dp")
    chunk_len = LEN // sections

    def remote(number, src, dst, target):
        return pltpu.make_async_remote_copy(
            src_ref=src,
            dst_ref=dst,
            send_sem=send_sem.at[number],
            recv_sem=recv_sem.at[number],
            device_id=(target, group),
            device_id_type=MESH,
        )

    def local_copy(number, src, dst):
        return pltpu.make_async_copy(src, dst, local_sem.at[number])

    def rows(base, start, count):
        return pool.at[pl.ds(pl.multiple_of(base + start, 16), count)]

    def out_rows(start, count):
        return o_dw.at[pl.ds(pl.multiple_of(start, 16), count)]

    bit = [lax.rem(group // 2**k, 2) for k in range(bits)]
    partner = [group + 2**k * (1 - 2 * bit[k]) for k in range(bits)]

    chips = 2 ** (bits - 1)
    chip = group // 2
    on_left = chip < chips // 2
    inward = jnp.where(on_left, group + 2, group - 2)
    outward = jnp.where(on_left, group - 2, group + 2)
    in_middle = (chip == chips // 2 - 1) | (chip == chips // 2)
    at_end = (chip == 0) | (chip == chips - 1)

    def along(number, src, dst, target):
        return pltpu.make_async_remote_copy(
            src_ref=src,
            dst_ref=dst,
            send_sem=send_sem.at[number],
            recv_sem=recv_sem.at[number],
            device_id=(me, target),
            device_id_type=MESH,
        )

    def across(number, src, dst, k):
        return pltpu.make_async_remote_copy(
            src_ref=src,
            dst_ref=dst,
            send_sem=send_sem.at[number],
            recv_sem=recv_sem.at[number],
            device_id=(me, partner[k]),
            device_id_type=MESH,
        )

    barrier = pltpu.get_barrier_semaphore()
    for step in range(1, sections):
        pl.semaphore_signal(
            barrier,
            inc=1,
            device_id=(lax.rem(me + step, sections), group),
            device_id_type=MESH,
        )
    for k in range(bits):
        pl.semaphore_signal(barrier, inc=1, device_id=(me, partner[k]), device_id_type=MESH)
    pl.semaphore_signal(barrier, inc=1, device_id=(me, inward), device_id_type=MESH)

    @pl.when(jnp.logical_not(at_end))
    def _():
        pl.semaphore_signal(barrier, inc=1, device_id=(me, outward), device_id_type=MESH)
        pl.semaphore_wait(barrier, sections + bits + 1)

    @pl.when(at_end)
    def _():
        pl.semaphore_wait(barrier, sections + bits)

    lane = iota((1, 128), 1)
    low_half = lane < HEAD

    def enc_copy(sender, p):
        return remote(
            places.enc[sender] + p,
            enc_ref.at[p],
            rows(X_ROWS, p * LEN + sender * chunk_len, chunk_len),
            0,
        )

    def small_copy(sender, target):
        return remote(places.small[sender] + target - 2, small_ref, small.at[sender], target)

    def direct_copy(p):
        return remote(
            places.direct + p, rows(H_ROWS, p * LEN, DIRECT), rows(FF_H, p * LEN, DIRECT), 1
        )

    def relay_copy(hop, index):
        p = index // CHUNKS
        piece = index % CHUNKS
        whole = p * LEN + DIRECT + piece * CHUNK
        src = rows(H_ROWS, whole, CHUNK) if hop == 0 else rows(RELAY_F, index * CHUNK, CHUNK)
        dst = rows(FF_H, whole, CHUNK) if hop == 2 else rows(RELAY_F, index * CHUNK, CHUNK)
        return remote(places.relay[hop] + index, src, dst, (2, 3, 1)[hop])

    def back_direct_copy(p):
        return remote(
            places.back_direct + p, rows(FF_H, p * LEN, DIRECT), rows(DH_ROWS, p * LEN, DIRECT), 0
        )

    def back_relay_copy(hop, index):
        p = index // CHUNKS
        piece = index % CHUNKS
        whole = p * LEN + DIRECT + piece * CHUNK
        src = rows(FF_H, whole, CHUNK) if hop == 0 else rows(RELAY_B, index * CHUNK, CHUNK)
        dst = rows(DH_ROWS, whole, CHUNK) if hop == 2 else rows(RELAY_B, index * CHUNK, CHUNK)
        return remote(places.back_relay[hop] + index, src, dst, (3, 2, 0)[hop])

    def qk_copy():
        return remote(places.qk, qk, qk, 1)

    def mix_copy(p):
        part = pl.ds(pl.multiple_of(p * 16, 16), 16)
        return remote(places.mix + p, mix.at[part], mix.at[part], 2)

    def state_copy():
        return remote(places.state, state, state, 3)

    def state_back_copy():
        return remote(places.state_back, state_back, state_back, 2)

    def g_copy():
        return remote(places.g, gk, gk, 1)

    def x_copy():
        return remote(places.x, xs, xs, 2)

    def out_enc_copy(target, p):
        return remote(
            places.out_enc[target] + p,
            rows(H_ROWS, p * LEN + target * chunk_len, chunk_len),
            o_enc.at[p],
            target,
        )

    def out_small_copy(target, kind):
        return remote(
            places.out_small[target] + kind, rows_out.at[kind], rows_in.at[kind], target
        )

    def each_passage(body):
        def step(p, carry):
            body(p)
            return carry

        lax.fori_loop(0, GROUP, step, 0)

    def weights_in(blocks):
        copies = [
            local_copy(
                i,
                w_ref.at[pl.ds(i * D, D)],
                pool.at[pl.ds(W_ROWS + i * D, D)],
            )
            for i in range(blocks)
        ]
        for c in copies:
            c.start()
        return copies

    def block(i):
        return pool[W_ROWS + i * D : W_ROWS + (i + 1) * D, :]

    def send_inputs():
        def step(p, carry):
            enc_copy(me, p).start()
            return carry

        lax.fori_loop(0, GROUP, step, 0)

    def dynamic_enc_copy(p):
        number = places.enc[0] + me * GROUP + p
        return remote(
            number, enc_ref.at[p], rows(X_ROWS, p * LEN + me * chunk_len, chunk_len), 0
        )

    def dynamic_small_copy(target):
        number = places.small[0] + me * 2 + target - 2
        return remote(number, small_ref, small.at[me], target)

    width = D // sections
    small_wide[...] = jnp.zeros_like(small_wide)
    small_wide[0:GROUP, 0:width] = dec_ref[...].astype(f32)
    small_wide[GROUP : 2 * GROUP, 0:width] = d_out_ref[...].astype(f32)
    small_ref[...] = small_wide[...].astype(bf16)

    @pl.when(me != 2)
    def _():
        dynamic_small_copy(2).start()

    @pl.when(me != 3)
    def _():
        dynamic_small_copy(3).start()

    @pl.when((me == 1) | (me == 2))
    def _():
        each_passage(lambda p: dynamic_enc_copy(p).start())

    @pl.when(me == 3)
    def _():
        dynamic_enc_copy(0).start()

    def halves_copy(n, landing):
        return across(
            places.halves + n,
            rows(W_ROWS + n * D, (1 - bit[0]) * HALF, HALF),
            rows(landing, n * HALF, HALF),
            0,
        )

    def add_rows(at, landing, count):
        at = pl.ds(pl.multiple_of(at, 16), count)
        landed = pl.ds(pl.multiple_of(landing, 16), count)
        pool[at, :] = (pool[at, :].astype(f32) + pool[landed, :].astype(f32)).astype(bf16)

    def add_halves(n, landing):
        halves_copy(n, landing).wait_recv()
        add_rows(W_ROWS + n * D + bit[0] * HALF, landing + n * HALF, HALF)

    def lend_copy(n, i, index, landing):
        return remote(
            places.lend + PARTS * n + i,
            rows(W_ROWS + n * D + i * JOB, bit[0] * HALF, JOB),
            rows(landing, index * HALF + i * JOB, JOB),
            lax.rem(me + 2, sections),
        )

    def lent_copy(n, i, index, result):
        return remote(
            places.lent + PARTS * n + i,
            rows(result, index * HALF + i * JOB, JOB),
            out_rows(n * D + bit[0] * HALF + i * JOB, JOB),
            lax.rem(me + 2, sections),
        )

    def whole_copy(n):
        half = out_rows(n * D + bit[0] * HALF, HALF)
        return across(places.whole + n, half, half, 0)

    class Job:
        def __init__(self, n, i, at, landing, index, result):
            self.number = PARTS * n + i
            self.place = rows(at, 0, JOB)
            self.at = at
            self.from_out = landing + 2 * index * JOB
            self.from_in = landing + (2 * index + 1) * JOB
            self.result = result(at)

        def to_inward(self):
            return along(
                places.inward + self.number, self.place, rows(self.from_out, 0, JOB), inward
            )

        def to_middle(self):
            return along(
                places.middle + self.number, self.place, rows(self.from_in, 0, JOB), inward
            )

        def total_out(self):
            return along(places.outward + self.number, self.place, self.result, outward)

        def total_on(self):
            return along(places.outward + self.number, self.result, self.result, outward)

        def own(self):
            return local_copy(24 + self.number, self.place, self.result)

        def one(self):
            @pl.when(at_end)
            def _():
                self.to_inward().start()

        def two(self):
            @pl.when(jnp.logical_not(at_end))
            def _():
                self.to_inward().wait_recv()
                add_rows(self.at, self.from_out, JOB)

            if chips > 4:

                @pl.when(jnp.logical_not(at_end) & jnp.logical_not(in_middle))
                def _():
                    self.to_inward().start()

            @pl.when(in_middle)
            def _():
                self.to_middle().start()

        def three(self):
            @pl.when(in_middle)
            def _():
                self.to_middle().wait_recv()
                self.to_middle().wait_send()
                add_rows(self.at, self.from_in, JOB)
                self.own().start()
                self.total_out().start()

        def four(self):
            @pl.when(in_middle)
            def _():
                self.own().wait()

            @pl.when(jnp.logical_not(in_middle))
            def _():
                self.total_on().wait_recv()

            if chips > 4:

                @pl.when(jnp.logical_not(at_end) & jnp.logical_not(in_middle))
                def _():
                    self.total_on().start()

        def end(self):
            @pl.when(jnp.logical_not(in_middle))
            def _():
                self.to_inward().wait_send()

            @pl.when(in_middle)
            def _():
                self.total_out().wait_send()

            if chips > 4:

                @pl.when(jnp.logical_not(at_end) & jnp.logical_not(in_middle))
                def _():
                    self.total_on().wait_send()

    def own_jobs(blocks, landing):
        return [
            Job(
                n,
                i,
                W_ROWS + n * D + bit[0] * HALF + i * JOB,
                landing,
                PARTS * index + i,
                lambda at: out_rows(at - W_ROWS, JOB),
            )
            for index, n in enumerate(blocks)
            for i in range(PARTS)
        ]

    def lent_jobs(blocks, arrived, landing, result):
        return [
            Job(
                n,
                i,
                arrived + index * HALF + i * JOB,
                landing,
                PARTS * index + i,
                lambda at: rows(at - arrived + result, 0, JOB),
            )
            for index, n in enumerate(blocks)
            for i in range(PARTS)
        ]

    def finish_jobs(jobs, done, steps=()):
        count = len(jobs)
        steps = list(steps) + [1] * (count - len(steps))
        for t in range(count + 3):
            if t < count and steps[t] < 2:
                jobs[t].two()
            if 0 <= t - 1 < count and steps[t - 1] < 3:
                jobs[t - 1].three()
            if 0 <= t - 3 < count:
                jobs[t - 3].four()
                if (t - 3) % PARTS == PARTS - 1:
                    done((t - 3) // PARTS)

    def lent_sums(blocks, arrived, landing, result, between):
        jobs = lent_jobs(blocks, arrived, landing, result)
        count = len(jobs)
        pieces = list(between)
        for t in range(count + 3):
            if t < count:
                lend_copy(blocks[t // PARTS], t % PARTS, t // PARTS, arrived).wait_recv()
                jobs[t].one()
                jobs[t].two()
            if 0 <= t - 1 < count:
                jobs[t - 1].three()
            if 0 <= t - 3 < count:
                jobs[t - 3].four()
                index, i = ((t - 3) // PARTS, (t - 3) % PARTS)
                lent_copy(blocks[index], i, index, result).start()
            if pieces:
                pieces.pop(0)()
        for piece in pieces:
            piece()
        for job in jobs:
            job.end()
        for index, n in enumerate(blocks):
            for i in range(PARTS):
                lent_copy(n, i, index, result).wait_send()

    def gain_copy(k):
        return across(places.gains + k, gain_sum, gain_in.at[k], k)

    def gains_step(k, last=False):
        for step in range(k, bits + 1 if last else k + 1):
            if 0 < step <= bits:
                gain_copy(step - 1).wait()
                gain_sum[...] += gain_in[step - 1]
            if step < bits:
                gain_copy(step).start()

    def slot(width, core, place):
        return rows(FAC_AT, (core * chips + place) * width, width)

    def to_right(width, h):
        number = places.facs + 2 * (h - 1)
        place = slot(width, bit[0], chip - (h - 1))
        return along(number, place, place, group + 2)

    def to_left(width, h):
        number = places.facs + 2 * (h - 1) + 1
        place = slot(width, bit[0], chip + (h - 1))
        return along(number, place, place, group - 2)

    def from_left(width, h):
        number = places.facs + 2 * (h - 1)
        place = slot(width, bit[0], chip - h)
        return along(number, place, place, group - 2)

    def from_right(width, h):
        number = places.facs + 2 * (h - 1) + 1
        place = slot(width, bit[0], chip + h)
        return along(number, place, place, group + 2)

    def gather_first(width):
        own = local_copy(21, fac.at[pl.ds(0, width)], slot(width, bit[0], chip))
        own.start()
        own.wait()

    def gather_send(width, h, act):
        @pl.when((chip >= h - 1) & (chip < chips - 1))
        def _():
            act(to_right(width, h))

        @pl.when((chip + h - 1 <= chips - 1) & (chip > 0))
        def _():
            act(to_left(width, h))

    def gather_take(width, h):
        @pl.when(chip >= h)
        def _():
            from_left(width, h).wait_recv()

        @pl.when(chip + h <= chips - 1)
        def _():
            from_right(width, h).wait_recv()

    def gather_step(width, h, last=False):
        for step in range(h, chips + 1 if last else h + 1):
            if step > 1:
                gather_take(width, step - 1)
            if step < chips:
                gather_send(width, step, lambda copy: copy.start())

    def gather_cores(width):
        half = rows(FAC_AT, bit[0] * chips * width, chips * width)
        return across(places.facs + 2 * (chips - 1), half, half, 0)

    def gather_end(width):
        for h in range(1, chips):
            gather_send(width, h, lambda copy: copy.wait_send())

    batch = min(2**bits, 8)

    def gathered_tile(width, first, count, part):
        return jnp.concatenate(
            [
                pool[
                    pl.ds(
                        pl.multiple_of(FAC_AT + (part * batch + i) * width + first, 16), count
                    ),
                    :,
                ]
                for i in range(batch)
            ],
            axis=0,
        )

    def store_block(n, sides):
        for c in range(3):
            columns = slice(256 * c, 256 * (c + 1))

            def term(part):
                left, right = sides(part)
                return tn(left, right[:, columns])

            if 2**bits == batch:
                total = term(0)
            else:
                total = lax.fori_loop(
                    0,
                    2**bits // batch,
                    lambda i, total: total + term(i),
                    jnp.zeros((D, 256), f32),
                )
            pool[W_ROWS + n * D : W_ROWS + (n + 1) * D, columns] = total.astype(bf16)
        local_copy(n, rows(W_ROWS + n * D, 0, D), out_rows(n * D, D)).start()

    def aligned(tile, i, j):
        count = tile.shape[0]
        row, column = iota((count, count), 0), iota((count, count), 1)
        member = row & 15
        pick = (column - row == GROUP * (j - i)) & (member >= GROUP * i) & (member < GROUP * (i + 1))
        return nn(jnp.where(pick, 1.0, 0.0).astype(bf16), tile).astype(bf16)

    def blocks_stored(count):
        for n in range(count):
            local_copy(n, rows(W_ROWS + n * D, 0, D), out_rows(n * D, D)).wait()

    @pl.when(me == 0)
    def _():
        own = [
            local_copy(8 + p, enc_ref.at[p], pool.at[pl.ds(X_ROWS + p * LEN, chunk_len)])
            for p in range(GROUP)
        ]
        for c in own:
            c.start()
        weights = weights_in(4)
        for c in weights:
            c.wait()
        for c in own:
            c.wait()
        gain_row = gain_ref[0:1, :].astype(f32)
        key_row = iota((LEN, 1), 0)

        def pair_columns(hp):
            return pl.ds(pl.multiple_of(hp * 128, 128), 128)

        def forward(p):
            for sender in range(1, sections):
                enc_copy(sender, p).wait_recv()

            @pl.when(p < GROUP - 1)
            def _():
                pl.semaphore_signal(
                    ready_sem.at[4], inc=1, device_id=(3, group), device_id_type=MESH
                )

            start = pl.multiple_of(p * LEN, LEN)
            x = pool[pl.ds(X_ROWS + start, LEN), :].astype(f32)
            a0 = (x * inverse_rms(x) * gain_row).astype(bf16)
            pool[pl.ds(Q_ROWS + start, LEN), :] = (nn(a0, block(0)) * log2_e).astype(bf16)
            pool[pl.ds(K_ROWS + start, LEN), :] = nn(a0, block(1)).astype(bf16)
            pool[pl.ds(V_ROWS + start, LEN), :] = nn(a0, block(2)).astype(bf16)
            bias = jnp.where(key_row < len_ref[p], 0.0, masked_score).astype(bf16)

            def pair(hp, carry):
                c = pair_columns(hp)
                q2 = pool[pl.ds(Q_ROWS + start, LEN), c]
                k2 = pool[pl.ds(K_ROWS + start, LEN), c]
                v2 = pool[pl.ds(V_ROWS + start, LEN), c]
                one = jnp.ones_like(q2)
                zero = jnp.zeros_like(q2)
                queries = [
                    jnp.where(low_half, q2, jnp.where(lane == HEAD, one, zero)),
                    jnp.where(low_half, jnp.where(lane == 0, one, zero), q2),
                ]
                keys = [
                    jnp.where(low_half, k2, jnp.where(lane == HEAD, bias, zero)),
                    jnp.where(low_half, jnp.where(lane == 0, bias, zero), k2),
                ]
                values = [jnp.where(low_half, v2, one), jnp.where(low_half, one, v2)]
                scores = [nt(queries[half], keys[half]) for half in range(2)]
                probs = [
                    jnp.exp2(s - jnp.max(s, axis=-1, keepdims=True)).astype(bf16) for s in scores
                ]
                for half, e in enumerate(probs):
                    at = pl.multiple_of((p * HEADS + hp * 2 + half) * 2 * LEN, 2 * LEN)
                    wide[pl.ds(at, LEN), :] = e[:, :256]
                    wide[pl.ds(at + LEN, LEN), :] = e[:, 256:]
                mixes = [nn(e, value) for e, value in zip(probs, values)]
                total = pltpu.roll(jnp.where(low_half, mixes[1], mixes[0]), HEAD, 1)
                inverse = 1.0 / total
                pool[pl.ds(O_ROWS + start, LEN), c] = (
                    jnp.where(low_half, mixes[0], mixes[1]) * inverse
                ).astype(bf16)
                pool[pl.ds(IL_ROWS + start, LEN), c] = inverse.astype(bf16)
                return carry

            lax.fori_loop(0, PAIRS, pair, 0)
            h = x + nn(pool[pl.ds(O_ROWS + start, LEN), :], block(3))
            pool[pl.ds(H_ROWS + start, LEN), :] = h.astype(bf16)
            direct_copy(p).start()
            for piece in range(CHUNKS):
                relay_copy(0, p * CHUNKS + piece).start()

        each_passage(forward)

        def sent(p):
            direct_copy(p).wait_send()
            for piece in range(CHUNKS):
                relay_copy(0, p * CHUNKS + piece).wait_send()

        each_passage(sent)
        gain_sum[...] = jnp.zeros_like(gain_sum)

        def backward(p):
            start = pl.multiple_of(p * LEN, LEN)
            back_direct_copy(p).wait_recv()
            for piece in range(CHUNKS):
                back_relay_copy(2, p * CHUNKS + piece).wait_recv()
            dh = pool[pl.ds(DH_ROWS + start, LEN), :]
            pool[pl.ds(H_ROWS + start, LEN), :] = nt(dh, block(3)).astype(bf16)

            def pair(hp, carry):
                c = pair_columns(hp)
                q2 = pool[pl.ds(Q_ROWS + start, LEN), c]
                k2 = pool[pl.ds(K_ROWS + start, LEN), c]
                v2 = pool[pl.ds(V_ROWS + start, LEN), c]
                da = pool[pl.ds(H_ROWS + start, LEN), c].astype(f32)
                mixed = pool[pl.ds(O_ROWS + start, LEN), c].astype(f32)
                da = da * pool[pl.ds(IL_ROWS + start, LEN), c].astype(f32)
                product = da * mixed
                da = da.astype(bf16)
                one = jnp.ones_like(q2)
                zero = jnp.zeros_like(q2)
                dq = []
                dk = []
                dv = []
                for half in range(2):
                    mine = low_half if half == 0 else lane >= HEAD
                    spare = HEAD if half == 0 else 0
                    centre = -jnp.sum(jnp.where(mine, product, 0.0), axis=-1, keepdims=True)
                    centre_high = centre.astype(bf16)
                    centre_low = (centre - centre_high.astype(f32)).astype(bf16)
                    da_own = jnp.where(mine, da, zero)
                    da_ext = jnp.where(
                        lane == spare,
                        centre_high,
                        jnp.where(lane == spare + 1, centre_low, da_own),
                    )
                    at = pl.multiple_of((p * HEADS + hp * 2 + half) * 2 * LEN, 2 * LEN)
                    e = jnp.concatenate(
                        [wide[pl.ds(at, LEN), :], wide[pl.ds(at + LEN, LEN), :]], axis=1
                    )
                    ds = e * nt(da_ext, jnp.where(mine, v2, one)).astype(bf16)
                    dq.append(nn(ds, k2))
                    dk.append(nn(jnp.where(mine, q2, zero).T, ds))
                    dv.append(nn(da_own.T, e))
                pool[pl.ds(Q_ROWS + start, LEN), c] = jnp.where(low_half, dq[0], dq[1]).astype(bf16)
                pool[pl.ds(K_ROWS + start, LEN), c] = (
                    (dk[0] + dk[1]).T * (1.0 / log2_e)
                ).astype(bf16)
                pool[pl.ds(V_ROWS + start, LEN), c] = (dv[0] + dv[1]).T.astype(bf16)
                return carry

            lax.fori_loop(0, PAIRS, pair, 0)
            grad = (
                nt(pool[pl.ds(Q_ROWS + start, LEN), :], block(0))
                + nt(pool[pl.ds(K_ROWS + start, LEN), :], block(1))
                + nt(pool[pl.ds(V_ROWS + start, LEN), :], block(2))
            )
            x = pool[pl.ds(X_ROWS + start, LEN), :].astype(f32)
            inverse = inverse_rms(x)
            normed = x * inverse
            d_in = dh.astype(f32) + norm_back(normed, inverse, gain_row, grad)
            pool[pl.ds(H_ROWS + start, LEN), :] = d_in.astype(bf16)
            gain_sum[0:1, :] += jnp.sum(grad * normed, axis=0, keepdims=True)
            pool[pl.ds(X_ROWS + start, LEN), :] = (normed * gain_row).astype(bf16)
            for target in range(1, sections):
                out_enc_copy(target, p).start()
            local_copy(8 + p, rows(H_ROWS, start, chunk_len), o_enc.at[p]).start()

        each_passage(backward)
        sides = (
            (X_ROWS, Q_ROWS),
            (X_ROWS, K_ROWS),
            (X_ROWS, V_ROWS),
            (O_ROWS, DH_ROWS),
        )
        own = OWN_BLOCKS[0]
        lent = LENT_BLOCKS[0][0]
        jobs = own_jobs(OWN_BLOCKS[0], O_ROWS)

        def compute(n):
            left, right = sides[n]

            def columns(k, carry):
                c = pl.ds(pl.multiple_of(k * 256, 256), 256)
                pool[pl.ds(W_ROWS + n * D, D), c] = tn(
                    pool[left : left + ROWS, :], pool[right : right + ROWS, c]
                ).astype(bf16)
                return carry

            lax.fori_loop(0, 3, columns, 0)

        def begin(index):
            add_halves(own[index], DH_ROWS)
            for job in jobs[PARTS * index : PARTS * (index + 1)]:
                job.one()

        gains_step(0)
        compute(own[0])
        gains_step(1)
        pl.semaphore_signal(
            ready_sem.at[0], inc=1, device_id=(me, partner[0]), device_id_type=MESH
        )

        @pl.when(in_middle)
        def _():
            pl.semaphore_signal(
                ready_sem.at[3], inc=1, device_id=(me, inward), device_id_type=MESH
            )

        @pl.when(jnp.logical_not(in_middle))
        def _():
            pl.semaphore_signal(
                ready_sem.at[1], inc=1, device_id=(me, inward), device_id_type=MESH
            )

        @pl.when(jnp.logical_not(at_end))
        def _():
            pl.semaphore_signal(
                ready_sem.at[2], inc=1, device_id=(me, outward), device_id_type=MESH
            )

        pl.semaphore_wait(ready_sem.at[0], 1)
        halves_copy(own[0], DH_ROWS).start()

        @pl.when(in_middle)
        def _():
            pl.semaphore_wait(ready_sem.at[3], 1)

        @pl.when(jnp.logical_not(in_middle))
        def _():
            pl.semaphore_wait(ready_sem.at[2], 1)

        @pl.when(jnp.logical_not(at_end))
        def _():
            pl.semaphore_wait(ready_sem.at[1], 1)

        begin(0)
        compute(lent)
        gains_step(2)
        halves_copy(lent, DH_ROWS).start()
        compute(own[1])
        gains_step(3, last=True)
        halves_copy(own[1], DH_ROWS).start()
        add_halves(lent, DH_ROWS)
        for i in range(PARTS):
            lend_copy(lent, i, 0, 4608).start()
        for job in jobs[: PARTS // 2]:
            job.two()
        compute(own[2])
        halves_copy(own[2], DH_ROWS).start()
        begin(1)
        for job in jobs[PARTS // 2 : PARTS]:
            job.two()
        for job in jobs[: PARTS // 2]:
            job.three()
        begin(2)
        finish_jobs(
            jobs,
            lambda index: whole_copy(own[index]).start(),
            (3,) * (PARTS // 2) + (2,) * (PARTS // 2),
        )
        for i in range(PARTS):
            lent_copy(lent, i, 0, 4608).wait_recv()
        whole_copy(lent).start()

        def finish(p):
            for target in range(1, sections):
                out_enc_copy(target, p).wait_send()
            local_copy(8 + p, rows(H_ROWS, p * LEN, chunk_len), o_enc.at[p]).wait()

        each_passage(finish)
        for n in own + (lent,):
            whole_copy(n).wait()
            halves_copy(n, DH_ROWS).wait_send()
        for i in range(PARTS):
            lend_copy(lent, i, 0, 4608).wait_send()
        for job in jobs:
            job.end()

    @pl.when(me == 1)
    def _():
        for c in weights_in(8):
            c.wait()
        gain_row = gain_ref[0:1, :].astype(f32)
        key_place = iota((1, LEN), 1)
        qk_copy().wait_recv()

        def tiles(b, p, base):
            return [
                pl.ds(pl.multiple_of(base + (3 * b + i) * ROWS + p * LEN, LEN), LEN)
                for i in range(3)
            ]

        def forward(p):
            start = pl.multiple_of(p * LEN, LEN)
            direct_copy(p).wait_recv()
            for piece in range(CHUNKS):
                relay_copy(2, p * CHUNKS + piece).wait_recv()
            h = pool[pl.ds(FF_H + start, LEN), :].astype(f32)
            a1 = (h * inverse_rms(h) * gain_row).astype(bf16)
            pool[pl.ds(FF_A + start, LEN), :] = a1
            acc[...] = h
            for b in range(4):
                r, slope = gelu_both(nn(a1, block(b)))
                r = r.astype(bf16)
                slope = slope.astype(bf16)
                for i, (at_r, at_s) in enumerate(zip(tiles(b, p, 0), tiles(b, p, GELU_ROWS))):
                    wide[at_r, :] = r[:, 256 * i : 256 * (i + 1)]
                    wide[at_s, :] = slope[:, 256 * i : 256 * (i + 1)]
                acc[...] += nn(r, block(4 + b))
            e = acc[...].astype(bf16)
            pool[pl.ds(FF_E + start, LEN), :] = e
            part = pl.ds(pl.multiple_of(p * 16, 16), 16)
            score = jnp.where(key_place < len_ref[p], nt(qk[part, :], e), masked_score)
            score = jnp.exp(score - jnp.max(score, axis=-1, keepdims=True))
            probs = score / jnp.sum(score, axis=-1, keepdims=True)
            cp[part, :] = probs
            mix[part, :] = nn(probs.astype(bf16), e).astype(bf16)
            mix_copy(p).start()

        each_passage(forward)
        each_passage(lambda p: mix_copy(p).wait_send())
        gain_sum[...] = jnp.zeros_like(gain_sum)
        g_copy().wait_recv()

        def backward(p):
            start = pl.multiple_of(p * LEN, LEN)
            part = pl.ds(pl.multiple_of(p * 16, 16), 16)
            e = pool[pl.ds(FF_E + start, LEN), :]
            probs = cp[part, :]
            d_probs = nt(gk[part, :], e)
            d_score = probs * (d_probs - jnp.sum(probs * d_probs, axis=-1, keepdims=True))
            d_score = d_score.astype(bf16)
            xs[part, :] = nn(d_score, e).astype(bf16)
            de = tn(d_score, qk[part, :]) + tn(probs.astype(bf16), gk[part, :])
            de = de.astype(bf16)
            pool[pl.ds(FF_E + start, LEN), :] = de
            for b in range(4):
                at = tiles(b, p, GELU_ROWS)
                slope = jnp.concatenate([wide[t, :] for t in at], axis=1)
                du = (nt(de, block(4 + b)) * slope.astype(f32)).astype(bf16)
                for i, t in enumerate(at):
                    wide[t, :] = du[:, 256 * i : 256 * (i + 1)]
                grad = nt(du, block(b))
                if b == 0:
                    acc[...] = grad
                else:
                    acc[...] += grad
            grad = acc[...]
            h = pool[pl.ds(FF_H + start, LEN), :].astype(f32)
            inverse = inverse_rms(h)
            normed = h * inverse
            dh = de.astype(f32) + norm_back(normed, inverse, gain_row, grad)
            gain_sum[0:1, :] += jnp.sum(grad * normed, axis=0, keepdims=True)
            pool[pl.ds(FF_H + start, LEN), :] = dh.astype(bf16)
            back_direct_copy(p).start()
            for piece in range(CHUNKS):
                back_relay_copy(0, p * CHUNKS + piece).start()

        each_passage(backward)
        x_copy().start()
        halves_at = FF_E + ROWS
        landing = halves_at + 8 * HALF

        def compute(n):
            b = n % 4
            for i in range(3):
                t = 3 * b + i
                if n < 4:
                    du = wide[GELU_ROWS + t * ROWS : GELU_ROWS + (t + 1) * ROWS, :]
                    pool[W_ROWS + n * D : W_ROWS + (n + 1) * D, 256 * i : 256 * (i + 1)] = tn(
                        pool[FF_A : FF_A + ROWS, :], du
                    ).astype(bf16)
                else:
                    first = W_ROWS + n * D + 256 * i
                    pool[first : first + 256, :] = tn(
                        wide[t * ROWS : (t + 1) * ROWS, :], pool[FF_E : FF_E + ROWS, :]
                    ).astype(bf16)
            halves_copy(n, halves_at).start()

        own = OWN_BLOCKS[1]
        lent = LENT_BLOCKS[1]
        jobs = own_jobs(own, landing)

        def begin(index):
            add_halves(own[index], halves_at)
            for job in jobs[PARTS * index : PARTS * (index + 1)]:
                job.one()

        half_parts = PARTS // 2

        def half_block(index):
            return jobs[half_parts * index : half_parts * (index + 1)]

        def lend(index):
            add_halves(lent[index], halves_at)
            for i in range(PARTS):
                lend_copy(lent[index], i, index, 11264).start()

        gains_step(0)
        compute(own[0])
        gains_step(1)
        compute(lent[0])
        begin(0)
        gains_step(2)
        compute(own[1])
        lend(0)
        gains_step(3, last=True)
        compute(lent[1])
        begin(1)
        compute(own[2])
        lend(1)
        for job in half_block(0):
            job.two()
        compute(lent[2])
        begin(2)
        for job in half_block(1):
            job.two()
        compute(own[3])
        lend(2)
        for job in half_block(0):
            job.three()
        compute(own[4])
        begin(3)
        for job in half_block(1):
            job.three()
        for job in half_block(2):
            job.two()
        begin(4)
        for job in half_block(3):
            job.two()
        finish_jobs(
            jobs,
            lambda index: whole_copy(own[index]).start(),
            (3,) * (2 * half_parts) + (2,) * (2 * half_parts),
        )
        for index, n in enumerate(lent):
            for i in range(PARTS):
                lent_copy(n, i, index, 11264).wait_recv()
            whole_copy(n).start()
        for n in range(8):
            whole_copy(n).wait()
            halves_copy(n, halves_at).wait_send()
        for index, n in enumerate(lent):
            for i in range(PARTS):
                lend_copy(n, i, index, 11264).wait_send()
        for job in jobs:
            job.end()
        x_copy().wait_send()

        def sent(p):
            back_direct_copy(p).wait_send()
            for piece in range(CHUNKS):
                back_relay_copy(0, p * CHUNKS + piece).wait_send()

        each_passage(sent)

    def gathered_rows(own):
        copy = local_copy(20, small_ref, small.at[own])
        copy.start()
        for sender in range(sections):
            if sender != own:
                small_copy(sender, own).wait_recv()
        copy.wait()
        total = jnp.zeros((16, D), f32)
        for sender in range(sections):
            row, column = iota((256, D), 0), iota((256, D), 1)
            pick = jnp.where((column == row + width * sender) & (row < width), 1.0, 0.0)
            total = total + nn(small[sender], pick.astype(bf16))
        return total

    def moved(values, first, to):
        row, column = iota((16, 16), 0), iota((16, 16), 1)
        pick = (column - first == row - to) & (row >= to) & (row < to + GROUP)
        return nn(jnp.where(pick, 1.0, 0.0).astype(bf16), values)

    def packed(values):
        total = moved(values[0], 0, 0)
        for i, value in enumerate(values[1:]):
            total = total + moved(value, 0, GROUP * (i + 1))
        return total.astype(bf16)

    head_mask = (iota((64, D), 1) >> 6) == (iota((64, D), 0) & 15)

    def spread_heads(values):
        pick = jnp.where((iota((64, 16), 0) >> 4) == iota((64, 16), 1), 1.0, 0.0)
        return jnp.where(head_mask, nn(pick.astype(bf16), values), 0.0).astype(bf16)

    def join_heads(values):
        pick = jnp.where(iota((16, 64), 0) == (iota((16, 64), 1) >> 4), 1.0, 0.0)
        return nn(pick.astype(bf16), jnp.where(head_mask, values, 0.0).astype(bf16)).astype(bf16)

    def pass_on(copies, number, first=0, last=GROUP * CHUNKS):
        def step(index, carry):
            copies(number - 1, index).wait_recv()
            copies(number, index).start()
            return carry

        lax.fori_loop(first, last, step, 0)

    def passed(copies, number):
        def step(index, carry):
            copies(number, index).wait_send()
            return carry

        lax.fori_loop(0, GROUP * CHUNKS, step, 0)

    @pl.when(me == 2)
    def _():
        weights = weights_in(6)
        x = moved(gathered_rows(2).astype(bf16), 0, 0)
        for c in weights:
            c.wait()
        gain_self = gain_ref[0:1, :].astype(f32)
        gain_cross = gain_ref[1:2, :].astype(f32)
        inverse_self = inverse_rms(x)
        normed_self = x * inverse_self
        a2 = (normed_self * gain_self).astype(bf16)
        sv = nn(a2, block(0)).astype(bf16)
        middle = x + nn(sv, block(1))
        inverse_cross = inverse_rms(middle)
        normed_cross = middle * inverse_cross
        a3 = (normed_cross * gain_cross).astype(bf16)
        cq = nn(a3, block(2)).astype(bf16)
        qk[...] = nt(spread_heads(cq), block(3)).astype(bf16)
        qk_copy().start()
        pass_on(relay_copy, 1)
        for p in range(GROUP):
            mix_copy(p).wait_recv()
        co = join_heads(nn(mix[...], block(4)))
        state[...] = (middle + nn(co, block(5))).astype(bf16)
        state_copy().start()
        state_back_copy().wait_recv()
        dy = state_back[...]
        dco = nt(dy, block(5)).astype(bf16)
        gk[...] = nt(spread_heads(dco), block(4)).astype(bf16)
        g_copy().start()
        pass_on(back_relay_copy, 2)
        x_copy().wait_recv()
        dcq = join_heads(nn(xs[...], block(3)))
        grad_cross = nt(dcq, block(2))
        dm = dy.astype(f32) + norm_back(normed_cross, inverse_cross, gain_cross, grad_cross)
        dm_low = dm.astype(bf16)
        dsv = nt(dm_low, block(1)).astype(bf16)
        grad_self = nt(dsv, block(0))
        d_in = dm + norm_back(normed_self, inverse_self, gain_self, grad_self)
        rows_out[1] = d_in.astype(bf16)
        gain_sum[...] = jnp.zeros_like(gain_sum)
        gain_sum[0:1, :] = jnp.sum(grad_self * normed_self, axis=0, keepdims=True)
        gain_sum[1:2, :] = jnp.sum(grad_cross * normed_cross, axis=0, keepdims=True)
        fac[0:16, :] = packed([a2, dsv, sv, dm_low])
        fac[16:32, :] = packed([a3, dcq, co, dy])
        fac[32:48, :] = packed([cq, dco])
        fac[48:112, :] = xs[...]
        fac[112:176, :] = mix[...]
        for target in range(sections):
            if target != 2:
                out_small_copy(target, 1).start()
        rows_in[1] = rows_out[1]
        gather_first(FAC_ROWS)
        gather_step(FAC_ROWS, 1)
        gains_step(0)
        gains_step(1)
        gather_step(FAC_ROWS, 2)
        gains_step(2)
        gather_step(FAC_ROWS, 3)
        gains_step(3, last=True)
        gather_step(FAC_ROWS, 4, last=True)
        gather_cores(FAC_ROWS).start()
        gather_cores(FAC_ROWS).wait()
        gather_end(FAC_ROWS)
        def pair_term(first, left, right):
            def term(part):
                tile = gathered_tile(FAC_ROWS, first, 16, part)
                return (tile, aligned(tile, left, right))

            return term

        def head_term(first, member):
            def term(part):
                tall, short = (64 * batch, 16 * batch)
                row, column = iota((tall, short), 0), iota((tall, short), 1)
                heads = (iota((tall, D), 1) >> 6) == (iota((tall, D), 0) & 15)
                pick = column == (row >> 6) * 16 + GROUP * member + ((row >> 4) & 3)
                short_rows = nn(
                    jnp.where(pick, 1.0, 0.0).astype(bf16), gathered_tile(FAC_ROWS, 32, 16, part)
                )
                short_rows = jnp.where(heads, short_rows, 0.0).astype(bf16)
                return (gathered_tile(FAC_ROWS, first, 64, part), short_rows)

            return term

        store_block(3, head_term(48, 0))
        store_block(4, head_term(112, 1))
        store_block(0, pair_term(0, 0, 1))
        store_block(1, pair_term(0, 2, 3))
        store_block(2, pair_term(16, 0, 1))
        store_block(5, pair_term(16, 2, 3))
        lent_sums(LENT_BLOCKS[0], 4608, 4608 + 2 * HALF, 4608 + HALF, ())
        blocks_stored(6)
        for target in range(sections):
            if target != 2:
                out_small_copy(target, 1).wait_send()
        passed(relay_copy, 1)
        passed(back_relay_copy, 2)
        qk_copy().wait_send()
        state_copy().wait_send()
        g_copy().wait_send()

    @pl.when(me == 3)
    def _():
        weights = weights_in(8)
        d_out = moved(gathered_rows(3).astype(bf16), GROUP, 0)
        d_low = d_out.astype(bf16)
        for c in weights:
            c.wait()
        gain_row = gain_ref[0:1, :].astype(f32)

        def next_passage(p):
            pl.semaphore_wait(ready_sem.at[4], 1)
            dynamic_enc_copy(p).start()

        next_passage(1)
        next_passage(2)
        pass_on(relay_copy, 2, 0, CHUNKS)
        next_passage(3)
        pass_on(relay_copy, 2, CHUNKS)
        state_copy().wait_recv()
        y = state[...].astype(f32)
        inverse = inverse_rms(y)
        normed = y * inverse
        a4 = (normed * gain_row).astype(bf16)
        r4 = []
        du4 = []
        result = y
        grad = jnp.zeros((16, D), f32)
        for b in range(4):
            r, slope = gelu_both(nn(a4, block(b)))
            r4.append(r.astype(bf16))
            result = result + nn(r4[b], block(4 + b))
            du4.append((nt(d_low, block(4 + b)) * slope).astype(bf16))
            grad = grad + nt(du4[b], block(b))
        state_back[...] = (d_out + norm_back(normed, inverse, gain_row, grad)).astype(bf16)
        state_back_copy().start()
        pass_on(back_relay_copy, 1)
        rows_out[0] = result.astype(bf16)
        gain_sum[...] = jnp.zeros_like(gain_sum)
        gain_sum[0:1, :] = jnp.sum(grad * normed, axis=0, keepdims=True)
        fac[...] = jnp.zeros_like(fac)
        fac[0:16, :] = packed([a4, d_low, r4[0], r4[1]])
        fac[16:32, :] = packed([r4[2], r4[3], du4[0], du4[1]])
        fac[32:48, :] = packed([du4[2], du4[3]])
        for target in range(sections):
            if target != 3:
                out_small_copy(target, 0).start()
        rows_in[0] = rows_out[0]
        gather_first(48)
        gather_step(48, 1)
        gains_step(0)
        gather_step(48, 2)
        gains_step(1)
        gather_step(48, 3)
        gains_step(2)
        gather_step(48, 4, last=True)
        gather_cores(48).start()
        gains_step(3, last=True)
        gather_cores(48).wait()
        gather_end(48)

        def member(slot, part):
            return aligned(gathered_tile(48, 16 * (slot // 4), 16, part), 0, slot % 4)

        def stored(n):
            b = n % 4
            sides = ((0, 6 + b), (2 + b, 1))[n // 4]
            return lambda: store_block(
                n, lambda part: (member(sides[0], part), member(sides[1], part))
            )

        count = len(LENT_BLOCKS[1])
        lent_sums(
            LENT_BLOCKS[1],
            11264,
            11264 + 2 * count * HALF,
            11264 + count * HALF,
            tuple(stored(n) for n in range(8)),
        )
        blocks_stored(8)
        for target in range(sections):
            if target != 3:
                out_small_copy(target, 0).wait_send()
        passed(relay_copy, 2)
        passed(back_relay_copy, 1)
        state_back_copy().wait_send()

    o_gain[...] = gain_sum[0:2, :]

    @pl.when(me != 2)
    def _():
        dynamic_small_copy(2).wait_send()
        remote(
            places.out_small[0] + me * 2 + 1, rows_out.at[1], rows_in.at[1], 2
        ).wait_recv()

    @pl.when(me != 3)
    def _():
        dynamic_small_copy(3).wait_send()
        remote(places.out_small[0] + me * 2, rows_out.at[0], rows_in.at[0], 3).wait_recv()

    @pl.when(me != 0)
    def _():
        def step(p, carry):
            dynamic_enc_copy(p).wait_send()
            remote(
                places.out_enc[0] + me * GROUP + p, rows(H_ROWS, p * LEN, chunk_len), o_enc.at[p], 0
            ).wait_recv()
            return carry

        lax.fori_loop(0, GROUP, step, 0)

    row, column = iota((D, width), 0), iota((D, width), 1)
    pick = jnp.where(row == column + me * width, 1.0, 0.0).astype(bf16)
    o_dec[...] = nn(rows_in[0], pick)[0:GROUP, :].astype(bf16)
    o_start[...] = nn(rows_in[1], pick)[0:GROUP, :].astype(bf16)


def relay_call(sections, bits, enc_in, lengths, dec_in, d_out, gains, weights):
    places = Places(sections, bits)
    any_space = pl.BlockSpec(memory_space=pl.ANY)
    vmem = pl.BlockSpec(memory_space=pltpu.VMEM)
    return pl.pallas_call(
        functools.partial(relay_kernel, sections, bits, places),
        out_shape=(
            jax.ShapeDtypeStruct(enc_in.shape, bf16),
            jax.ShapeDtypeStruct(dec_in.shape, bf16),
            jax.ShapeDtypeStruct(dec_in.shape, bf16),
            jax.ShapeDtypeStruct((8 * D, D), bf16),
            jax.ShapeDtypeStruct((2, D), f32),
        ),
        in_specs=[
            pl.BlockSpec(memory_space=pltpu.SMEM),
            any_space,
            vmem,
            vmem,
            any_space,
            vmem,
        ],
        out_specs=(any_space, vmem, vmem, any_space, vmem),
        scratch_shapes=[
            pltpu.VMEM((POOL_ROWS, D), bf16),
            pltpu.VMEM((WIDE_ROWS, 256), bf16),
            pltpu.VMEM((LEN, D), f32),
            pltpu.VMEM((64, LEN), f32),
            pltpu.VMEM((sections, 16, 256), bf16),
            pltpu.VMEM((64, D), bf16),
            pltpu.VMEM((64, D), bf16),
            pltpu.VMEM((64, D), bf16),
            pltpu.VMEM((64, D), bf16),
            pltpu.VMEM((16, D), bf16),
            pltpu.VMEM((16, D), bf16),
            pltpu.VMEM((FAC_ROWS, D), bf16),
            pltpu.VMEM((2, 16, D), bf16),
            pltpu.VMEM((2, 16, D), bf16),
            pltpu.VMEM((16, 256), f32),
            pltpu.VMEM((16, 256), bf16),
            pltpu.VMEM((8, D), f32),
            pltpu.VMEM((bits, 8, D), f32),
            pltpu.SemaphoreType.DMA((places.count,)),
            pltpu.SemaphoreType.DMA((places.count,)),
            pltpu.SemaphoreType.DMA((24 + 8 * PARTS,)),
            pltpu.SemaphoreType.REGULAR((5,)),
        ],
        compiler_params=pltpu.CompilerParams(
            collective_id=0, has_side_effects=True, vmem_limit_bytes=67_000_000
        ),
    )(lengths, enc_in, dec_in, d_out, weights, gains)


def widen_kernel(in_ref, out_ref, narrow, wide, in_sem, out_sem):
    section = lax.axis_index("section")
    used = jnp.where(section == 0, 4, jnp.where(section == 2, 6, 8))
    parts = [pl.ds(n * D, D) for n in range(8)]
    ins = [
        pltpu.make_async_copy(in_ref.at[part], narrow.at[part], in_sem.at[n])
        for n, part in enumerate(parts)
    ]
    outs = [
        pltpu.make_async_copy(wide.at[part], out_ref.at[part], out_sem.at[n])
        for n, part in enumerate(parts)
    ]
    for copy in ins:
        copy.start()
    for n, part in enumerate(parts):
        ins[n].wait()

        @pl.when(n < used)
        def _():
            wide[part, :] = narrow[part, :].astype(f32)

        @pl.when(n >= used)
        def _():
            wide[part, :] = jnp.zeros((D, D), f32)

        outs[n].start()
    for copy in outs:
        copy.wait()


def widen(total):
    any_space = pl.BlockSpec(memory_space=pl.ANY)
    return pl.pallas_call(
        widen_kernel,
        out_shape=jax.ShapeDtypeStruct(total.shape, f32),
        in_specs=[any_space],
        out_specs=any_space,
        scratch_shapes=[
            pltpu.VMEM(total.shape, bf16),
            pltpu.VMEM(total.shape, f32),
            pltpu.SemaphoreType.DMA((8,)),
            pltpu.SemaphoreType.DMA((8,)),
        ],
        compiler_params=pltpu.CompilerParams(vmem_limit_bytes=48 * 1024 * 1024),
    )(total)


def local(enc_in, lengths, dec_in, gains, weights, d_out):
    sections = lax.axis_size("section")
    bits = lax.axis_size("dp").bit_length() - 1
    d_enc, decoded, d_start, total, total_gains = relay_call(
        sections, bits, enc_in, lengths, dec_in, d_out, gains[0], weights[0].reshape(8 * D, D)
    )
    total_weights = widen(total).reshape(1, 8, D, D)
    return (decoded, d_enc, d_start, total_gains[None], total_weights)


def solution(mesh):
    in_specs = (
        P("dp", "section", None),
        P("dp"),
        P("dp", "section"),
        P("section", None, None),
        P("section", None, None, None),
        P("dp", "section"),
    )
    out_specs = (
        P("dp", "section"),
        P("dp", "section", None),
        P("dp", "section"),
        P("section", None, None),
        P("section", None, None, None),
    )
    return jax.shard_map(local, mesh=mesh, in_specs=in_specs, out_specs=out_specs, check_vma=False)
```
